32 devices in a mesh: rep: 8 (over y, x, core), fsdp: 4 (over z).
Axes of the slice: x: 2, y: 2, z: 4, core: 2. Of those that a mesh axis runs over, the one named last changes fastest.
Arguments:
- hidden: bfloat16 [96, 2048, 768], P(('rep', 'fsdp')), may hold values from -6 to 6
- segments: int32 [96, 2048], P(('rep', 'fsdp')), may hold values from 0 to 5, never falling along the last dimension, each value on 1 to 682 neighbouring positions
- selected: int32 [96, 256], P(('rep', 'fsdp')), may hold values from 0 to 2047, as said below
- w_query: bfloat16 [768, 768], P('fsdp'), may hold values from -0.21875 to 0.21875
- w_key: bfloat16 [768, 768], P('fsdp'), may hold values from -0.21875 to 0.21875
- w_value: bfloat16 [768, 768], P('fsdp'), may hold values from -0.21875 to 0.21875
- w_out: bfloat16 [768, 768], P('fsdp'), may hold values from -0.875 to 0.875
- w_up: bfloat16 [768, 3072], P('fsdp'), may hold values from -0.21875 to 0.21875
- w_down: bfloat16 [3072, 768], P('fsdp'), may hold values from -0.109375 to 0.109375
- w_router: bfloat16 [768], P('fsdp'), may hold values from -0.21875 to 0.21875
- gain_attn: bfloat16 [768], P('fsdp'), may hold values from 0.099609375 to 1.8984375
- gain_mlp: bfloat16 [768], P('fsdp'), may hold values from 0.099609375 to 1.8984375
- cotangent: bfloat16 [96, 2048, 768], P(('rep', 'fsdp')), may hold values from -6 to 6
Outputs:
- out_hidden: bfloat16 [96, 2048, 768], P(('rep', 'fsdp'))
- grad_hidden: bfloat16 [96, 2048, 768], P(('rep', 'fsdp'))
- grad_query: float32 [768, 768], P('fsdp')
- grad_key: float32 [768, 768], P('fsdp')
- grad_value: float32 [768, 768], P('fsdp')
- grad_out: float32 [768, 768], P('fsdp')
- grad_up: float32 [768, 3072], P('fsdp')
- grad_down: float32 [3072, 768], P('fsdp')
- grad_router: float32 [768], P('fsdp')
- grad_gain_attn: float32 [768], P('fsdp')
- grad_gain_mlp: float32 [768], P('fsdp')
The draws below stay inside these ranges and needn't reach their ends.
Inputs may be any that keep to these rules, and one draw needn't show every extreme that they name: `selected`: each row holds 256 distinct positions of its sequence in ascending order; 0 and 2047 are always among them.
All inputs are finite; a program needn't handle non-finite values.
Results may differ from the reference program's by a relative error of at most 0.015.
Values may be sent and summed in bfloat16 or wider, within the bound.
No kernel may reach another device: no remote copies, remote signals or barrier semaphores. Data moves between devices by JAX's collectives and lax.ppermute only.
A program may use at most 320 MiB of HBM per device.

```python
import math
import jax
import jax.numpy as jnp
import numpy as np
from jax import lax

D = 768
HEADS = 12
HEAD_DIM = 64
FF = 3072
LEN = 2048
KEEP = 256
SEQS = 96


def draw_selected(key, part):
    key = jax.random.fold_in(key, 11)
    middle_count = LEN - 2
    scores = jax.random.randint(key, (SEQS, middle_count), 0, 2 ** 16) * middle_count + jnp.arange(middle_count, dtype=jnp.int32)[None, :]
    ranking = jnp.argsort(scores, axis=1).astype(jnp.int32)
    routed_tokens = ranking[:, :KEEP - 2] + 1
    first_col = jnp.zeros((SEQS, 1), jnp.int32)
    last_col = jnp.full((SEQS, 1), LEN - 1, jnp.int32)
    return jnp.sort(jnp.concatenate([first_col, routed_tokens, last_col], axis=1), axis=1).astype(jnp.int32)


def shard_levels(own_key, shape, pieces, low, high):
    def one(axis_at, shards_of):
        steps = jax.random.uniform(jax.random.fold_in(jax.random.fold_in(own_key, 6), axis_at), (shards_of,), jnp.float32, low / len(pieces), high / len(pieces))
        return jnp.repeat(jnp.exp(steps), shape[axis_at] // shards_of).reshape((-1,) + (1,) * (len(shape) - axis_at - 1))

    factor_of = one(*pieces[0])
    for cut in pieces[1:]:
        factor_of = factor_of * one(*cut)
    return factor_of


def profile(amount, total, limit, lean):
    loads = [(1 << 20) // math.isqrt(rank ** lean) + 1 for rank in range(2, amount + 1)]
    surplus, counts = total - limit - (amount - 1), [1] * (amount - 1)
    while surplus > 0:
        movable = [i for i in range(amount - 1) if counts[i] < limit]
        pool, left = sum([loads[i] for i in movable]), surplus
        for i in movable:
            extra = min(limit - counts[i], max(1, left * loads[i] // pool), surplus)
            counts[i] = counts[i] + extra
            surplus = surplus - extra
    return np.array([limit] + counts)


def uneven_parts(rng, amount, total, reach, skew):
    if amount == 2:
        one = jax.random.randint(rng, (), max(1, total - reach), min(reach, total - 1) + 1)
        return jnp.stack([one, total - one])
    tallies = jnp.asarray(profile(amount, total, reach, skew), jnp.int32)
    couples = (amount - 1) // 2
    source_of, taker = tallies[1:1 + 2 * couples:2], tallies[2:2 + 2 * couples:2]
    margin = jnp.minimum(source_of - 1, reach - taker)
    shifted = jax.random.randint(jax.random.fold_in(rng, 1), (couples,), 0, 1 << 20) % (margin + 1)
    tallies = tallies.at[1:1 + 2 * couples:2].set(source_of - shifted).at[2:2 + 2 * couples:2].set(taker + shifted)
    return tallies[jax.random.permutation(jax.random.fold_in(rng, 2), amount)]


def normal_values(stream_key, shape, scale, bound, shards=(), kind=jnp.bfloat16):
    values = jax.random.normal(stream_key, shape, jnp.float32) * scale
    if len(shards) > 0:
        values = shard_levels(stream_key, shape, shards, -0.22, 0.18) * values
    return jnp.clip(values, min=-bound, max=bound).astype(kind)


def setup_inputs(seed: int = 0) -> dict:
    key_of = jax.random.split(jax.random.key(seed), 14)
    hidden = normal_values(key_of[0], (SEQS, LEN, D), 1.0, 6.0, ((0, 32),))
    segments = jax.vmap(lambda own: jnp.searchsorted(jnp.cumsum(uneven_parts(own, 6, LEN, LEN // 3, 1)), jnp.arange(LEN), side="right"))(jax.random.split(key_of[1], SEQS)).reshape((SEQS, LEN)).astype(jnp.int32)
    selected = draw_selected(jax.random.fold_in(key_of[13], 71), 0)
    w_query = normal_values(key_of[3], (D, D), D ** -0.5, 0.21875, ((0, 4),))
    w_key = normal_values(key_of[4], (D, D), D ** -0.5, 0.21875, ((0, 4),))
    w_value = normal_values(key_of[5], (D, D), D ** -0.5, 0.21875, ((0, 4),))
    w_out = normal_values(key_of[6], (D, D), (D // 16) ** -0.5, 0.875, ((0, 4),))
    w_up = normal_values(key_of[7], (D, FF), D ** -0.5, 0.21875, ((0, 4),))
    w_down = normal_values(key_of[8], (FF, D), FF ** -0.5, 0.109375, ((0, 4),))
    w_router = normal_values(key_of[9], (D,), D ** -0.5, 0.21875, ((0, 4),))
    gain_attn = jnp.clip(1.0 + 0.18 * jax.random.normal(key_of[10], (D,), jnp.float32), 0.099609375, 1.8984375).astype(jnp.bfloat16)
    gain_mlp = jnp.clip(1.0 + 0.18 * jax.random.normal(key_of[11], (D,), jnp.float32), 0.099609375, 1.8984375).astype(jnp.bfloat16)
    cotangent = normal_values(key_of[12], (SEQS, LEN, D), 1.0, 6.0, ((0, 32),))
    return {"hidden": hidden, "segments": segments, "selected": selected, "w_query": w_query, "w_key": w_key, "w_value": w_value, "w_out": w_out, "w_up": w_up, "w_down": w_down, "w_router": w_router, "gain_attn": gain_attn, "gain_mlp": gain_mlp, "cotangent": cotangent}


@jax.custom_vjp
def low(v):
    return lax.optimization_barrier(v.astype(jnp.bfloat16)).astype(jnp.float32)

@jax.custom_vjp
def low_back(v):
    return v

def low_keep(v):
    return (low(v), None)

def low_pass(kept, grad):
    return (grad,)

def back_keep(v):
    return (v, None)

def back_low(kept, grad):
    return (low(grad),)
low.defvjp(low_keep, low_pass)
low_back.defvjp(back_keep, back_low)
EPSILON = 1e-06
HIGHEST = lax.Precision.HIGHEST

def rms_scale(values):
    return lax.rsqrt(lax.optimization_barrier(jnp.mean(values * values, axis=-1, keepdims=True)) + EPSILON)

def one_sequence(weight_list, sequence):
    w_query, w_key, w_value, w_out, w_up, w_down, w_router, gain_attn, gain_mlp = weight_list
    tokens, segment_ids, chosen = sequence
    router_scores = jnp.dot(tokens, w_router, precision=HIGHEST)
    routed_tokens = tokens[chosen]
    gating = jax.nn.sigmoid(router_scores[chosen])
    normed = low(routed_tokens * rms_scale(routed_tokens) * gain_attn)
    query_rows = low_back(low(jnp.dot(normed, w_query, precision=HIGHEST))).reshape(KEEP, HEADS, HEAD_DIM)
    key_rows = low_back(low(jnp.dot(normed, w_key, precision=HIGHEST))).reshape(KEEP, HEADS, HEAD_DIM)
    value_rows = low_back(low(jnp.dot(normed, w_value, precision=HIGHEST))).reshape(KEEP, HEADS, HEAD_DIM)
    scores = low_back(jnp.einsum('qhe,khe->hqk', query_rows, key_rows, precision=HIGHEST) * 0.125)
    chosen_docs = segment_ids[chosen]
    allowed = (chosen[:, None] >= chosen[None, :]) & (chosen_docs[:, None] == chosen_docs[None, :])
    scores = jnp.where(allowed[None], scores, -1e+30)
    row_max = lax.optimization_barrier(jnp.max(scores, axis=-1, keepdims=True))
    exponent = jnp.exp(scores - row_max)
    probabilities = low(exponent / lax.optimization_barrier(jnp.sum(exponent, axis=-1, keepdims=True)))
    attended = jnp.einsum('hqk,khe->qhe', probabilities, value_rows, precision=HIGHEST).reshape(KEEP, D)
    attended = low_back(low(attended))
    attention_output = low_back(jnp.dot(attended, w_out, precision=HIGHEST))
    middle = routed_tokens + attention_output
    feedforward_normalized = low(middle * rms_scale(middle) * gain_mlp)
    before = low_back(jnp.dot(feedforward_normalized, w_up, precision=HIGHEST))
    activated = low(jax.nn.gelu(before, approximate=False))
    mlp_out = low_back(jnp.dot(activated, w_down, precision=HIGHEST))
    branch = gating[:, None] * (attention_output + mlp_out)
    return tokens.at[chosen].add(branch)

def reference(hidden, segments, selected, w_query, w_key, w_value, w_out, w_up, w_down, w_router, gain_attn, gain_mlp, cotangent):
    weight_list = tuple((weight.astype(jnp.float32) for weight in (w_query, w_key, w_value, w_out, w_up, w_down, w_router, gain_attn, gain_mlp)))

    def forward(tokens_all, weights_all):
        stepper = jax.checkpoint(lambda sequence: one_sequence(weights_all, sequence))
        return lax.map(stepper, (tokens_all, segments, selected))
    result, pullback = jax.vjp(forward, hidden.astype(jnp.float32), weight_list)
    grad_tokens, grads = pullback(cotangent.astype(jnp.float32))
    return (result.astype(jnp.bfloat16), grad_tokens.astype(jnp.bfloat16), grads[0], grads[1], grads[2], grads[3], grads[4], grads[5], grads[6], grads[7], grads[8])
```

```python
import functools

import jax
import jax.numpy as jnp
from jax import lax
from jax.experimental import pallas as pl
from jax.experimental.pallas import tpu as pltpu
from jax.sharding import PartitionSpec as P

HEADS = 12
HEAD_DIM = 64
PAIR = 2 * HEAD_DIM
EPSILON = 1e-06
F32 = jnp.float32
BF16 = jnp.bfloat16
TILE = 256
VECTOR_ROWS = 16
VMEM_BYTES = 56 * 1024 * 1024


def dot(left, right):
    return jnp.dot(left, right, preferred_element_type=F32)


def dot_nt(left, right):
    return lax.dot_general(left, right, (((1,), (1,)), ((), ())), preferred_element_type=F32)


def dot_tn(left, right):
    return lax.dot_general(left, right, (((0,), (0,)), ((), ())), preferred_element_type=F32)


def swap_bits(place):
    return ((place & 1) << 1) | (place >> 1)


def cost(flops, moved, transcendentals=0):
    return pl.CostEstimate(flops=flops, bytes_accessed=moved, transcendentals=transcendentals)


def params():
    return pltpu.CompilerParams(vmem_limit_bytes=VMEM_BYTES, dimension_semantics=None)


def column_of(row):
    size = row.shape[1]
    shape = (size, size)
    diagonal = lax.broadcasted_iota(jnp.int32, shape, 0) == lax.broadcasted_iota(jnp.int32, shape, 1)
    return jnp.sum(jnp.where(diagonal, row, 0.0), axis=1, keepdims=True)


def pick_kernel(with_mask, sel_ref, seg_ref, rows_ref, picked_ref, *rest):
    seq = pl.program_id(0)
    row = sel_ref[pl.ds(seq, 1), :].astype(F32)
    column = column_of(row)
    keep = row.shape[1]
    length = rows_ref.shape[1]
    places = lax.broadcasted_iota(jnp.int32, (keep, length), 1)
    chosen = jnp.where(column.astype(jnp.int32) == places, 1.0, 0.0).astype(BF16)
    picked_ref[0] = dot(chosen, rows_ref[0]).astype(BF16)
    if with_mask:
        (bias_ref,) = rest
        documents = jnp.broadcast_to(seg_ref[pl.ds(seq, 1), :].astype(F32), (8, length)).astype(BF16)
        of_column = dot_nt(chosen, documents)[:, :1]
        of_row = dot_nt(documents, chosen)[:1, :]
        allowed = (column >= row) & (of_column == of_row)
        bias_ref[0] = jnp.where(allowed, 0.0, -1e30).astype(BF16)


def pick_rows(selected, segments, rows, with_mask):
    seqs, length, width = rows.shape
    keep = selected.shape[1]
    whole = lambda a: pl.BlockSpec(a.shape, lambda s: (0, 0))
    out_shape = [jax.ShapeDtypeStruct((seqs, keep, width), BF16)]
    out_specs = [pl.BlockSpec((1, keep, width), lambda s: (s, 0, 0))]
    if with_mask:
        out_shape.append(jax.ShapeDtypeStruct((seqs, keep, keep), BF16))
        out_specs.append(pl.BlockSpec((1, keep, keep), lambda s: (s, 0, 0)))
    return pl.pallas_call(
        functools.partial(pick_kernel, with_mask),
        grid=(seqs,),
        in_specs=[whole(selected), whole(segments), pl.BlockSpec((1, length, width), lambda s: (s, 0, 0))],
        out_specs=out_specs,
        out_shape=out_shape,
        compiler_params=params(),
        cost_estimate=cost(2 * seqs * keep * length * width, rows.size * 2),
        name="pick_rows",
    )(selected, segments, rows)


def place_kernel(sel_ref, new_ref, base_ref, out_ref):
    seq, block = pl.program_id(0), pl.program_id(1)
    row = sel_ref[pl.ds(seq, 1), :]
    count = base_ref.shape[1]
    places = lax.broadcasted_iota(jnp.int32, (count, row.shape[1]), 0) + block * count
    hits = jnp.where(places == row, 1.0, 0.0)
    placed = dot(hits.astype(BF16), new_ref[0])
    hit = jnp.max(hits, axis=1, keepdims=True) > 0.0
    out_ref[0] = jnp.where(hit, placed, base_ref[0].astype(F32)).astype(BF16)


def place_rows(selected, new_rows, base):
    seqs, length, width = base.shape
    keep = selected.shape[1]
    count = length // 2
    return pl.pallas_call(
        place_kernel,
        grid=(seqs, length // count),
        in_specs=[
            pl.BlockSpec(selected.shape, lambda s, b: (0, 0)),
            pl.BlockSpec((1, keep, width), lambda s, b: (s, 0, 0)),
            pl.BlockSpec((1, count, width), lambda s, b: (s, b, 0)),
        ],
        out_specs=pl.BlockSpec((1, count, width), lambda s, b: (s, b, 0)),
        out_shape=jax.ShapeDtypeStruct(base.shape, BF16),
        compiler_params=params(),
        cost_estimate=cost(2 * seqs * keep * length * width, base.size * 4),
        name="place_rows",
    )(selected, new_rows.reshape(seqs, keep, width), base)


class Weight:
    def __init__(self, start, rows, columns, lanes):
        self.start, self.rows, self.columns, self.lanes = start, rows, columns, lanes


def weight_copies(idx_ref, parts, piece_refs, weight, own_ref, dst_ref, sem):
    shard, chip, core = idx_ref[0], idx_ref[1], idx_ref[2]
    shard_rows = own_ref.shape[0]
    lanes = weight.lanes
    own_at = pl.multiple_of(shard * shard_rows, 16)
    pltpu.make_async_copy(own_ref, dst_ref.at[pl.ds(own_at, shard_rows), :], sem).start()
    for (low, high, order), refs in zip(parts, piece_refs):
        for column in range(weight.columns):
            begin = weight.start + column * weight.rows
            lo, hi = max(begin, low), min(begin + weight.rows, high)
            if lo >= hi:
                continue
            for half in range(2):
                for second in range(2):
                    src = refs[2 * half + second]
                    for first in range(2):
                        x_bit, y_bit = (first, second) if order == "xy" else (second, first)
                        for other in range(3):
                            row = (shard ^ (other + 1)) * shard_rows + (chip ^ (2 * y_bit + x_bit)) * weight.rows
                            at = pl.multiple_of(row + (lo - begin), 16)
                            lane = pl.multiple_of((core ^ half) * (lanes * weight.columns) + column * lanes, 128)
                            pltpu.make_async_copy(
                                src.at[first, other, pl.ds(lo - low, hi - lo), :],
                                dst_ref.at[pl.ds(at, hi - lo), pl.ds(lane, lanes)],
                                sem,
                            ).start()

    def wait():
        pltpu.make_async_copy(dst_ref, dst_ref, sem).wait()

    return wait


def write_blocks(idx_ref, grad_ref, keep_ref, send_ref, start, rows, shard_rows):
    shard, chip, core = idx_ref[0], idx_ref[1], idx_ref[2]
    lanes = keep_ref.shape[-1]
    for x_bit in range(2):
        for y_bit in range(2):
            for place in range(4):
                row = (shard ^ swap_bits(place)) * shard_rows + (chip ^ (2 * y_bit + x_bit)) * rows
                at = pl.ds(pl.multiple_of(row, 16), rows)
                for half, out in ((0, keep_ref), (1, send_ref)):
                    lane = pl.ds(pl.multiple_of((core ^ half) * lanes, 128), lanes)
                    out[x_bit, y_bit, place, pl.ds(start, rows), :] = grad_ref[at, lane].astype(BF16)


def tiles_of(size):
    return size // TILE


def tile(index):
    return pl.ds(pl.multiple_of(index * TILE, TILE), TILE)


def loop(count, body):
    lax.fori_loop(0, count, lambda i, c: (body(i), c)[1], 0)


def inverse_rms(values):
    return lax.rsqrt(jnp.mean(values * values, axis=-1, keepdims=True) + EPSILON)


def attend_kernel(parts, weights, idx_ref, *refs):
    picked_ref, bias_ref, vec_ref, wq, wk, wv = refs[:6]
    count = 4 * len(parts)
    piece_refs = [refs[6 + 4 * i : 10 + 4 * i] for i in range(len(parts))]
    normed_ref, q_ref, k_ref, v_ref, probs_ref, att_ref, w_ref, sems = refs[6 + count :]
    seq = pl.program_id(0)
    keep = bias_ref.shape[1]
    seqs = picked_ref.shape[0] // keep

    @pl.when(seq == 0)
    def _():
        waits = [
            weight_copies(idx_ref, parts, piece_refs, weights[i], own, w_ref.at[i], sems.at[i])
            for i, own in enumerate((wq, wk, wv))
        ]
        gain = vec_ref[1:2, :]

        def norm(i):
            at = tile(i)
            values = picked_ref[at, :].astype(F32)
            normed_ref[at, :] = (values * inverse_rms(values) * gain).astype(BF16)

        loop(tiles_of(picked_ref.shape[0]), norm)
        for i, (out, scale) in enumerate(((q_ref, 0.125), (k_ref, 1.0), (v_ref, 1.0))):
            waits[i]()

            def project(n, i=i, out=out, scale=scale):
                result = dot(normed_ref[...], w_ref[i, :, tile(n)]).astype(BF16)
                out[:, tile(n)] = result * scale if scale != 1.0 else result

            loop(tiles_of(out.shape[1]), project)

    rows = pl.ds(pl.multiple_of(seq * keep, keep), keep)
    bias = bias_ref[0].astype(F32)
    low_half = lax.broadcasted_iota(jnp.int32, (keep, PAIR), 1) < HEAD_DIM

    def heads(pair):
        lanes = pl.ds(pl.multiple_of(pair * PAIR, PAIR), PAIR)
        queries, keys, values = q_ref[rows, lanes], k_ref[rows, lanes], v_ref[rows, lanes]
        results = []
        for half in range(2):
            mine = low_half if half == 0 else ~low_half
            scores = dot_nt(jnp.where(mine, queries, 0), keys) + bias
            exponent = jnp.exp(scores - jnp.max(scores, axis=-1, keepdims=True))
            probs = (exponent * (1.0 / jnp.sum(exponent, axis=-1, keepdims=True))).astype(BF16)
            probs_ref[0, 2 * pair + half] = probs
            results.append(dot(probs, values))
        att_ref[rows, lanes] = jnp.where(low_half, results[0], results[1]).astype(BF16)

    loop(HEADS // 2, heads)


def attend(idx, parts, weights, picked, bias, vectors, owns, pieces):
    tokens, width = picked.shape
    seqs, keep, _ = bias.shape
    fixed = lambda shape: pl.BlockSpec(shape, lambda s, i: (0,) * len(shape))
    anywhere = pl.BlockSpec(memory_space=pl.ANY)
    flat = jax.ShapeDtypeStruct((tokens, width), BF16)
    return pl.pallas_call(
        functools.partial(attend_kernel, parts, weights),
        grid_spec=pltpu.PrefetchScalarGridSpec(
            num_scalar_prefetch=1,
            grid=(seqs,),
            in_specs=[
                fixed((tokens, width)),
                pl.BlockSpec((1, keep, keep), lambda s, i: (s, 0, 0)),
                fixed(vectors.shape),
            ]
            + [anywhere] * (3 + len(pieces)),
            out_specs=[fixed((tokens, width))] * 4
            + [
                pl.BlockSpec((1, HEADS, keep, keep), lambda s, i: (s, 0, 0, 0)),
                fixed((tokens, width)),
            ],
            scratch_shapes=[pltpu.VMEM((3, width, width), BF16), pltpu.SemaphoreType.DMA((3,))],
        ),
        out_shape=[flat] * 4 + [jax.ShapeDtypeStruct((seqs, HEADS, keep, keep), BF16), flat],
        compiler_params=params(),
        cost_estimate=cost(2 * tokens * width * (3 * width + 8 * keep), tokens * width * 16),
        name="project_attend",
    )(idx, picked, bias, vectors, *owns, *pieces)


def gelu_parts(values):
    size = jnp.abs(values) * 0.7071067811865476
    bell = jnp.exp(-(size * size))
    t = 1.0 / (1.0 + 0.3275911 * size)
    poly = t * (0.254829592 + t * (-0.284496736 + t * (1.421413741 + t * (-1.453152027 + t * 1.061405429))))
    tail = 0.5 * poly * bell
    cdf = jnp.where(values >= 0.0, 1.0 - tail, tail)
    return values * cdf, cdf + values * (bell * 0.3989422804014327)


def up_kernel(parts, weights, idx_ref, *refs):
    att_ref, picked_ref, gbr_ref, vec_ref, w_out, w_up = refs[:6]
    count = 4 * len(parts)
    piece_refs = [refs[6 + 4 * i : 10 + 4 * i] for i in range(len(parts))]
    outs = refs[6 + count :]
    attn_ref, nm_ref, gmlp_ref, gating_ref, act_ref, slope_ref, keep_ref, send_ref, wo_ref, wu_ref, grad_ref, sems = outs
    step = pl.program_id(0)
    tokens = att_ref.shape[0]
    block = act_ref.shape[1]

    @pl.when(step == 0)
    def _():
        wait_out = weight_copies(idx_ref, parts, piece_refs, weights[0], w_out, wo_ref, sems.at[0])
        wait_up = weight_copies(idx_ref, parts, piece_refs, weights[1], w_up, wu_ref, sems.at[1])
        wait_out()

        def project(n):
            attn_ref[:, tile(n)] = dot(att_ref[...], wo_ref[:, tile(n)])

        loop(tiles_of(attn_ref.shape[1]), project)

        def norm(i):
            at = tile(i)
            values = picked_ref[at, :].astype(F32)
            middle = values + attn_ref[at, :]
            nm_ref[at, :] = (middle * inverse_rms(middle) * vec_ref[2:3, :]).astype(BF16)
            logit = jnp.sum(values * vec_ref[0:1, :], axis=-1, keepdims=True)
            gating = 1.0 / (1.0 + jnp.exp(-logit))
            gating_ref[at, :] = gating
            gmlp_ref[at, :] = (gating * gbr_ref[at, :].astype(F32)).astype(BF16)

        loop(tiles_of(tokens), norm)
        wait_up()

    base = (idx_ref[0] ^ swap_bits(step)) * block

    def columns(n):
        at = pl.ds(pl.multiple_of(base + n * TILE, TILE), TILE)
        before = dot(nm_ref[...], wu_ref[:, at])
        activated, slope = gelu_parts(before)
        activated = activated.astype(BF16)
        act_ref[:, tile(n)] = activated
        slope_ref[:, tile(n)] = slope.astype(BF16)
        grad_ref[tile(n), :] = dot_tn(activated, gmlp_ref[...])

    loop(tiles_of(block), columns)
    chip, core = idx_ref[1], idx_ref[2]
    rows, lanes = keep_ref.shape[-2:]
    for x_bit in range(2):
        for y_bit in range(2):
            at = pl.ds(pl.multiple_of((chip ^ (2 * y_bit + x_bit)) * rows, 16), rows)
            for half, out in ((0, keep_ref), (1, send_ref)):
                lane = pl.ds(pl.multiple_of((core ^ half) * lanes, 128), lanes)
                out[x_bit, y_bit, 0] = grad_ref[at, lane].astype(BF16)


def up(idx, parts, weights, attended, picked, branch_grad, vectors, owns, pieces):
    tokens, width = picked.shape
    hidden_units = owns[1].shape[1]
    block = hidden_units // 4
    rows, lanes = block // 4, width // 2
    fixed = lambda shape: pl.BlockSpec(shape, lambda s, i: (0,) * len(shape))
    anywhere = pl.BlockSpec(memory_space=pl.ANY)
    wide = pl.BlockSpec((tokens, block), lambda s, i: (0, i[0] ^ swap_bits(s)))
    grads = pl.BlockSpec((2, 2, 1, rows, lanes), lambda s, i: (0, 0, s, 0, 0))
    shape = jax.ShapeDtypeStruct
    return pl.pallas_call(
        functools.partial(up_kernel, parts, weights),
        grid_spec=pltpu.PrefetchScalarGridSpec(
            num_scalar_prefetch=1,
            grid=(4,),
            in_specs=[fixed((tokens, width))] * 3 + [fixed(vectors.shape)] + [anywhere] * (2 + len(pieces)),
            out_specs=[fixed((tokens, width))] * 3 + [fixed((tokens, 1)), wide, wide, grads, grads],
            scratch_shapes=[
                pltpu.VMEM((width, width), BF16),
                pltpu.VMEM((width, hidden_units), BF16),
                pltpu.VMEM((block, width), F32),
                pltpu.SemaphoreType.DMA((2,)),
            ],
        ),
        out_shape=[
            shape((tokens, width), F32),
            shape((tokens, width), BF16),
            shape((tokens, width), BF16),
            shape((tokens, 1), F32),
            shape((tokens, hidden_units), BF16),
            shape((tokens, hidden_units), BF16),
            shape((2, 2, 4, rows, lanes), BF16),
            shape((2, 2, 4, rows, lanes), BF16),
        ],
        compiler_params=params(),
        cost_estimate=cost(2 * tokens * width * (width + 2 * hidden_units), tokens * hidden_units * 8),
        name="project_up",
    )(idx, attended, picked, branch_grad, vectors, *owns, *pieces)


def norm_back(grad_normed, values, inverse, gain):
    scaled = grad_normed * gain
    grad_gain = jnp.sum(grad_normed * values * inverse, axis=0, keepdims=True)
    grad_values = inverse * scaled - values * (inverse * inverse * inverse) * jnp.mean(
        scaled * values, axis=-1, keepdims=True
    )
    return grad_values, grad_gain


def down_kernel(parts_up, weight_up, parts_down, weight_down, idx_ref, *refs):
    act_ref, slope_ref, nm_ref, gmlp_ref, attn_ref, picked_ref, gbr_ref, gating_ref, vec_ref, w_up, w_down = refs[:11]
    at = 11
    pieces_up = [refs[at + 4 * i : at + 4 * i + 4] for i in range(len(parts_up))]
    at += 4 * len(parts_up)
    pieces_down = [refs[at + 4 * i : at + 4 * i + 4] for i in range(len(parts_down))]
    at += 4 * len(parts_down)
    new_ref, gattn_ref, gmid_ref, glogit_ref, ggain_ref, keep_ref, send_ref = refs[at : at + 7]
    wu_ref, wd_ref, nmt_ref, mlp_ref, gnm_ref, grad_ref, sems = refs[at + 7 :]
    step = pl.program_id(0)
    tokens, block = act_ref.shape
    core = idx_ref[2]

    @pl.when(step == 0)
    def _():
        wait_up = weight_copies(idx_ref, parts_up, pieces_up, weight_up, w_up, wu_ref, sems.at[0])
        wait_down = weight_copies(idx_ref, parts_down, pieces_down, weight_down, w_down, wd_ref, sems.at[1])

        def turn(n):
            nmt_ref[tile(n), :] = nm_ref[:, tile(n)].T

        loop(tiles_of(nm_ref.shape[1]), turn)
        mlp_ref[...] = jnp.zeros_like(mlp_ref)
        gnm_ref[...] = jnp.zeros_like(gnm_ref)
        wait_up()
        wait_down()

    base = (step ^ (2 * core)) * block

    def columns(n):
        at = pl.ds(pl.multiple_of(base + n * TILE, TILE), TILE)
        down = wd_ref[at, :]
        mlp_ref[...] += dot(act_ref[:, tile(n)], down)
        grad_act = dot_nt(gmlp_ref[...], down)
        grad_before = (grad_act * slope_ref[:, tile(n)].astype(F32)).astype(BF16)
        grad_ref[:, tile(n)] = dot(nmt_ref[...], grad_before)
        gnm_ref[...] += dot_nt(grad_before, wu_ref[:, at])

    loop(tiles_of(block), columns)
    shard, chip = idx_ref[0], idx_ref[1]
    rows = weight_up.rows
    lanes = keep_ref.shape[-1]
    shard_rows = w_up.shape[0]

    def write(out):
        for x_bit in range(2):
            for y_bit in range(2):
                for place in range(4):
                    row = (shard ^ swap_bits(place)) * shard_rows + (chip ^ (2 * y_bit + x_bit)) * rows
                    at = pl.ds(pl.multiple_of(row, 16), rows)
                    for part in range(block // lanes):
                        out[x_bit, y_bit, place, pl.ds(part * rows, rows), :] = grad_ref[
                            at, pl.ds(part * lanes, lanes)
                        ].astype(BF16)

    @pl.when(step < 2)
    def _():
        write(keep_ref)

    @pl.when(step >= 2)
    def _():
        write(send_ref)

    @pl.when(step == pl.num_programs(0) - 1)
    def _():
        ggain_ref[...] = jnp.zeros_like(ggain_ref)

        def finish(i):
            at = tile(i)
            attention = attn_ref[at, :]
            values = picked_ref[at, :].astype(F32)
            gating = gating_ref[at, :]
            branch_grad = gbr_ref[at, :].astype(F32)
            delta = attention + mlp_ref[at, :]
            new_ref[at, :] = (values + gating * delta).astype(BF16)
            grad_gating = jnp.sum(branch_grad * delta, axis=-1, keepdims=True)
            glogit_ref[at, :] = grad_gating * gating * (1.0 - gating)
            middle = values + attention
            grad_middle, grad_gain = norm_back(gnm_ref[at, :], middle, inverse_rms(middle), vec_ref[2:3, :])
            gmid_ref[at, :] = grad_middle
            gattn_ref[at, :] = (gating * branch_grad + grad_middle).astype(BF16)
            ggain_ref[0:1, :] += grad_gain

        loop(tiles_of(tokens), finish)


def down(idx, parts_up, weight_up, parts_down, weight_down, arrays, vectors, owns, pieces):
    activated, slope, normed, grad_mlp, attn_out, picked, branch_grad, gating = arrays
    tokens, width = picked.shape
    hidden_units = activated.shape[1]
    block = hidden_units // 4
    lanes = width // 2
    parts_of = block // lanes
    rows = weight_up.rows
    fixed = lambda shape: pl.BlockSpec(shape, lambda s, i: (0,) * len(shape))
    anywhere = pl.BlockSpec(memory_space=pl.ANY)
    wide = pl.BlockSpec((tokens, block), lambda s, i: (0, s ^ (2 * i[2])))
    grads = lambda at: pl.BlockSpec((2, 2, 4, parts_of * rows, lanes), lambda s, i: (0, 0, 0, at(s), 0))
    shape = jax.ShapeDtypeStruct
    flat = fixed((tokens, width))
    column = fixed((tokens, 1))
    grad_shape = shape((2, 2, 4, 2 * parts_of * rows, lanes), BF16)
    return pl.pallas_call(
        functools.partial(down_kernel, parts_up, weight_up, parts_down, weight_down),
        grid_spec=pltpu.PrefetchScalarGridSpec(
            num_scalar_prefetch=1,
            grid=(4,),
            in_specs=[wide, wide] + [flat] * 5 + [column, fixed(vectors.shape)] + [anywhere] * (2 + len(pieces)),
            out_specs=[flat] * 3
            + [
                column,
                fixed((8, width)),
                grads(lambda s: jnp.minimum(s, 1)),
                grads(lambda s: jnp.maximum(s, 2) - 2),
            ],
            scratch_shapes=[
                pltpu.VMEM((width, hidden_units), BF16),
                pltpu.VMEM((hidden_units, width), BF16),
                pltpu.VMEM((width, tokens), BF16),
                pltpu.VMEM((tokens, width), F32),
                pltpu.VMEM((tokens, width), F32),
                pltpu.VMEM((width, block), F32),
                pltpu.SemaphoreType.DMA((2,)),
            ],
        ),
        out_shape=[
            shape((tokens, width), BF16),
            shape((tokens, width), BF16),
            shape((tokens, width), F32),
            shape((tokens, 1), F32),
            shape((8, width), F32),
            grad_shape,
            grad_shape,
        ],
        compiler_params=params(),
        cost_estimate=cost(2 * tokens * width * 4 * hidden_units, tokens * hidden_units * 8),
        name="project_down_and_back",
    )(idx, activated, slope, normed, grad_mlp, attn_out, picked, branch_grad, gating, vectors, *owns, *pieces)


def attend_back_kernel(parts, weight, idx_ref, *refs):
    gattn_ref, att_ref, q_ref, k_ref, v_ref, probs_ref, w_out = refs[:7]
    count = 4 * len(parts)
    piece_refs = [refs[7 + 4 * i : 11 + 4 * i] for i in range(len(parts))]
    gq_ref, gk_ref, gv_ref, keep_ref, send_ref, w_ref, gatt_ref, grad_ref, sems = refs[7 + count :]
    seq = pl.program_id(0)
    keep = probs_ref.shape[2]

    @pl.when(seq == 0)
    def _():
        wait = weight_copies(idx_ref, parts, piece_refs, weight, w_out, w_ref, sems.at[0])

        def grads(n):
            grad_ref[tile(n), :] = dot_tn(att_ref[:, tile(n)], gattn_ref[...])

        loop(tiles_of(att_ref.shape[1]), grads)
        write_blocks(idx_ref, grad_ref, keep_ref, send_ref, 0, weight.rows, w_out.shape[0])
        wait()

        def project(n):
            gatt_ref[:, tile(n)] = dot_nt(gattn_ref[...], w_ref[tile(n), :]).astype(BF16)

        loop(tiles_of(att_ref.shape[1]), project)

    rows = pl.ds(pl.multiple_of(seq * keep, keep), keep)
    low_half = lax.broadcasted_iota(jnp.int32, (keep, PAIR), 1) < HEAD_DIM

    def heads(pair):
        lanes = pl.ds(pl.multiple_of(pair * PAIR, PAIR), PAIR)
        queries, keys, values = q_ref[rows, lanes], k_ref[rows, lanes], v_ref[rows, lanes]
        grad_att = gatt_ref[rows, lanes]
        found = []
        for half in range(2):
            mine = low_half if half == 0 else ~low_half
            probs = probs_ref[0, 2 * pair + half]
            grad_values = dot_tn(probs, grad_att)
            wide = probs.astype(F32)
            weighted = wide * dot_nt(jnp.where(mine, grad_att, 0), values)
            scores = (weighted - wide * jnp.sum(weighted, axis=-1, keepdims=True)).astype(BF16)
            found.append((dot(scores, keys) * 0.125, dot_tn(scores, queries), grad_values))
        for out, first, second in zip((gq_ref, gk_ref, gv_ref), *found):
            out[rows, lanes] = jnp.where(low_half, first, second).astype(BF16)

    loop(HEADS // 2, heads)


def attend_back(idx, parts, weight, grad_attn, attended, queries, keys, values, probs, own, pieces):
    tokens, width = grad_attn.shape
    seqs, _, keep, _ = probs.shape
    lanes = width // 2
    fixed = lambda shape: pl.BlockSpec(shape, lambda s, i: (0,) * len(shape))
    anywhere = pl.BlockSpec(memory_space=pl.ANY)
    flat = fixed((tokens, width))
    grad_shape = (2, 2, 4, weight.rows, lanes)
    shape = jax.ShapeDtypeStruct
    return pl.pallas_call(
        functools.partial(attend_back_kernel, parts, weight),
        grid_spec=pltpu.PrefetchScalarGridSpec(
            num_scalar_prefetch=1,
            grid=(seqs,),
            in_specs=[flat] * 5
            + [pl.BlockSpec((1, HEADS, keep, keep), lambda s, i: (s, 0, 0, 0))]
            + [anywhere] * (1 + len(pieces)),
            out_specs=[flat] * 3 + [fixed(grad_shape)] * 2,
            scratch_shapes=[
                pltpu.VMEM((width, width), BF16),
                pltpu.VMEM((tokens, width), BF16),
                pltpu.VMEM((width, width), F32),
                pltpu.SemaphoreType.DMA((1,)),
            ],
        ),
        out_shape=[shape((tokens, width), BF16)] * 3 + [shape(grad_shape, BF16)] * 2,
        compiler_params=params(),
        cost_estimate=cost(2 * tokens * width * (2 * width + 20 * keep), tokens * width * 24),
        name="attend_back",
    )(idx, grad_attn, attended, queries, keys, values, probs, own, *pieces)


def project_back_kernel(parts, weights, idx_ref, *refs):
    gq_ref, gk_ref, gv_ref, normed_ref, picked_ref, gmid_ref, gbr_ref, glogit_ref, vec_ref, ggain_ref = refs[:10]
    wq, wk, wv = refs[10:13]
    count = 4 * len(parts)
    piece_refs = [refs[13 + 4 * i : 17 + 4 * i] for i in range(len(parts))]
    new_ref, keep_ref, send_ref, w_ref, nt_ref, gn_ref, grad_ref, sum_ref, sems = refs[13 + count :]
    waits = [
        weight_copies(idx_ref, parts, piece_refs, weights[i], own, w_ref.at[i], sems.at[i])
        for i, own in enumerate((wq, wk, wv))
    ]
    width = normed_ref.shape[1]

    def turn(n):
        nt_ref[tile(n), :] = normed_ref[:, tile(n)].T

    loop(tiles_of(width), turn)
    for i, grad in enumerate((gq_ref, gk_ref, gv_ref)):
        def grads(n, grad=grad):
            grad_ref[:, tile(n)] = dot(nt_ref[...], grad[:, tile(n)])

        loop(tiles_of(width), grads)
        write_blocks(idx_ref, grad_ref, keep_ref, send_ref, i * weights[i].rows, weights[i].rows, wq.shape[0])
        waits[i]()

        def project(n, i=i, grad=grad):
            result = dot_nt(grad[...], w_ref[i, tile(n), :])
            gn_ref[:, tile(n)] = result if i == 0 else gn_ref[:, tile(n)] + result

        loop(tiles_of(width), project)
    sum_ref[...] = jnp.zeros_like(sum_ref)

    def finish(i):
        at = tile(i)
        values = picked_ref[at, :].astype(F32)
        grad_picked, grad_gain = norm_back(gn_ref[at, :], values, inverse_rms(values), vec_ref[1:2, :])
        grad_logit = glogit_ref[at, :]
        new_ref[at, :] = (
            gbr_ref[at, :].astype(F32) + grad_logit * vec_ref[0:1, :] + (grad_picked + gmid_ref[at, :])
        ).astype(BF16)
        sum_ref[0:1, :] += jnp.sum(grad_logit * values, axis=0, keepdims=True)
        sum_ref[1:2, :] += grad_gain

    loop(tiles_of(picked_ref.shape[0]), finish)
    sum_ref[2:3, :] = ggain_ref[0:1, :]
    lanes = keep_ref.shape[-1]
    start = sum(weight.rows for weight in weights)
    lows = sum_ref[:, :lanes]
    highs = sum_ref[:, lanes:]
    both = jnp.concatenate([lows, highs], axis=0).astype(BF16)
    for x_bit in range(2):
        for y_bit in range(2):
            for place in range(4):
                for out in (keep_ref, send_ref):
                    out[x_bit, y_bit, place, pl.ds(start, VECTOR_ROWS), :] = both


def project_back(idx, parts, weights, arrays, vectors, grad_gain, owns, pieces):
    tokens, width = arrays[0].shape
    lanes = width // 2
    fixed = lambda shape: pl.BlockSpec(shape, lambda g, i: (0,) * len(shape))
    anywhere = pl.BlockSpec(memory_space=pl.ANY)
    flat = fixed((tokens, width))
    grad_shape = (2, 2, 4, sum(weight.rows for weight in weights) + VECTOR_ROWS, lanes)
    shape = jax.ShapeDtypeStruct
    return pl.pallas_call(
        functools.partial(project_back_kernel, parts, weights),
        grid_spec=pltpu.PrefetchScalarGridSpec(
            num_scalar_prefetch=1,
            grid=(1,),
            in_specs=[flat] * 7
            + [fixed((tokens, 1)), fixed(vectors.shape), fixed(grad_gain.shape)]
            + [anywhere] * (3 + len(pieces)),
            out_specs=[flat] + [fixed(grad_shape)] * 2,
            scratch_shapes=[
                pltpu.VMEM((3, width, width), BF16),
                pltpu.VMEM((width, tokens), BF16),
                pltpu.VMEM((tokens, width), F32),
                pltpu.VMEM((width, width), F32),
                pltpu.VMEM((8, width), F32),
                pltpu.SemaphoreType.DMA((3,)),
            ],
        ),
        out_shape=[shape((tokens, width), BF16)] + [shape(grad_shape, BF16)] * 2,
        compiler_params=params(),
        cost_estimate=cost(2 * tokens * width * 6 * width, tokens * width * 30),
        name="project_back",
    )(idx, *arrays, vectors, grad_gain, *owns, *pieces)


def solution(mesh):
    replicas, shards = mesh.shape["rep"], mesh.shape["fsdp"]
    rep_pairs = lambda bit: [(i, i ^ bit) for i in range(replicas)]
    shard_pairs = lambda bit: [(i, i ^ bit) for i in range(shards)]
    groups = [list(range(i, i + 8)) for i in range(0, replicas, 8)]
    plane = {"c": 1, "x": 2, "y": 4}

    def swap(values, way):
        return lax.ppermute(values, "rep", rep_pairs(plane[way]))

    def swap_shard(values, bit):
        return lax.ppermute(values, "fsdp", shard_pairs(bit))

    def gather_shards(own):
        second = swap_shard(own, 2)
        pair = swap_shard(jnp.stack([own, second]), 1)
        return jnp.stack([pair[0], second, pair[1]])

    def gather_plane(blocks, parts):
        pieces = []
        for low, high, order in parts:
            mine = blocks[:, low:high]
            both = jnp.stack([mine, swap(mine, order[0])])
            other = swap(both, order[1])
            pieces += [both, other, swap(both, "c"), swap(other, "c")]
        return pieces

    def add(left, right):
        return (left.astype(F32) + right.astype(F32)).astype(BF16)

    def reduce_blocks(keep, send, order):
        got = swap(send, "c")
        if order == "yx":
            keep, got = keep.swapaxes(0, 1), got.swapaxes(0, 1)
        for way in order:
            away, keep = add(keep[1], got[1]), add(keep[0], got[0])
            got = swap(away, way)
        keep, got = [a.reshape((2, 2) + a.shape[1:]) for a in (keep, got)]
        for bit in (1, 2):
            away, keep = add(keep[1], got[1]), add(keep[0], got[0])
            got = swap_shard(away, bit)
        total = keep.astype(F32) + got.astype(F32)
        bit = 8
        while bit < replicas:
            total = total + lax.ppermute(total, "rep", rep_pairs(bit))
            bit *= 2
        return total

    def gather_rows(total):
        return lax.all_gather(
            total.astype(BF16), "rep", axis=0, tiled=False, axis_index_groups=groups if len(groups) > 1 else None
        )

    def unpack(rows, weight, start):
        part = rows[:, start : start + weight.rows * weight.columns]
        part = part.reshape(4, 2, weight.columns, weight.rows, weight.lanes)
        part = part.transpose(0, 3, 1, 2, 4)
        return part.reshape(4 * weight.rows, 2 * weight.columns * weight.lanes).astype(F32)

    def on_device(
        hidden,
        segments,
        selected,
        w_query,
        w_key,
        w_value,
        w_out,
        w_up,
        w_down,
        w_router,
        gain_attn,
        gain_mlp,
        cotangent,
    ):
        seqs, length, width = hidden.shape
        keep = selected.shape[1]
        tokens = seqs * keep
        lanes = width // 2
        place = lax.axis_index("rep") % 8
        shard, chip, core = lax.axis_index("fsdp"), place // 2, place % 2
        idx = jnp.stack([shard, chip, core]).astype(jnp.int32)

        def cut(weight):
            rows, columns = weight.shape[0] // 4, weight.shape[1] // 2
            block = lax.dynamic_slice(weight, (chip * rows, core * columns), (rows, columns))
            parts = columns // lanes
            if parts > 1:
                block = block.reshape(rows, parts, lanes).swapaxes(0, 1).reshape(rows * parts, lanes)
            return block

        small, tall = w_query.shape[0] // 4, w_down.shape[0] // 4
        wide = w_up.shape[1] // 2 // lanes
        q_at, k_at, v_at = [Weight(i * small, small, 1, lanes) for i in range(3)]
        out_at, up_at = Weight(0, small, 1, lanes), Weight(small, small, wide, lanes)
        down_at = Weight(0, tall, 1, lanes)
        first_rows = 3 * small
        first_parts = [(0, 64, "xy"), (64, first_rows, "yx")]
        second_rows = small + small * wide
        second_parts = [(0, 128, "xy"), (128, second_rows, "yx")]
        third_parts = [(0, tall // 2, "xy"), (tall // 2, tall, "yx")]

        with jax.named_scope("gather_weights"):
            vectors = jnp.stack([w_router, gain_attn, gain_mlp])
            first_own = jnp.concatenate([cut(w) for w in (w_query, w_key, w_value)])
            padded = jnp.pad(vectors, ((0, VECTOR_ROWS - 3), (0, lanes - vectors.shape[1])))
            first = gather_shards(jnp.concatenate([first_own, padded]))
            first_pieces = gather_plane(first, first_parts)
            second = gather_shards(jnp.concatenate([cut(w_out), cut(w_up)]))
            second_pieces = gather_plane(second, second_parts)
            third = gather_shards(cut(w_down))
            third_pieces = gather_plane(third, third_parts)
            others = first[:, first_rows : first_rows + 3, : vectors.shape[1]]
            by_place = jnp.concatenate([vectors[None], others])
            at = jnp.arange(shards)
            vec = sum(
                jnp.where((at == (shard ^ i))[None, :, None], by_place[i][:, None, :], 0) for i in range(shards)
            )
            vec = jnp.pad(vec.reshape(3, width).astype(F32), ((0, 5), (0, 0)))

        picked, bias = pick_rows(selected, segments, hidden, True)
        (branch_grad,) = pick_rows(selected, segments, cotangent, False)
        picked, branch_grad = picked.reshape(tokens, width), branch_grad.reshape(tokens, width)
        normed, queries, keys, values, probs, attended = attend(
            idx, first_parts, (q_at, k_at, v_at), picked, bias, vec, (w_query, w_key, w_value), first_pieces
        )
        attn_out, normed_mlp, grad_mlp, gating, activated, slope, down_keep, down_send = up(
            idx, second_parts, (out_at, up_at), attended, picked, branch_grad, vec, (w_out, w_up), second_pieces
        )
        with jax.named_scope("reduce_down"):
            total_down = gather_rows(reduce_blocks(down_keep, down_send, "xy"))
        new_rows, grad_attn, grad_middle, grad_logit, grad_gain_m, up_keep, up_send = down(
            idx,
            second_parts,
            up_at,
            third_parts,
            down_at,
            (activated, slope, normed_mlp, grad_mlp, attn_out, picked, branch_grad, gating),
            vec,
            (w_up, w_down),
            second_pieces + third_pieces,
        )
        with jax.named_scope("reduce_up"):
            total_up = gather_rows(reduce_blocks(up_keep, up_send, "yx"))
        grad_q, grad_k, grad_v, out_keep, out_send = attend_back(
            idx, second_parts, out_at, grad_attn, attended, queries, keys, values, probs, w_out, second_pieces
        )
        grad_rows, first_keep, first_send = project_back(
            idx,
            first_parts,
            (q_at, k_at, v_at),
            (grad_q, grad_k, grad_v, normed, picked, grad_middle, branch_grad, grad_logit),
            vec,
            grad_gain_m,
            (w_query, w_key, w_value),
            first_pieces,
        )
        with jax.named_scope("reduce_out"):
            total_out = gather_rows(reduce_blocks(out_keep, out_send, "xy"))
        with jax.named_scope("reduce_first"):
            summed = reduce_blocks(first_keep, first_send, "yx")
            total_first = gather_rows(summed[:first_rows])
            sums = summed[first_rows:].reshape(2, 8, lanes)[:, :3].swapaxes(0, 1).reshape(3, width)
            sums = lax.dynamic_slice(sums, (0, shard * w_router.shape[0]), (3, w_router.shape[0]))
        out_hidden = place_rows(selected, new_rows, hidden)
        grad_hidden = place_rows(selected, grad_rows, cotangent)
        return (
            out_hidden,
            grad_hidden,
            unpack(total_first, q_at, 0),
            unpack(total_first, k_at, small),
            unpack(total_first, v_at, 2 * small),
            unpack(total_out, out_at, 0),
            unpack(total_up, up_at, 0),
            unpack(total_down, down_at, 0),
            sums[0],
            sums[1],
            sums[2],
        )

    placed = (
        P(("rep", "fsdp"), None, None),
        P(("rep", "fsdp"), None),
        P(("rep", "fsdp"), None),
        P("fsdp", None),
        P("fsdp", None),
        P("fsdp", None),
        P("fsdp", None),
        P("fsdp", None),
        P("fsdp", None),
        P("fsdp"),
        P("fsdp"),
        P("fsdp"),
        P(("rep", "fsdp"), None, None),
    )
    return jax.shard_map(
        on_device,
        mesh=mesh,
        in_specs=placed,
        out_specs=(
            P(("rep", "fsdp"), None, None),
            P(("rep", "fsdp"), None, None),
            P("fsdp", None),
            P("fsdp", None),
            P("fsdp", None),
            P("fsdp", None),
            P("fsdp", None),
            P("fsdp", None),
            P("fsdp"),
            P("fsdp"),
            P("fsdp"),
        ),
        check_vma=False,
    )
```

```python
import functools

import jax
import jax.numpy as jnp
from jax import lax
from jax.experimental import pallas as pl
from jax.experimental.pallas import tpu as pltpu
from jax.sharding import PartitionSpec as P

HEADS = 12
HEAD_DIM = 64
PAIR = 2 * HEAD_DIM
EPSILON = 1e-06
F32 = jnp.float32
BF16 = jnp.bfloat16
TILE = 256
VECTOR_ROWS = 16
VMEM_BYTES = 16 * 1024 * 1024


def dot(left, right):
    return jnp.dot(left, right, preferred_element_type=F32)


def dot_nt(left, right):
    return lax.dot_general(left, right, (((1,), (1,)), ((), ())), preferred_element_type=F32)


def dot_tn(left, right):
    return lax.dot_general(left, right, (((0,), (0,)), ((), ())), preferred_element_type=F32)


def swap_bits(place):
    return ((place & 1) << 1) | (place >> 1)


def own_place():
    member = lax.axis_index("rep") & 7
    return lax.axis_index("fsdp"), member >> 1, member & 1


def micros(time):
    return pl.CostEstimate(flops=int(time * 1.1e9), bytes_accessed=0, transcendentals=0)


def like(shape, dtype):
    return jax.ShapeDtypeStruct(shape, dtype)


def params(limit=VMEM_BYTES):
    return pltpu.CompilerParams(vmem_limit_bytes=limit)


ANYWHERE = pl.BlockSpec(memory_space=pl.ANY)
INSIDE = pl.BlockSpec(memory_space=pltpu.VMEM)
LAST = []


def ordered(kernel, ins, in_specs, **options):
    before = tuple(LAST)

    def body(*refs):
        kernel(*refs[len(before) :])

    outs = pl.pallas_call(body, in_specs=[ANYWHERE] * len(before) + in_specs, **options)(*before, *ins)
    LAST[:] = [min(outs, key=lambda out: out.size)]
    return outs


def call(kernel, name, ins, outs, estimate, scratch=()):
    return ordered(
        kernel,
        ins,
        [INSIDE] * len(ins),
        out_specs=[INSIDE] * len(outs),
        out_shape=list(outs),
        scratch_shapes=list(scratch),
        compiler_params=params(),
        cost_estimate=micros(estimate),
        name=name,
    )


def pick_kernel(with_mask, sel_ref, seg_ref, rows_ref, picked_ref, *rest):
    seq = pl.program_id(0)
    row = sel_ref[pl.ds(seq, 1), :].astype(F32)
    keep = row.shape[1]
    square = (keep, keep)
    diagonal = lax.broadcasted_iota(jnp.int32, square, 0) == lax.broadcasted_iota(jnp.int32, square, 1)
    column = jnp.sum(jnp.where(diagonal, row, 0.0), axis=1, keepdims=True)
    length = rows_ref.shape[1]
    places = lax.broadcasted_iota(jnp.int32, (keep, length), 1)
    chosen = jnp.where(column.astype(jnp.int32) == places, 1.0, 0.0).astype(BF16)
    picked_ref[...] = dot(chosen, rows_ref[0]).astype(BF16)
    if with_mask:
        (bias_ref,) = rest
        documents = jnp.broadcast_to(seg_ref[pl.ds(seq, 1), :].astype(F32), (8, length)).astype(BF16)
        of_column = dot_nt(chosen, documents)[:, :1]
        of_row = jnp.sum(jnp.where(diagonal, of_column, 0.0), axis=0, keepdims=True)
        allowed = (row >= column) & (of_column == of_row)
        bias_ref[0] = jnp.where(allowed, 0.0, -1e30).astype(BF16)


def pick_rows(selected, segments, rows, with_mask):
    seqs, length, width = rows.shape
    keep = selected.shape[1]
    whole = lambda a: pl.BlockSpec(a.shape, lambda s: (0, 0))
    outs = [(like((seqs * keep, width), BF16), pl.BlockSpec((keep, width), lambda s: (s, 0)))]
    if with_mask:
        outs.append((like((seqs, keep, keep), BF16), pl.BlockSpec((1, keep, keep), lambda s: (s, 0, 0))))
    return ordered(
        functools.partial(pick_kernel, with_mask),
        (selected, segments, rows),
        [whole(selected), whole(segments), pl.BlockSpec((1, length, width), lambda s: (s, 0, 0))],
        grid=(seqs,),
        out_specs=[spec for _, spec in outs],
        out_shape=[shape for shape, _ in outs],
        compiler_params=params(),
        cost_estimate=micros(8),
        name="pick_rows",
    )


def place_kernel(sel_ref, new_ref, base_ref, out_ref):
    seq, block = pl.program_id(0), pl.program_id(1)
    row = sel_ref[pl.ds(seq, 1), :]
    count = base_ref.shape[1]
    places = lax.broadcasted_iota(jnp.int32, (count, row.shape[1]), 0) + block * count
    hits = jnp.where(places == row, 1.0, 0.0)
    placed = dot(hits.astype(BF16), new_ref[...])
    hit = jnp.max(hits, axis=1, keepdims=True) > 0.0
    out_ref[0] = jnp.where(hit, placed, base_ref[0].astype(F32)).astype(BF16)


def place_rows(selected, new_rows, base):
    seqs, length, width = base.shape
    keep = selected.shape[1]
    count = length // 2
    block = pl.BlockSpec((1, count, width), lambda s, b: (s, b, 0))
    return ordered(
        place_kernel,
        (selected, new_rows, base),
        [
            pl.BlockSpec(selected.shape, lambda s, b: (0, 0)),
            pl.BlockSpec((keep, width), lambda s, b: (s, 0)),
            block,
        ],
        grid=(seqs, length // count),
        out_specs=[block],
        out_shape=[like(base.shape, BF16)],
        compiler_params=params(),
        cost_estimate=micros(11),
        name="place_rows",
    )[0]


class Weight:
    def __init__(self, start, rows, columns, lanes, split=None):
        self.start, self.rows, self.columns, self.lanes, self.split = start, rows, columns, lanes, split
        self.parts = 1 if split is None else 2
        self.half = columns * lanes
        self.shape = (16 * rows, 2 * self.half)

    def slots(self):
        return [(self.start + c * self.rows, c * self.lanes) for c in range(self.columns)]


def aligned(value, size, multiple):
    return pl.ds(pl.multiple_of(value, multiple), size)


def pack_kernel(weights, *refs):
    _, chip, core = own_place()
    *ins, out_ref = refs
    for own, weight in zip(ins, weights):
        for start, lane in weight.slots():
            out_ref[start : start + weight.rows, :] = own[
                aligned(chip * weight.rows, weight.rows, 16), aligned(core * weight.half + lane, weight.lanes, 128)
            ]
    for extra in ins[len(weights) :]:
        out_ref[out_ref.shape[0] - extra.shape[0] :, :] = extra[...]


def pack(owns, weights, extra=()):
    rows = sum(w.rows * w.columns for w in weights) + sum(e.shape[0] for e in extra)
    return call(
        functools.partial(pack_kernel, weights),
        "pack_blocks",
        (*owns, *extra),
        [like((rows, weights[0].lanes), BF16)],
        0.5,
    )[0]


def join_own_kernel(own_ref, second_ref, out_ref):
    out_ref[0] = own_ref[...]
    out_ref[1] = second_ref[...]


def join_own(own, second):
    return call(join_own_kernel, "join_own", (own, second), [like((2, *own.shape), BF16)], 0.2)[0]


def join_shards_kernel(pair_ref, second_ref, *outs):
    start = 0
    for out in outs:
        rows = slice(start, start + out.shape[1])
        start = rows.stop
        out[0] = pair_ref[0, rows, :]
        out[1] = second_ref[rows, :]
        out[2] = pair_ref[1, rows, :]


def join_shards(pair, second, cuts):
    _, rows, lanes = pair.shape
    edges = [0, *cuts, rows]
    outs = [like((3, high - low, lanes), BF16) for low, high in zip(edges, edges[1:])]
    return call(join_shards_kernel, "join_shards", (pair, second), outs, 0.3)


def join_chips_kernel(first_ref, first_got, last_ref, last_got, first_out, last_out, both_out):
    cut = first_ref.shape[1]
    for at, (first, last) in enumerate(((first_ref, last_ref), (first_got, last_got))):
        first_out[at] = first[...]
        last_out[at] = last[...]
        both_out[at, :, :cut, :] = first[...]
        both_out[at, :, cut:, :] = last[...]


def join_chips(first, first_got, last, last_got):
    count, cut, lanes = first.shape
    rows = last.shape[1]
    shapes = [(2, count, cut, lanes), (2, count, rows, lanes), (2, count, cut + rows, lanes)]
    return call(
        join_chips_kernel, "join_chips", (first, first_got, last, last_got), [like(s, BF16) for s in shapes], 0.5
    )


def join_rows_kernel(*refs):
    *ins, out = refs
    start = 0
    for ref in ins:
        rows = ref.shape[-2]
        out[..., start : start + rows, :] = ref[...]
        start += rows


def join_rows(*arrays):
    shape = list(arrays[0].shape)
    shape[-2] = sum(a.shape[-2] for a in arrays)
    return call(join_rows_kernel, "join_rows", arrays, [like(shape, BF16)], 0.3)[0]


def join_kernel(*refs):
    *ins, out = refs
    for at, ref in enumerate(ins):
        out[at] = ref[...]


def join(*arrays):
    return call(join_kernel, "join", arrays, [like((len(arrays), *arrays[0].shape), BF16)], 0.2)[0]


def assemble_kernel(weights, layout, *refs):
    shard, chip, core = own_place()
    count = len(layout)
    owns, refs = refs[: len(weights)], refs[len(weights) :]
    pieces, outs = (refs[:count], refs[count : 2 * count]), list(refs[2 * count :])
    for weight, own in zip(weights, owns):
        shard_rows = own.shape[0]
        targets = [outs.pop(0) for _ in range(weight.parts)]

        def fill(place_of):
            if weight.split == "columns":
                for half in range(2):
                    out, row, lane = place_of(0, half)
                    out[row, lane] = own[:, aligned((core ^ half) * weight.half, weight.half, 128)]
            else:
                out, row, _ = place_of(0, 0)
                out[row, :] = own[...]
            for half in range(2):
                for number, ranges in enumerate(layout):
                    ref = pieces[half][number]
                    for start, lane in weight.slots():
                        for low, high, chips in ranges:
                            lo, hi = max(start, low), min(start + weight.rows, high)
                            if lo >= hi:
                                continue
                            for at, offset in enumerate(chips):
                                for other in range(3):
                                    inner = (chip ^ offset) * weight.rows + (lo - start)
                                    out, row, lanes = place_of(other + 1, half, inner, hi - lo, lane, weight.lanes)
                                    out[row, lanes] = ref[at, other, lo:hi, :]

        if weight.split == "columns":

            def place_of(other, half, inner=0, rows=shard_rows, lane=0, lanes=weight.half):
                return targets[half], aligned((shard ^ other) * shard_rows + inner, rows, 16), slice(lane, lane + lanes)

            fill(place_of)
        elif weight.split == "rows":
            for near in range(2):

                def place_of(other, half, inner=0, rows=shard_rows, lane=0, lanes=0):
                    row = ((shard ^ other) & 1) * shard_rows + inner
                    at = aligned((core ^ half) * weight.half + lane, lanes, 128) if lanes else slice(None)
                    return targets[near ^ (other >> 1)], aligned(row, rows, 16), at

                pl.when(((shard >> 1) ^ core) == near)(functools.partial(fill, place_of))
        else:

            def place_of(other, half, inner=0, rows=shard_rows, lane=0, lanes=0):
                at = aligned((core ^ half) * weight.half + lane, lanes, 128) if lanes else slice(None)
                return targets[0], aligned((shard ^ other) * shard_rows + inner, rows, 16), at

            fill(place_of)


def assemble(owns, weights, layout, pieces):
    outs = []
    for weight in weights:
        rows, columns = weight.shape
        if weight.split == "columns":
            outs += [like((rows, columns // 2), BF16)] * 2
        elif weight.split == "rows":
            outs += [like((rows // 2, columns), BF16)] * 2
        else:
            outs.append(like((rows, columns), BF16))
    return call(
        functools.partial(assemble_kernel, weights, layout),
        "assemble_weights",
        (*owns, *pieces),
        outs,
        0.3 * sum(w.columns * w.rows for w in weights) / 48,
    )


def write_blocks(grad_ref, keep_ref, send_ref, start, rows):
    shard, chip, core = own_place()
    lanes = keep_ref.shape[-1]
    for x_bit in range(2):
        for y_bit in range(2):
            for place in range(4):
                row = (shard ^ swap_bits(place)) * (4 * rows) + (chip ^ (2 * y_bit + x_bit)) * rows
                for half, out in ((0, keep_ref), (1, send_ref)):
                    out[x_bit, y_bit, place, start : start + rows, :] = grad_ref[
                        aligned(row, rows, 16), aligned((core ^ half) * lanes, lanes, 128)
                    ].astype(BF16)


def tiles(size, step=TILE):
    return [slice(i, i + step) for i in range(0, size, step)]


def inverse_rms(values):
    return lax.rsqrt(jnp.mean(values * values, axis=-1, keepdims=True) + EPSILON)


def project_kernel(picked_ref, vec_ref, wq, wk, wv, normed_ref, q_ref, k_ref, v_ref):
    for at in tiles(picked_ref.shape[0]):
        values = picked_ref[at, :].astype(F32)
        normed_ref[at, :] = (values * inverse_rms(values) * vec_ref[1:2, :]).astype(BF16)
    q_ref[...] = dot(normed_ref[...], wq[...]).astype(BF16) * 0.125
    k_ref[...] = dot(normed_ref[...], wk[...]).astype(BF16)
    v_ref[...] = dot(normed_ref[...], wv[...]).astype(BF16)


def project(picked, vectors, weights):
    flat = like(picked.shape, BF16)
    return call(project_kernel, "project", (picked, vectors, *weights), [flat] * 4, 4.5)


def low_half_lanes(rows):
    return lax.broadcasted_iota(jnp.int32, (rows, PAIR), 1) < HEAD_DIM


def attend_kernel(bias_ref, q_ref, k_ref, v_ref, probs_ref, att_ref):
    seqs, keep, _ = bias_ref.shape
    low_half = low_half_lanes(keep)

    def sequence(seq, carry):
        bias = bias_ref[seq].astype(F32)
        rows = aligned(seq * keep, keep, keep)
        for pair in range(HEADS // 2):
            lanes = slice(pair * PAIR, (pair + 1) * PAIR)
            queries, keys, values = q_ref[rows, lanes], k_ref[rows, lanes], v_ref[rows, lanes]
            results = []
            for half in range(2):
                mine = low_half if half == 0 else ~low_half
                scores = dot_nt(jnp.where(mine, keys, 0), queries) + bias
                exponent = jnp.exp(scores - jnp.max(scores, axis=0, keepdims=True))
                probs = (exponent * (1.0 / jnp.sum(exponent, axis=0, keepdims=True))).astype(BF16)
                probs_ref[seq, 2 * pair + half] = probs
                results.append(dot_tn(probs, values))
            att_ref[rows, lanes] = jnp.where(low_half, results[0], results[1]).astype(BF16)
        return carry

    lax.fori_loop(0, seqs, sequence, 0)


def attend(bias, queries, keys, values):
    seqs, keep, _ = bias.shape
    return call(
        attend_kernel,
        "attend",
        (bias, queries, keys, values),
        [like((seqs, HEADS, keep, keep), BF16), like(queries.shape, BF16)],
        6.5,
    )


def out_kernel(att_ref, wo_ref, picked_ref, gbr_ref, vec_ref, attn_ref, nm_ref, gmlp_ref, gating_ref):
    attn_ref[...] = dot(att_ref[...], wo_ref[...])
    for at in tiles(picked_ref.shape[0]):
        values = picked_ref[at, :].astype(F32)
        middle = values + attn_ref[at, :]
        nm_ref[at, :] = (middle * inverse_rms(middle) * vec_ref[2:3, :]).astype(BF16)
        logit = jnp.sum(values * vec_ref[0:1, :], axis=-1, keepdims=True)
        gating = 1.0 / (1.0 + jnp.exp(-logit))
        gating_ref[at, :] = gating
        gmlp_ref[at, :] = (gating * gbr_ref[at, :].astype(F32)).astype(BF16)


def project_out(attended, w_out, picked, branch_grad, vectors):
    flat = like(picked.shape, BF16)
    return call(
        out_kernel,
        "project_out",
        (attended, w_out, picked, branch_grad, vectors),
        [like(picked.shape, F32), flat, flat, like((picked.shape[0], 1), F32)],
        2.0,
    )


def gelu_parts(values):
    cdf = 0.5 * (1.0 + lax.erf(values * 0.7071067811865476))
    return values * cdf, cdf + values * (jnp.exp(-0.5 * values * values) * 0.3989422804014327)


def up_kernel(nm_ref, gmlp_ref, wu_ref, act_ref, slope_ref, grad_ref):
    tokens = nm_ref.shape[0]
    for columns in tiles(wu_ref.shape[1], wu_ref.shape[1] // 2):
        for at in tiles(tokens, 128):
            activated, slope = gelu_parts(dot(nm_ref[at, :], wu_ref[:, columns]))
            act_ref[at, columns] = activated.astype(BF16)
            slope_ref[at, columns] = slope.astype(BF16)
        grad_ref[columns, :] = dot_tn(act_ref[:, columns], gmlp_ref[...]).astype(BF16)


def project_up(normed, grad_mlp, w_up):
    tokens, width = normed.shape
    units = w_up.shape[1]
    wide = like((tokens, units), BF16)
    return call(
        up_kernel,
        "project_up",
        (normed, grad_mlp, w_up),
        [wide, wide, like((units, width), BF16)],
        6.0,
    )


def down_blocks_kernel(near_ref, far_ref, keep_ref, send_ref):
    shard, chip, core = own_place()
    rows, lanes = keep_ref.shape[-2:]
    shard_rows = 4 * rows

    def fill(near):
        for place in range(4):
            other = swap_bits(place)
            ref = (near_ref, far_ref)[near ^ (other >> 1)]
            for x_bit in range(2):
                for y_bit in range(2):
                    row = ((shard ^ other) & 1) * shard_rows + (chip ^ (2 * y_bit + x_bit)) * rows
                    for half, out in ((0, keep_ref), (1, send_ref)):
                        out[x_bit, y_bit, place] = ref[
                            aligned(row, rows, 16), aligned((core ^ half) * lanes, lanes, 128)
                        ]

    for near in range(2):
        pl.when(((shard >> 1) ^ core) == near)(functools.partial(fill, near))


def down_blocks(near, far):
    units, width = near.shape
    blocks = like((2, 2, 4, units // 8, width // 2), BF16)
    return call(down_blocks_kernel, "down_blocks", (near, far), [blocks, blocks], 0.7)


def norm_back(grad_normed, values, inverse, gain):
    scaled = grad_normed * gain
    grad_gain = jnp.sum(grad_normed * values * inverse, axis=0, keepdims=True)
    grad_values = inverse * scaled - values * (inverse * inverse * inverse) * jnp.mean(
        scaled * values, axis=-1, keepdims=True
    )
    return grad_values, grad_gain


def down_kernel(weight, act_ref, slope_ref, nm_ref, gmlp_ref, wu_ref, wd_ref, *refs):
    *starts, mlp_ref, gnm_ref, out_ref, grad_ref = refs
    shard, chip, core = own_place()
    block = wd_ref.shape[0] // 2
    rows, lanes = weight.rows, weight.lanes

    for step, at in enumerate(tiles(wd_ref.shape[0], block)):
        down = wd_ref[at, :]
        mlp = dot(act_ref[:, at], down)
        grad_before = (dot_nt(gmlp_ref[...], down) * slope_ref[:, at].astype(F32)).astype(BF16)
        grad_ref[...] = dot_tn(nm_ref[...], grad_before)
        grad_nm = dot_nt(grad_before, wu_ref[:, at])
        if step == 1:
            mlp_ref[...] += mlp
            gnm_ref[...] += grad_nm
        elif starts:
            mlp_ref[...] = starts[0][...] + mlp
            gnm_ref[...] = starts[1][...] + grad_nm
        else:
            mlp_ref[...] = mlp
            gnm_ref[...] = grad_nm
        for x_bit in range(2):
            for y_bit in range(2):
                for place in range(4):
                    row = (shard ^ swap_bits(place)) * (4 * rows) + (chip ^ (2 * y_bit + x_bit)) * rows
                    for part in range(block // lanes):
                        start = (step * (block // lanes) + part) * rows
                        out_ref[x_bit, y_bit, place, start : start + rows, :] = grad_ref[
                            aligned(row, rows, 16), part * lanes : (part + 1) * lanes
                        ].astype(BF16)


def down(weight, activated, slope, normed, grad_mlp, w_up, w_down, starts=()):
    tokens, width = normed.shape
    total = like((tokens, width), F32)
    return call(
        functools.partial(down_kernel, weight),
        "down_and_back",
        (activated, slope, normed, grad_mlp, w_up, w_down, *starts),
        [total, total, like((2, 2, 4, weight.rows * weight.columns, weight.lanes), BF16)],
        8.5,
        scratch=[pltpu.VMEM((width, w_up.shape[1] // 2), F32)],
    )


def branch_kernel(
    mlp_ref, gnm_ref, attn_ref, picked_ref, gbr_ref, gating_ref, vec_ref, new_ref, gattn_ref, gmid_ref, glogit_ref, sum_ref
):
    total = jnp.zeros((1, vec_ref.shape[1]), F32)
    for at in tiles(picked_ref.shape[0]):
        attention = attn_ref[at, :]
        values = picked_ref[at, :].astype(F32)
        gating = gating_ref[at, :]
        branch_grad = gbr_ref[at, :].astype(F32)
        delta = attention + mlp_ref[at, :]
        new_ref[at, :] = (values + gating * delta).astype(BF16)
        grad_gating = jnp.sum(branch_grad * delta, axis=-1, keepdims=True)
        glogit_ref[at, :] = grad_gating * gating * (1.0 - gating)
        middle = values + attention
        grad_middle, grad_gain = norm_back(gnm_ref[at, :], middle, inverse_rms(middle), vec_ref[2:3, :])
        gmid_ref[at, :] = grad_middle
        gattn_ref[at, :] = (gating * branch_grad + grad_middle).astype(BF16)
        total = total + grad_gain
    sum_ref[...] = jnp.broadcast_to(total, sum_ref.shape)


def branch(mlp, grad_nm, attn_out, picked, branch_grad, gating, vectors):
    tokens, width = picked.shape
    return call(
        branch_kernel,
        "branch_and_norm_back",
        (mlp, grad_nm, attn_out, picked, branch_grad, gating, vectors),
        [
            like((tokens, width), BF16),
            like((tokens, width), BF16),
            like((tokens, width), F32),
            like((tokens, 1), F32),
            like((8, width), F32),
        ],
        2.0,
    )


def out_back_kernel(weight, gattn_ref, att_ref, wo_ref, gatt_ref, keep_ref, send_ref, grad_ref):
    grad_ref[...] = dot_tn(att_ref[...], gattn_ref[...])
    gatt_ref[...] = dot_nt(gattn_ref[...], wo_ref[...]).astype(BF16)
    write_blocks(grad_ref, keep_ref, send_ref, 0, weight.rows)


def out_back(weight, grad_attn, attended, w_out):
    blocks = like((2, 2, 4, weight.rows, weight.lanes), BF16)
    return call(
        functools.partial(out_back_kernel, weight),
        "project_out_back",
        (grad_attn, attended, w_out),
        [like(grad_attn.shape, BF16), blocks, blocks],
        2.5,
        scratch=[pltpu.VMEM(weight.shape, F32)],
    )


def attend_back_kernel(seq, gatt_ref, q_ref, k_ref, v_ref, probs_ref, gq_ref, gk_ref, gv_ref):
    keep = probs_ref.shape[2]
    low_half = low_half_lanes(keep)
    rows = slice(seq * keep, (seq + 1) * keep)
    for pair in range(HEADS // 2):
        lanes = slice(pair * PAIR, (pair + 1) * PAIR)
        queries, keys, values = q_ref[rows, lanes], k_ref[rows, lanes], v_ref[rows, lanes]
        grad_att = gatt_ref[rows, lanes]
        found = []
        for half in range(2):
            mine = low_half if half == 0 else ~low_half
            probs = probs_ref[seq, 2 * pair + half]
            wide = probs.astype(F32)
            weighted = wide * dot_nt(jnp.where(mine, values, 0), grad_att)
            scores = (weighted - wide * jnp.sum(weighted, axis=0, keepdims=True)).astype(BF16)
            found.append((dot_tn(scores, keys) * 0.125, dot(scores, queries), dot(probs, grad_att)))
        for out, first, second in zip((gq_ref, gk_ref, gv_ref), *found):
            out[:, lanes] = jnp.where(low_half, first, second).astype(BF16)


def attend_back(seq, grad_attended, queries, keys, values, probs):
    rows = like((probs.shape[2], queries.shape[1]), BF16)
    return call(
        functools.partial(attend_back_kernel, seq),
        "attend_back",
        (grad_attended, queries, keys, values, probs),
        [rows] * 3,
        4.0,
    )


def project_grads_kernel(weights, normed_ref, *refs):
    *grads, keep_ref, send_ref, grad_ref = refs
    for i, weight in enumerate(weights):
        grad_ref[...] = dot_tn(normed_ref[...], rows_of(grads, i))
        write_blocks(grad_ref, keep_ref, send_ref, weight.start, weight.rows)


def rows_of(grads, i):
    return jnp.concatenate([ref[...] for ref in grads[i::3]], axis=0)


def project_grads(weights, normed, grads):
    blocks = like((2, 2, 4, sum(w.rows for w in weights), weights[0].lanes), BF16)
    return call(
        functools.partial(project_grads_kernel, weights),
        "project_gradients",
        (normed, *grads),
        [blocks, blocks],
        4.0,
        scratch=[pltpu.VMEM(weights[0].shape, F32)],
    )


def project_back_kernel(count, *refs):
    grads, refs = refs[:count], refs[count:]
    wq, wk, wv, picked_ref, gmid_ref, gbr_ref, glogit_ref, vec_ref, middle_ref, new_ref, sum_ref, gn_ref = refs
    gn_ref[...] = sum(dot_nt(rows_of(grads, i), w[...]) for i, w in enumerate((wq, wk, wv)))
    router = jnp.zeros((1, vec_ref.shape[1]), F32)
    total = router
    for at in tiles(picked_ref.shape[0]):
        values = picked_ref[at, :].astype(F32)
        grad_picked, grad_gain = norm_back(gn_ref[at, :], values, inverse_rms(values), vec_ref[1:2, :])
        grad_logit = glogit_ref[at, :]
        new_ref[at, :] = (
            gbr_ref[at, :].astype(F32) + grad_logit * vec_ref[0:1, :] + (grad_picked + gmid_ref[at, :])
        ).astype(BF16)
        router = router + jnp.sum(grad_logit * values, axis=0, keepdims=True)
        total = total + grad_gain
    rows = jnp.concatenate([router, total, middle_ref[0:1, :], jnp.zeros((5, router.shape[1]), F32)], axis=0)
    lanes = sum_ref.shape[1]
    sum_ref[...] = jnp.concatenate([rows[:, :lanes], rows[:, lanes:]], axis=0).astype(BF16)


def project_back(grads, weights, picked, grad_middle, branch_grad, grad_logit, vectors, gain_sums):
    tokens, width = picked.shape
    return call(
        functools.partial(project_back_kernel, len(grads)),
        "project_back",
        (*grads, *weights, picked, grad_middle, branch_grad, grad_logit, vectors, gain_sums),
        [like((tokens, width), BF16), like((VECTOR_ROWS, width // 2), BF16)],
        5.0,
        scratch=[pltpu.VMEM((tokens, width), F32)],
    )


def total_of(left, right):
    return (left.astype(F32) + right.astype(F32)).astype(BF16)


def add_first_kernel(cut, parts, extra, *refs):
    *refs, a_away, a_keep, b_away, b_keep = refs
    start = 0

    def put(x_bit, y_bit, at, begin, value):
        low, high = begin, begin + value.shape[-2]
        if low < cut:
            out = a_away if x_bit else a_keep
            out[y_bit, at, low : min(high, cut), :] = value[: min(high, cut) - low]
        if high > cut:
            out = b_away if y_bit else b_keep
            out[x_bit, at, max(low, cut) - cut : high - cut, :] = value[max(low, cut) - low :]

    for number in range(parts):
        keep, got = refs[2 * number], refs[2 * number + 1]
        for x_bit in range(2):
            for y_bit in range(2):
                for at in range(keep.shape[2]):
                    put(x_bit, y_bit, at, start, total_of(keep[x_bit, y_bit, at], got[x_bit, y_bit, at]))
        start += keep.shape[3]
    if extra:
        value = total_of(refs[-2][...], refs[-1][...])
        for x_bit in range(2):
            for y_bit in range(2):
                for at in range(4):
                    put(x_bit, y_bit, at, start, value)


def add_first(pairs, cut, extra=()):
    lanes = pairs[0][0].shape[-1]
    rows = sum(keep.shape[3] for keep, _ in pairs) + (extra[0].shape[0] if extra else 0)
    out = lambda n: like((2, 4, n, lanes), BF16)
    return call(
        functools.partial(add_first_kernel, cut, len(pairs), bool(extra)),
        "add_first",
        [array for pair in pairs for array in pair] + list(extra),
        [out(cut), out(cut), out(rows - cut), out(rows - cut)],
        0.7,
    )


def add_second_kernel(a_ref, a_got, b_ref, b_got, a_away, a_keep, b_away, b_keep):
    for ref, got, away, keep in ((a_ref, a_got, a_away, a_keep), (b_ref, b_got, b_away, b_keep)):
        for at in range(ref.shape[1]):
            keep[at] = total_of(ref[0, at], got[0, at])
            away[at] = total_of(ref[1, at], got[1, at])


def add_second(a_keep, a_got, b_keep, b_got):
    a_like, b_like = [like(array.shape[1:], BF16) for array in (a_keep, b_keep)]
    return call(
        add_second_kernel, "add_second", (a_keep, a_got, b_keep, b_got), [a_like, a_like, b_like, b_like], 0.5
    )


def add_third_kernel(a_ref, a_got, b_ref, b_got, away, keep):
    cut = a_ref.shape[1]
    for out, first in ((away, 2), (keep, 0)):
        for at in range(2):
            out[at, :cut, :] = total_of(a_ref[first + at], a_got[first + at])
            out[at, cut:, :] = total_of(b_ref[first + at], b_got[first + at])


def add_third(a_keep, a_got, b_keep, b_got):
    half = like((2, a_keep.shape[1] + b_keep.shape[1], a_keep.shape[2]), BF16)
    return call(add_third_kernel, "add_third", (a_keep, a_got, b_keep, b_got), [half, half], 0.4)


def add_fourth_kernel(keep_ref, got_ref, away, keep):
    away[...] = total_of(keep_ref[1], got_ref[1])
    keep[...] = total_of(keep_ref[0], got_ref[0])


def add_fourth(keep, got):
    half = like(keep.shape[1:], BF16)
    return call(add_fourth_kernel, "add_fourth", (keep, got), [half, half], 0.3)


def add_last_kernel(*refs):
    *refs, out = refs
    start = 0
    for keep, got in zip(refs[::2], refs[1::2]):
        rows = keep.shape[0]
        out[start : start + rows, :] = total_of(keep[...], got[...])
        start += rows


def add_last(*pairs):
    shape = (sum(keep.shape[0] for keep, _ in pairs), pairs[0][0].shape[1])
    return call(add_last_kernel, "add_last", [a for pair in pairs for a in pair], [like(shape, BF16)], 0.3)[0]


def unpack_kernel(weights, own_ref, other_ref, own_far_ref, other_far_ref, *outs):
    _, chip, core = own_place()
    for weight, out in zip(weights, outs):
        for half, (own, other) in enumerate(((own_ref, other_ref), (own_far_ref, other_far_ref))):
            for offset in range(4):
                at = aligned((chip ^ offset) * weight.rows, weight.rows, 16)
                for start, lane in weight.slots():
                    rows = slice(start, start + weight.rows)
                    block = own[rows, :] if offset == 0 else other[offset - 1, rows, :]
                    out[at, aligned((core ^ half) * weight.half + lane, weight.lanes, 128)] = block.astype(F32)


def unpack(weights, own, other, own_far, other_far):
    return call(
        functools.partial(unpack_kernel, weights),
        "unpack_gradients",
        (own, other, own_far, other_far),
        [like((weight.shape[0] // 4, weight.shape[1]), F32) for weight in weights],
        2.0,
    )


def solution(mesh):
    replicas, shards = mesh.shape["rep"], mesh.shape["fsdp"]
    rep_pairs = lambda bits: [(i, i ^ bits) for i in range(replicas)]
    shard_pairs = lambda bits: [(i, i ^ bits) for i in range(shards)]
    plane = {"c": 1, "x": 2, "y": 4, "d": 6}

    def swap(values, way):
        return lax.ppermute(values, "rep", rep_pairs(plane[way]))

    def swap_shard(values, bits):
        return lax.ppermute(values, "fsdp", shard_pairs(bits))

    def swap_halves(halves, order="xy"):
        first, last = halves[:2]
        return first, swap(first, order[0]), last, swap(last, order[1])

    def swap_sums(sums, order):
        a_away, a_keep, b_away, b_keep = sums
        return a_keep, swap(a_away, order[0]), b_keep, swap(b_away, order[1])

    def over_planes(own):
        bit = 8
        while bit < replicas:
            own = total_of(own, lax.ppermute(own, "rep", rep_pairs(bit)))
            bit *= 2
        return own

    def on_device(
        hidden,
        segments,
        selected,
        w_query,
        w_key,
        w_value,
        w_out,
        w_up,
        w_down,
        w_router,
        gain_attn,
        gain_mlp,
        cotangent,
    ):
        LAST.clear()
        width = hidden.shape[2]
        seqs = hidden.shape[0]
        lanes = width // 2
        shard = lax.axis_index("fsdp")

        small, tall = w_query.shape[0] // 4, w_down.shape[0] // 4
        wide = w_up.shape[1] // 2 // lanes
        first_weights = [Weight(i * small, small, 1, lanes) for i in range(3)]
        up_at, out_at = Weight(0, small, wide, lanes, "columns"), Weight(small * wide, small, 1, lanes)
        down_at = Weight(0, tall, 1, lanes, "rows")
        first_rows, second_rows = 3 * small, small * (wide + 1)
        first_cut, second_cut, third_cut = 64, 128, tall // 2
        halved = lambda rows, cut: [
            [(0, cut, (0, 1)), (cut, rows, (0, 2))],
            [(0, cut, (2, 3)), (cut, rows, (1, 3))],
        ]
        vectors = jnp.stack([w_router, gain_attn, gain_mlp])
        padded = jnp.pad(vectors, ((0, VECTOR_ROWS - 3), (0, lanes - vectors.shape[1])))

        first_own = pack((w_query, w_key, w_value), first_weights)
        first_second = swap_shard(first_own, 2)
        first_pair = swap_shard(join_own(first_own, first_second), 1)
        second_own = pack((w_up, w_out), (up_at, out_at), (padded,))
        second_second = swap_shard(second_own, 2)
        first = swap_halves(join_shards(first_pair, first_second, [first_cut]))
        third_own = pack((w_down,), (down_at,))
        third_second = swap_shard(third_own, 2)
        picked, bias = pick_rows(selected, segments, hidden, True)
        *first, first_both = join_chips(*first)
        first = swap_halves(first, "yx")
        first_both_far = swap(first_both, "c")
        second_pair = swap_shard(join_own(second_own, second_second), 1)
        (branch_grad,) = pick_rows(selected, segments, cotangent, False)
        *second, others = join_shards(second_pair, second_second, [second_cut, second_rows])
        second = swap_halves(second)
        third_pair = swap_shard(join_own(third_own, third_second), 1)
        by_place = jnp.concatenate([vectors[None], others[:, :3, : vectors.shape[1]]])
        at = jnp.arange(shards)
        vec = sum(jnp.where((at == (shard ^ i))[None, :, None], by_place[i][:, None, :], 0) for i in range(shards))
        vec = jnp.pad(vec.reshape(3, width).astype(F32), ((0, 5), (0, 0)))
        first_other = join_rows(first[1], first[3])
        first_other_far = swap(first_other, "c")
        third = swap_halves(join_shards(third_pair, third_second, [third_cut]))
        qkv = assemble(
            (w_query, w_key, w_value),
            first_weights,
            halved(first_rows, first_cut),
            (first_both, first_other, first_both_far, first_other_far),
        )
        normed, queries, keys, values = project(picked, vec, qkv)
        *second, second_both = join_chips(*second)
        second = swap_halves(second, "yx")
        second_both_far = swap(second_both, "c")
        probs, attended = attend(bias, queries, keys, values)
        *third, third_both = join_chips(*third)
        second_other = join_rows(second[1], second[3])
        second_other_far = swap(second_other, "c")
        third = swap_halves(third, "yx")
        third_both_far = swap(third_both, "c")
        up_near, up_far, full_out = assemble(
            (w_up, w_out),
            (up_at, out_at),
            halved(second_rows, second_cut),
            (second_both, second_other, second_both_far, second_other_far),
        )
        attn_out, normed_mlp, grad_mlp, gating = project_out(attended, full_out, picked, branch_grad, vec)
        act_far, slope_far, grad_far = project_up(normed_mlp, grad_mlp, up_far)
        act_near, slope_near, grad_near = project_up(normed_mlp, grad_mlp, up_near)

        down_keep, down_send = down_blocks(grad_near, grad_far)
        down_got = swap(down_send, "c")
        third_other = join_rows(third[1], third[3])
        third_other_far = swap(third_other, "c")
        down_near, down_far = assemble(
            (w_down,), (down_at,), halved(tall, third_cut), (third_both, third_other, third_both_far, third_other_far)
        )
        mlp, grad_nm, up_send = down(up_at, act_far, slope_far, normed_mlp, grad_mlp, up_far, down_far)
        up_got = swap(up_send, "c")
        d_sums = swap_sums(add_first([(down_keep, down_got)], tall // 2), "xy")
        mlp, grad_nm, up_keep = down(
            up_at, act_near, slope_near, normed_mlp, grad_mlp, up_near, down_near, (mlp, grad_nm)
        )
        new_rows, grad_attn, grad_middle, grad_logit, gain_sums = branch(
            mlp, grad_nm, attn_out, picked, branch_grad, gating, vec
        )
        grad_attended, out_keep, out_send = out_back(out_at, grad_attn, attended, full_out)
        out_got = swap(out_send, "c")
        d_sums = swap_sums(add_second(*d_sums), "yx")
        u_sums = swap_sums(add_first([(up_keep, up_got), (out_keep, out_got)], 112), "xy")
        grads = []
        for seq in range(seqs - 1):
            grads += attend_back(seq, grad_attended, queries, keys, values, probs)
        d_away, d_keep = add_third(*d_sums)
        d_got = swap_shard(d_away, 1)
        grads += attend_back(seqs - 1, grad_attended, queries, keys, values, probs)
        first_keep, first_send = project_grads(first_weights, normed, grads)
        first_got = swap(first_send, "c")
        d_away, d_keep = add_fourth(d_keep, d_got)
        d_got = swap_shard(d_away, 2)
        grad_rows, sums = project_back(
            grads, qkv, picked, grad_middle, branch_grad, grad_logit, vec, gain_sums
        )
        sums_got = swap(sums, "c")
        f_sums = swap_sums(add_first([(first_keep, first_got)], 80, (sums, sums_got)), "xy")
        u_sums = swap_sums(add_second(*u_sums), "yx")
        out_hidden = place_rows(selected, new_rows, hidden)
        u_away, u_keep = add_third(*u_sums)
        u_got = swap_shard(u_away, 1)
        grad_hidden = place_rows(selected, grad_rows, cotangent)
        f_sums = swap_sums(add_second(*f_sums), "yx")
        u_away, u_keep = add_fourth(u_keep, u_got)
        u_got = swap_shard(u_away, 2)
        f_away, f_keep = add_third(*f_sums)
        f_got = swap_shard(f_away, 1)
        mlp_own = over_planes(add_last((d_keep, d_got), (u_keep, u_got)))
        mlp_spread = [swap(mlp_own, way) for way in "xyd"]
        mlp_far = swap(mlp_own, "c")
        f_away, f_keep = add_fourth(f_keep, f_got)
        f_got = swap_shard(f_away, 2)
        mlp_others = join(*mlp_spread)
        mlp_others_far = swap(mlp_others, "c")
        f_own = over_planes(add_last((f_keep, f_got)))
        f_spread = [swap(f_own, way) for way in "xyd"]
        f_far = swap(f_own, "c")
        places = (Weight(0, tall, 1, lanes), Weight(tall, small, wide, lanes), Weight(tall + small * wide, small, 1, lanes))
        grad_down, grad_up, grad_out = unpack(places, mlp_own, mlp_others, mlp_far, mlp_others_far)
        f_others = join(*f_spread)
        grad_qkv = unpack(first_weights, f_own, f_others, f_far, swap(f_others, "c"))
        sums = f_own[first_rows:].reshape(2, 8, lanes)[:, :3].swapaxes(0, 1).reshape(3, width).astype(F32)
        sums = lax.dynamic_slice(sums, (0, shard * w_router.shape[0]), (3, w_router.shape[0]))
        return (out_hidden, grad_hidden, *grad_qkv, grad_out, grad_up, grad_down, sums[0], sums[1], sums[2])

    placed = (
        P(("rep", "fsdp"), None, None),
        P(("rep", "fsdp"), None),
        P(("rep", "fsdp"), None),
        P("fsdp", None),
        P("fsdp", None),
        P("fsdp", None),
        P("fsdp", None),
        P("fsdp", None),
        P("fsdp", None),
        P("fsdp"),
        P("fsdp"),
        P("fsdp"),
        P(("rep", "fsdp"), None, None),
    )
    return jax.shard_map(
        on_device,
        mesh=mesh,
        in_specs=placed,
        out_specs=(
            P(("rep", "fsdp"), None, None),
            P(("rep", "fsdp"), None, None),
            P("fsdp", None),
            P("fsdp", None),
            P("fsdp", None),
            P("fsdp", None),
            P("fsdp", None),
            P("fsdp", None),
            P("fsdp"),
            P("fsdp"),
            P("fsdp"),
        ),
        check_vma=False,
    )
```

```python
import functools

import jax
import jax.numpy as jnp
from jax import lax
from jax.experimental import pallas as pl
from jax.experimental.pallas import tpu as pltpu
from jax.sharding import PartitionSpec as P

HEADS = 12
HEAD_DIM = 64
PAIR = 2 * HEAD_DIM
EPSILON = 1e-06
F32 = jnp.float32
BF16 = jnp.bfloat16
TILE = 256
VECTOR_ROWS = 16
VMEM_BYTES = 10 * 1024 * 1024
STREAM_BYTES = 28 * 1024 * 1024


def dot(left, right):
    return jnp.dot(left, right, preferred_element_type=F32)


def dot_nt(left, right):
    return lax.dot_general(left, right, (((1,), (1,)), ((), ())), preferred_element_type=F32)


def dot_tn(left, right):
    return lax.dot_general(left, right, (((0,), (0,)), ((), ())), preferred_element_type=F32)


def swap_bits(place):
    return ((place & 1) << 1) | (place >> 1)


def own_place():
    member = lax.axis_index("rep") & 7
    return lax.axis_index("fsdp"), member >> 1, member & 1


def micros(time):
    return pl.CostEstimate(flops=int(time * 1.1e9), bytes_accessed=0, transcendentals=0)


BESIDE = {
    "choose": (0.1,),
    "pick_rows": (1.6, 3.0),
    "join_chips": (1.2, 9.0, 9.0),
    "join_rows": (0.1, 0.2, 9.0),
    "join_own": (0.2, 0.1, 4.4),
    "pack_blocks": (0.1, 0.1, 2.0),
    "project": (1.4,),
    "attend": (2.7,),
    "project_out": (0.8,),
    "project_up": (2.0, 2.0),
    "down_and_back": (24.0, 24.0),
    "attend_back": (6.0, 2.5, 2.9),
    "project_back": (3.8,),
    "place_rows": (3.3, 2.0, 2.5),
    "add_fourth": (0.1, 0.1, 6.0),
    "add_last": (14.5, 0.1, 7.5),
    "join": (0.1, 2.5, 0.1, 0.1),
    "unpack_gradients": (1.3, 1.3, 0.1),
}
CALLS = {}


def beside(name):
    number = CALLS.get(name, 0)
    CALLS[name] = number + 1
    times = BESIDE.get(name, (0.1,))
    return micros(times[min(number, len(times) - 1)])


def like(shape, dtype):
    return jax.ShapeDtypeStruct(shape, dtype)


def params(limit=VMEM_BYTES):
    return pltpu.CompilerParams(vmem_limit_bytes=limit)


ANYWHERE = pl.BlockSpec(memory_space=pl.ANY)
INSIDE = pl.BlockSpec(memory_space=pltpu.VMEM)
OUTSIDE = pl.BlockSpec(memory_space=pltpu.HBM)
LAST = []


def ordered(kernel, ins, in_specs, aliases=(), **options):
    before = tuple(LAST)

    def body(*refs):
        kernel(*refs[len(before) :])

    ins = [pltpu.with_memory_space_constraint(a, pltpu.HBM) if s is OUTSIDE else a for a, s in zip(ins, in_specs)]
    outs = pl.pallas_call(
        body,
        in_specs=[ANYWHERE] * len(before) + in_specs,
        input_output_aliases={len(before) + at: out for at, out in aliases},
        **options,
    )(*before, *ins)
    LAST[:] = [min(outs, key=lambda out: out.size)]
    return outs


def call(kernel, name, ins, outs, estimate, scratch=(), outside=0, aliases=()):
    return ordered(
        kernel,
        ins,
        [OUTSIDE] * outside + [INSIDE] * (len(ins) - outside),
        aliases,
        out_specs=[INSIDE] * len(outs),
        out_shape=list(outs),
        scratch_shapes=list(scratch),
        compiler_params=params(),
        cost_estimate=beside(name),
        name=name,
    )


def choose_kernel(sel_from, seg_from, chosen_ref, bias_ref, sel_ref, seg_ref, sems):
    copies = [
        pltpu.make_async_copy(sel_from, sel_ref, sems.at[0]),
        pltpu.make_async_copy(seg_from, seg_ref, sems.at[1]),
    ]
    for copy in copies:
        copy.start()
    for copy in copies:
        copy.wait()
    seqs, keep, length = chosen_ref.shape
    square = (keep, keep)
    diagonal = lax.broadcasted_iota(jnp.int32, square, 0) == lax.broadcasted_iota(jnp.int32, square, 1)
    places = lax.broadcasted_iota(jnp.int32, (keep, length), 1)
    for seq in range(seqs):
        row = sel_ref[seq : seq + 1, :].astype(F32)
        column = jnp.sum(jnp.where(diagonal, row, 0.0), axis=1, keepdims=True)
        chosen = jnp.where(column.astype(jnp.int32) == places, 1.0, 0.0).astype(BF16)
        chosen_ref[seq] = chosen
        documents = jnp.broadcast_to(seg_ref[seq : seq + 1, :].astype(F32), (8, length)).astype(BF16)
        of_column = dot_nt(chosen, documents)[:, :1]
        of_row = jnp.sum(jnp.where(diagonal, of_column, 0.0), axis=0, keepdims=True)
        allowed = (row >= column) & (of_column == of_row)
        bias_ref[seq] = jnp.where(allowed, 0.0, -1e30).astype(BF16)


def choose(selected, segments):
    seqs, keep = selected.shape
    length = segments.shape[1]
    return ordered(
        choose_kernel,
        (selected, segments),
        [OUTSIDE] * 2,
        out_specs=[INSIDE] * 2,
        out_shape=[like((seqs, keep, length), BF16), like((seqs, keep, keep), BF16)],
        scratch_shapes=[
            pltpu.VMEM(selected.shape, selected.dtype),
            pltpu.VMEM(segments.shape, segments.dtype),
            pltpu.SemaphoreType.DMA((2,)),
        ],
        compiler_params=params(),
        cost_estimate=beside("choose"),
        name="choose_rows",
    )


def pick_kernel(rows_ref, chosen_ref, picked_ref, buffer, sems):
    seqs, keep, _ = chosen_ref.shape
    copies = [pltpu.make_async_copy(rows_ref.at[seq], buffer.at[seq], sems.at[seq]) for seq in range(seqs)]
    for copy in copies:
        copy.start()
    for seq, copy in enumerate(copies):
        copy.wait()
        picked_ref[seq * keep : (seq + 1) * keep, :] = dot(chosen_ref[seq], buffer[seq]).astype(BF16)


def pick_rows(rows, chosen):
    seqs, _, width = rows.shape
    return ordered(
        pick_kernel,
        (rows, chosen),
        [OUTSIDE, INSIDE],
        out_specs=[INSIDE],
        out_shape=[like((seqs * chosen.shape[1], width), BF16)],
        scratch_shapes=[pltpu.VMEM(rows.shape, BF16), pltpu.SemaphoreType.DMA((seqs,))],
        compiler_params=params(STREAM_BYTES),
        cost_estimate=beside("pick_rows"),
        name="pick_rows",
    )[0]


def place_kernel(seqs, sel_ref, new_ref, base_ref, *refs):
    out_ref, done_ref, buffer, in_sems, out_sems = refs[-5:]
    done_ref[...] = jnp.zeros_like(done_ref)
    length = base_ref.shape[1]
    keep = sel_ref.shape[1]
    chunks = [(number, seq, part) for number, seq in enumerate(seqs) for part in tiles(length, length // 2)]
    copies = [
        pltpu.make_async_copy(base_ref.at[seq, part, :], buffer.at[number, part, :], in_sems.at[at])
        for at, (number, seq, part) in enumerate(chunks)
    ]
    for copy in copies:
        copy.start()
    results = []
    for at, (number, seq, part) in enumerate(chunks):
        places = lax.broadcasted_iota(jnp.int32, (part.stop - part.start, keep), 0) + part.start
        hits = jnp.where(places == sel_ref[seq : seq + 1, :], 1.0, 0.0)
        placed = dot(hits.astype(BF16), new_ref[seq * keep : (seq + 1) * keep, :])
        hit = jnp.max(hits, axis=1, keepdims=True) > 0.0
        copies[at].wait()
        buffer[number, part, :] = jnp.where(hit, placed, buffer[number, part, :].astype(F32)).astype(BF16)
        back = pltpu.make_async_copy(buffer.at[number, part, :], out_ref.at[seq, part, :], out_sems.at[at])
        back.start()
        results.append(back)
    for back in results:
        back.wait()


def place_rows(seqs, selected, new_rows, base, placed=None):
    _, length, width = base.shape
    earlier = () if placed is None else (placed,)
    return ordered(
        functools.partial(place_kernel, tuple(seqs)),
        (selected, new_rows, base, *earlier),
        [INSIDE, INSIDE, OUTSIDE] + [OUTSIDE] * len(earlier),
        aliases=[(3, 0)] if earlier else [],
        out_specs=[OUTSIDE, INSIDE],
        out_shape=[pltpu.HBM(base.shape, BF16), like((8, 128), F32)],
        scratch_shapes=[pltpu.VMEM((len(seqs), length, width), BF16)]
        + [pltpu.SemaphoreType.DMA((2 * len(seqs),))] * 2,
        compiler_params=params(STREAM_BYTES),
        cost_estimate=beside("place_rows"),
        name="place_rows",
    )[0]


class Weight:
    def __init__(self, start, rows, columns, lanes, split=None):
        self.start, self.rows, self.columns, self.lanes, self.split = start, rows, columns, lanes, split
        self.parts = 1 if split is None else 2
        self.half = columns * lanes
        self.shape = (16 * rows, 2 * self.half)

    def slots(self):
        return [(self.start + c * self.rows, c * self.lanes) for c in range(self.columns)]


def aligned(value, size, multiple):
    return pl.ds(pl.multiple_of(value, multiple), size)


def pack_kernel(weights, *refs):
    _, chip, core = own_place()
    *ins, out_ref, sem = refs
    for own, weight in zip(ins, weights):
        for start, lane in weight.slots():
            pltpu.make_async_copy(
                own.at[
                    aligned(chip * weight.rows, weight.rows, 16), aligned(core * weight.half + lane, weight.lanes, 128)
                ],
                out_ref.at[start : start + weight.rows, :],
                sem,
            ).start()
    for extra in ins[len(weights) :]:
        pltpu.make_async_copy(extra, out_ref.at[out_ref.shape[0] - extra.shape[0] :, :], sem).start()
    pltpu.make_async_copy(out_ref, out_ref, sem).wait()


def pack(owns, weights, extra=()):
    rows = sum(w.rows * w.columns for w in weights) + sum(e.shape[0] for e in extra)
    return call(
        functools.partial(pack_kernel, weights),
        "pack_blocks",
        (*owns, *extra),
        [like((rows, weights[0].lanes), BF16)],
        0.5,
        scratch=[pltpu.SemaphoreType.DMA],
        outside=len(owns) + len(extra),
    )[0]


def join_own_kernel(own_ref, second_ref, out_ref):
    out_ref[0] = own_ref[...]
    out_ref[1] = second_ref[...]


def join_own(own, second):
    return call(join_own_kernel, "join_own", (own, second), [like((2, *own.shape), BF16)], 0.2)[0]


def join_shards_kernel(pair_ref, second_ref, *outs):
    start = 0
    for out in outs:
        rows = slice(start, start + out.shape[1])
        start = rows.stop
        out[0] = pair_ref[0, rows, :]
        out[1] = second_ref[rows, :]
        out[2] = pair_ref[1, rows, :]


def join_shards(pair, second, cuts):
    _, rows, lanes = pair.shape
    edges = [0, *cuts, rows]
    outs = [like((3, high - low, lanes), BF16) for low, high in zip(edges, edges[1:])]
    return call(join_shards_kernel, "join_shards", (pair, second), outs, 0.3)


def join_chips_kernel(first_ref, first_got, last_ref, last_got, first_out, last_out, both_out):
    cut = first_ref.shape[1]
    for at, (first, last) in enumerate(((first_ref, last_ref), (first_got, last_got))):
        first_out[at] = first[...]
        last_out[at] = last[...]
        both_out[at, :, :cut, :] = first[...]
        both_out[at, :, cut:, :] = last[...]


def join_chips(first, first_got, last, last_got):
    count, cut, lanes = first.shape
    rows = last.shape[1]
    shapes = [(2, count, cut, lanes), (2, count, rows, lanes), (2, count, cut + rows, lanes)]
    return call(
        join_chips_kernel, "join_chips", (first, first_got, last, last_got), [like(s, BF16) for s in shapes], 0.5
    )


def vectors_kernel(own_ref, others_ref, out_ref):
    shard, _, _ = own_place()
    lanes = out_ref.shape[1] // 4
    pieces = [own_ref[...].astype(F32)] + [others_ref[other].astype(F32) for other in range(3)]
    for place in range(4):
        value = pieces[3]
        for other in range(3):
            value = jnp.where((shard ^ place) == other, pieces[other], value)
        out_ref[:, place * lanes : (place + 1) * lanes] = value[:8, :lanes]


def whole_vectors(own, others, width):
    return call(vectors_kernel, "vectors", (own, others), [like((8, width), F32)], 0.2)[0]


def join_rows_kernel(*refs):
    *ins, out = refs
    start = 0
    for ref in ins:
        rows = ref.shape[-2]
        out[..., start : start + rows, :] = ref[...]
        start += rows


def join_rows(*arrays):
    shape = list(arrays[0].shape)
    shape[-2] = sum(a.shape[-2] for a in arrays)
    return call(join_rows_kernel, "join_rows", arrays, [like(shape, BF16)], 0.3)[0]


def join_kernel(*refs):
    *ins, out = refs
    for at, ref in enumerate(ins):
        out[at] = ref[...]


def join(*arrays):
    return call(join_kernel, "join", arrays, [like((len(arrays), *arrays[0].shape), BF16)], 0.2)[0]


def assemble_kernel(weights, layout, *refs):
    shard, chip, core = own_place()
    count = len(layout)
    owns, refs = refs[: len(weights)], refs[len(weights) :]
    *refs, sems = refs
    pieces, outs = (refs[:count], refs[count : 2 * count]), list(refs[2 * count :])
    for number, (weight, own) in enumerate(zip(weights, owns)):
        shard_rows = own.shape[0]
        sem = sems.at[number]
        targets = [outs.pop(0) for _ in range(weight.parts)]

        def fill(place_of):
            copies = []
            if weight.split == "columns":
                for half in range(2):
                    out, row, _ = place_of(0, half)
                    lane = aligned((core ^ half) * weight.half, weight.half, 128)
                    copies.append(pltpu.make_async_copy(own.at[:, lane], out.at[row, :], sem.at[half]))
            else:
                out, row, _ = place_of(0, 0)
                copies.append(pltpu.make_async_copy(own, out.at[row, :], sem.at[0]))
            for copy in copies:
                copy.start()
            for half in range(2):
                for number, ranges in enumerate(layout):
                    ref = pieces[half][number]
                    for start, lane in weight.slots():
                        for low, high, chips in ranges:
                            lo, hi = max(start, low), min(start + weight.rows, high)
                            if lo >= hi:
                                continue
                            for at, offset in enumerate(chips):
                                for other in range(3):
                                    inner = (chip ^ offset) * weight.rows + (lo - start)
                                    out, row, lanes = place_of(other + 1, half, inner, hi - lo, lane, weight.lanes)
                                    out[row, lanes] = ref[at, other, lo:hi, :]
            for copy in copies:
                copy.wait()

        if weight.split == "columns":

            def place_of(other, half, inner=0, rows=shard_rows, lane=0, lanes=weight.half):
                return targets[half], aligned((shard ^ other) * shard_rows + inner, rows, 16), slice(lane, lane + lanes)

            fill(place_of)
        elif weight.split == "rows":
            for near in range(2):

                def place_of(other, half, inner=0, rows=shard_rows, lane=0, lanes=0):
                    row = ((shard ^ other) & 1) * shard_rows + inner
                    at = aligned((core ^ half) * weight.half + lane, lanes, 128) if lanes else slice(None)
                    return targets[near ^ (other >> 1)], aligned(row, rows, 16), at

                pl.when(((shard >> 1) ^ core) == near)(functools.partial(fill, place_of))
        else:

            def place_of(other, half, inner=0, rows=shard_rows, lane=0, lanes=0):
                at = aligned((core ^ half) * weight.half + lane, lanes, 128) if lanes else slice(None)
                return targets[0], aligned((shard ^ other) * shard_rows + inner, rows, 16), at

            fill(place_of)


def assemble(owns, weights, layout, pieces):
    outs = []
    for weight in weights:
        rows, columns = weight.shape
        if weight.split == "columns":
            outs += [like((rows, columns // 2), BF16)] * 2
        elif weight.split == "rows":
            outs += [like((rows // 2, columns), BF16)] * 2
        else:
            outs.append(like((rows, columns), BF16))
    return call(
        functools.partial(assemble_kernel, weights, layout),
        "assemble_weights",
        (*owns, *pieces),
        outs,
        0.3 * sum(w.columns * w.rows for w in weights) / 48,
        scratch=[pltpu.SemaphoreType.DMA((len(weights), 2))],
    )


def write_blocks(grad_ref, keep_ref, send_ref, start, rows):
    shard, chip, core = own_place()
    lanes = keep_ref.shape[-1]
    for x_bit in range(2):
        for y_bit in range(2):
            for place in range(4):
                row = (shard ^ swap_bits(place)) * (4 * rows) + (chip ^ (2 * y_bit + x_bit)) * rows
                for half, out in ((0, keep_ref), (1, send_ref)):
                    out[x_bit, y_bit, place, start : start + rows, :] = grad_ref[
                        aligned(row, rows, 16), aligned((core ^ half) * lanes, lanes, 128)
                    ].astype(BF16)


def tiles(size, step=TILE):
    return [slice(i, i + step) for i in range(0, size, step)]


def inverse_rms(values):
    return lax.rsqrt(jnp.mean(values * values, axis=-1, keepdims=True) + EPSILON)


def project_kernel(picked_ref, vec_ref, wq, wk, wv, normed_ref, q_ref, k_ref, v_ref):
    for at in tiles(picked_ref.shape[0]):
        values = picked_ref[at, :].astype(F32)
        normed_ref[at, :] = (values * inverse_rms(values) * vec_ref[1:2, :]).astype(BF16)
    q_ref[...] = dot(normed_ref[...], wq[...]).astype(BF16) * 0.125
    k_ref[...] = dot(normed_ref[...], wk[...]).astype(BF16)
    v_ref[...] = dot(normed_ref[...], wv[...]).astype(BF16)


def project(picked, vectors, weights):
    flat = like(picked.shape, BF16)
    return call(project_kernel, "project", (picked, vectors, *weights), [flat] * 4, 4.5)


def low_half_lanes(rows):
    return lax.broadcasted_iota(jnp.int32, (rows, PAIR), 1) < HEAD_DIM


def attend_kernel(bias_ref, q_ref, k_ref, v_ref, probs_ref, att_ref):
    seqs, keep, _ = bias_ref.shape
    low_half = low_half_lanes(keep)

    def sequence(seq, carry):
        bias = bias_ref[seq].astype(F32)
        rows = aligned(seq * keep, keep, keep)
        for pair in range(HEADS // 2):
            lanes = slice(pair * PAIR, (pair + 1) * PAIR)
            queries, keys, values = q_ref[rows, lanes], k_ref[rows, lanes], v_ref[rows, lanes]
            results = []
            for half in range(2):
                mine = low_half if half == 0 else ~low_half
                scores = dot_nt(jnp.where(mine, keys, 0), queries) + bias
                exponent = jnp.exp(scores - jnp.max(scores, axis=0, keepdims=True))
                probs = (exponent * (1.0 / jnp.sum(exponent, axis=0, keepdims=True))).astype(BF16)
                probs_ref[seq, 2 * pair + half] = probs
                results.append(dot_tn(probs, values))
            att_ref[rows, lanes] = jnp.where(low_half, results[0], results[1]).astype(BF16)
        return carry

    lax.fori_loop(0, seqs, sequence, 0)


def attend(bias, queries, keys, values):
    seqs, keep, _ = bias.shape
    return call(
        attend_kernel,
        "attend",
        (bias, queries, keys, values),
        [like((seqs, HEADS, keep, keep), BF16), like(queries.shape, BF16)],
        6.5,
    )


def out_kernel(att_ref, wo_ref, picked_ref, gbr_ref, vec_ref, attn_ref, nm_ref, gmlp_ref, gating_ref):
    attn_ref[...] = dot(att_ref[...], wo_ref[...])
    for at in tiles(picked_ref.shape[0]):
        values = picked_ref[at, :].astype(F32)
        middle = values + attn_ref[at, :]
        nm_ref[at, :] = (middle * inverse_rms(middle) * vec_ref[2:3, :]).astype(BF16)
        logit = jnp.sum(values * vec_ref[0:1, :], axis=-1, keepdims=True)
        gating = 1.0 / (1.0 + jnp.exp(-logit))
        gating_ref[at, :] = gating
        gmlp_ref[at, :] = (gating * gbr_ref[at, :].astype(F32)).astype(BF16)


def project_out(attended, w_out, picked, branch_grad, vectors):
    flat = like(picked.shape, BF16)
    return call(
        out_kernel,
        "project_out",
        (attended, w_out, picked, branch_grad, vectors),
        [like(picked.shape, F32), flat, flat, like((picked.shape[0], 1), F32)],
        2.0,
    )


def gelu_parts(values):
    cdf = 0.5 * (1.0 + lax.erf(values * 0.7071067811865476))
    return values * cdf, cdf + values * (jnp.exp(-0.5 * values * values) * 0.3989422804014327)


def up_kernel(nm_ref, gmlp_ref, wu_ref, act_ref, slope_ref, grad_ref):
    tokens = nm_ref.shape[0]
    for columns in tiles(wu_ref.shape[1], wu_ref.shape[1] // 2):
        for at in tiles(tokens, 128):
            activated, slope = gelu_parts(dot(nm_ref[at, :], wu_ref[:, columns]))
            act_ref[at, columns] = activated.astype(BF16)
            slope_ref[at, columns] = slope.astype(BF16)
        grad_ref[columns, :] = dot_tn(act_ref[:, columns], gmlp_ref[...]).astype(BF16)


def project_up(normed, grad_mlp, w_up):
    tokens, width = normed.shape
    units = w_up.shape[1]
    wide = like((tokens, units), BF16)
    return call(
        up_kernel,
        "project_up",
        (normed, grad_mlp, w_up),
        [wide, wide, like((units, width), BF16)],
        6.0,
    )


def down_blocks_kernel(near_ref, far_ref, keep_ref, send_ref):
    shard, chip, core = own_place()
    rows, lanes = keep_ref.shape[-2:]
    shard_rows = 4 * rows

    def fill(near):
        for place in range(4):
            other = swap_bits(place)
            ref = (near_ref, far_ref)[near ^ (other >> 1)]
            for x_bit in range(2):
                for y_bit in range(2):
                    row = ((shard ^ other) & 1) * shard_rows + (chip ^ (2 * y_bit + x_bit)) * rows
                    for half, out in ((0, keep_ref), (1, send_ref)):
                        out[x_bit, y_bit, place] = ref[
                            aligned(row, rows, 16), aligned((core ^ half) * lanes, lanes, 128)
                        ]

    for near in range(2):
        pl.when(((shard >> 1) ^ core) == near)(functools.partial(fill, near))


def down_blocks(near, far):
    units, width = near.shape
    blocks = like((2, 2, 4, units // 8, width // 2), BF16)
    return call(down_blocks_kernel, "down_blocks", (near, far), [blocks, blocks], 0.7)


def norm_back(grad_normed, values, inverse, gain):
    scaled = grad_normed * gain
    grad_gain = jnp.sum(grad_normed * values * inverse, axis=0, keepdims=True)
    grad_values = inverse * scaled - values * (inverse * inverse * inverse) * jnp.mean(
        scaled * values, axis=-1, keepdims=True
    )
    return grad_values, grad_gain


def down_kernel(weight, act_ref, slope_ref, nm_ref, gmlp_ref, wu_ref, wd_ref, *refs):
    *starts, mlp_ref, gnm_ref, out_ref, grad_ref = refs
    shard, chip, core = own_place()
    block = wd_ref.shape[0] // 2
    rows, lanes = weight.rows, weight.lanes

    for step, at in enumerate(tiles(wd_ref.shape[0], block)):
        down = wd_ref[at, :]
        mlp = dot(act_ref[:, at], down)
        grad_before = (dot_nt(gmlp_ref[...], down) * slope_ref[:, at].astype(F32)).astype(BF16)
        grad_ref[...] = dot_tn(nm_ref[...], grad_before)
        grad_nm = dot_nt(grad_before, wu_ref[:, at])
        if step == 1:
            mlp_ref[...] += mlp
            gnm_ref[...] += grad_nm
        elif starts:
            mlp_ref[...] = starts[0][...] + mlp
            gnm_ref[...] = starts[1][...] + grad_nm
        else:
            mlp_ref[...] = mlp
            gnm_ref[...] = grad_nm
        for x_bit in range(2):
            for y_bit in range(2):
                for place in range(4):
                    row = (shard ^ swap_bits(place)) * (4 * rows) + (chip ^ (2 * y_bit + x_bit)) * rows
                    for part in range(block // lanes):
                        start = (step * (block // lanes) + part) * rows
                        out_ref[x_bit, y_bit, place, start : start + rows, :] = grad_ref[
                            aligned(row, rows, 16), part * lanes : (part + 1) * lanes
                        ].astype(BF16)


def down(weight, activated, slope, normed, grad_mlp, w_up, w_down, starts=()):
    tokens, width = normed.shape
    total = like((tokens, width), F32)
    return call(
        functools.partial(down_kernel, weight),
        "down_and_back",
        (activated, slope, normed, grad_mlp, w_up, w_down, *starts),
        [total, total, like((2, 2, 4, weight.rows * weight.columns, weight.lanes), BF16)],
        8.5,
        scratch=[pltpu.VMEM((width, w_up.shape[1] // 2), F32)],
    )


def branch_kernel(
    mlp_ref, gnm_ref, attn_ref, picked_ref, gbr_ref, gating_ref, vec_ref, new_ref, gattn_ref, gmid_ref, glogit_ref, sum_ref
):
    total = jnp.zeros((1, vec_ref.shape[1]), F32)
    for at in tiles(picked_ref.shape[0]):
        attention = attn_ref[at, :]
        values = picked_ref[at, :].astype(F32)
        gating = gating_ref[at, :]
        branch_grad = gbr_ref[at, :].astype(F32)
        delta = attention + mlp_ref[at, :]
        new_ref[at, :] = (values + gating * delta).astype(BF16)
        grad_gating = jnp.sum(branch_grad * delta, axis=-1, keepdims=True)
        glogit_ref[at, :] = grad_gating * gating * (1.0 - gating)
        middle = values + attention
        grad_middle, grad_gain = norm_back(gnm_ref[at, :], middle, inverse_rms(middle), vec_ref[2:3, :])
        gmid_ref[at, :] = grad_middle
        gattn_ref[at, :] = (gating * branch_grad + grad_middle).astype(BF16)
        total = total + grad_gain
    sum_ref[...] = jnp.broadcast_to(total, sum_ref.shape)


def branch(mlp, grad_nm, attn_out, picked, branch_grad, gating, vectors):
    tokens, width = picked.shape
    return call(
        branch_kernel,
        "branch_and_norm_back",
        (mlp, grad_nm, attn_out, picked, branch_grad, gating, vectors),
        [
            like((tokens, width), BF16),
            like((tokens, width), BF16),
            like((tokens, width), F32),
            like((tokens, 1), F32),
            like((8, width), F32),
        ],
        2.0,
    )


def out_back_kernel(weight, gattn_ref, att_ref, wo_ref, gatt_ref, keep_ref, send_ref, grad_ref):
    grad_ref[...] = dot_tn(att_ref[...], gattn_ref[...])
    gatt_ref[...] = dot_nt(gattn_ref[...], wo_ref[...]).astype(BF16)
    write_blocks(grad_ref, keep_ref, send_ref, 0, weight.rows)


def out_back(weight, grad_attn, attended, w_out):
    blocks = like((2, 2, 4, weight.rows, weight.lanes), BF16)
    return call(
        functools.partial(out_back_kernel, weight),
        "project_out_back",
        (grad_attn, attended, w_out),
        [like(grad_attn.shape, BF16), blocks, blocks],
        2.5,
        scratch=[pltpu.VMEM(weight.shape, F32)],
    )


def attend_back_kernel(seq, gatt_ref, q_ref, k_ref, v_ref, probs_ref, gq_ref, gk_ref, gv_ref):
    keep = probs_ref.shape[2]
    low_half = low_half_lanes(keep)
    rows = slice(seq * keep, (seq + 1) * keep)
    for pair in range(HEADS // 2):
        lanes = slice(pair * PAIR, (pair + 1) * PAIR)
        queries, keys, values = q_ref[rows, lanes], k_ref[rows, lanes], v_ref[rows, lanes]
        grad_att = gatt_ref[rows, lanes]
        found = []
        for half in range(2):
            mine = low_half if half == 0 else ~low_half
            probs = probs_ref[seq, 2 * pair + half]
            wide = probs.astype(F32)
            weighted = wide * dot_nt(jnp.where(mine, values, 0), grad_att)
            scores = (weighted - wide * jnp.sum(weighted, axis=0, keepdims=True)).astype(BF16)
            found.append((dot_tn(scores, keys) * 0.125, dot(scores, queries), dot(probs, grad_att)))
        for out, first, second in zip((gq_ref, gk_ref, gv_ref), *found):
            out[:, lanes] = jnp.where(low_half, first, second).astype(BF16)


def attend_back(seq, grad_attended, queries, keys, values, probs):
    rows = like((probs.shape[2], queries.shape[1]), BF16)
    return call(
        functools.partial(attend_back_kernel, seq),
        "attend_back",
        (grad_attended, queries, keys, values, probs),
        [rows] * 3,
        4.0,
    )


def project_grads_kernel(weights, normed_ref, *refs):
    *grads, keep_ref, send_ref, grad_ref = refs
    for i, weight in enumerate(weights):
        grad_ref[...] = dot_tn(normed_ref[...], rows_of(grads, i))
        write_blocks(grad_ref, keep_ref, send_ref, weight.start, weight.rows)


def rows_of(grads, i):
    return jnp.concatenate([ref[...] for ref in grads[i::3]], axis=0)


def project_grads(weights, normed, grads):
    blocks = like((2, 2, 4, sum(w.rows for w in weights), weights[0].lanes), BF16)
    return call(
        functools.partial(project_grads_kernel, weights),
        "project_gradients",
        (normed, *grads),
        [blocks, blocks],
        4.0,
        scratch=[pltpu.VMEM(weights[0].shape, F32)],
    )


def project_back_kernel(count, *refs):
    grads, refs = refs[:count], refs[count:]
    wq, wk, wv, picked_ref, gmid_ref, gbr_ref, glogit_ref, vec_ref, middle_ref, new_ref, sum_ref, gn_ref = refs
    gn_ref[...] = sum(dot_nt(rows_of(grads, i), w[...]) for i, w in enumerate((wq, wk, wv)))
    router = jnp.zeros((1, vec_ref.shape[1]), F32)
    total = router
    for at in tiles(picked_ref.shape[0]):
        values = picked_ref[at, :].astype(F32)
        grad_picked, grad_gain = norm_back(gn_ref[at, :], values, inverse_rms(values), vec_ref[1:2, :])
        grad_logit = glogit_ref[at, :]
        new_ref[at, :] = (
            gbr_ref[at, :].astype(F32) + grad_logit * vec_ref[0:1, :] + (grad_picked + gmid_ref[at, :])
        ).astype(BF16)
        router = router + jnp.sum(grad_logit * values, axis=0, keepdims=True)
        total = total + grad_gain
    rows = jnp.concatenate([router, total, middle_ref[0:1, :], jnp.zeros((5, router.shape[1]), F32)], axis=0)
    lanes = sum_ref.shape[1]
    sum_ref[...] = jnp.concatenate([rows[:, :lanes], rows[:, lanes:]], axis=0).astype(BF16)


def project_back(grads, weights, picked, grad_middle, branch_grad, grad_logit, vectors, gain_sums):
    tokens, width = picked.shape
    return call(
        functools.partial(project_back_kernel, len(grads)),
        "project_back",
        (*grads, *weights, picked, grad_middle, branch_grad, grad_logit, vectors, gain_sums),
        [like((tokens, width), BF16), like((VECTOR_ROWS, width // 2), BF16)],
        5.0,
        scratch=[pltpu.VMEM((tokens, width), F32)],
    )


def total_of(left, right):
    return (left.astype(F32) + right.astype(F32)).astype(BF16)


def add_first_kernel(cut, parts, extra, *refs):
    *refs, a_away, a_keep, b_away, b_keep = refs
    start = 0

    def put(x_bit, y_bit, at, begin, value):
        low, high = begin, begin + value.shape[-2]
        if low < cut:
            out = a_away if x_bit else a_keep
            out[y_bit, at, low : min(high, cut), :] = value[: min(high, cut) - low]
        if high > cut:
            out = b_away if y_bit else b_keep
            out[x_bit, at, max(low, cut) - cut : high - cut, :] = value[max(low, cut) - low :]

    for number in range(parts):
        keep, got = refs[2 * number], refs[2 * number + 1]
        for x_bit in range(2):
            for y_bit in range(2):
                for at in range(keep.shape[2]):
                    put(x_bit, y_bit, at, start, total_of(keep[x_bit, y_bit, at], got[x_bit, y_bit, at]))
        start += keep.shape[3]
    if extra:
        value = total_of(refs[-2][...], refs[-1][...])
        for x_bit in range(2):
            for y_bit in range(2):
                for at in range(4):
                    put(x_bit, y_bit, at, start, value)


def add_first(pairs, cut, extra=()):
    lanes = pairs[0][0].shape[-1]
    rows = sum(keep.shape[3] for keep, _ in pairs) + (extra[0].shape[0] if extra else 0)
    out = lambda n: like((2, 4, n, lanes), BF16)
    return call(
        functools.partial(add_first_kernel, cut, len(pairs), bool(extra)),
        "add_first",
        [array for pair in pairs for array in pair] + list(extra),
        [out(cut), out(cut), out(rows - cut), out(rows - cut)],
        0.7,
    )


def add_second_kernel(a_ref, a_got, b_ref, b_got, a_away, a_keep, b_away, b_keep):
    for ref, got, away, keep in ((a_ref, a_got, a_away, a_keep), (b_ref, b_got, b_away, b_keep)):
        for at in range(ref.shape[1]):
            keep[at] = total_of(ref[0, at], got[0, at])
            away[at] = total_of(ref[1, at], got[1, at])


def add_second(a_keep, a_got, b_keep, b_got):
    a_like, b_like = [like(array.shape[1:], BF16) for array in (a_keep, b_keep)]
    return call(
        add_second_kernel, "add_second", (a_keep, a_got, b_keep, b_got), [a_like, a_like, b_like, b_like], 0.5
    )


def add_third_kernel(a_ref, a_got, b_ref, b_got, away, keep):
    cut = a_ref.shape[1]
    for out, first in ((away, 2), (keep, 0)):
        for at in range(2):
            out[at, :cut, :] = total_of(a_ref[first + at], a_got[first + at])
            out[at, cut:, :] = total_of(b_ref[first + at], b_got[first + at])


def add_third(a_keep, a_got, b_keep, b_got):
    half = like((2, a_keep.shape[1] + b_keep.shape[1], a_keep.shape[2]), BF16)
    return call(add_third_kernel, "add_third", (a_keep, a_got, b_keep, b_got), [half, half], 0.4)


def add_fourth_kernel(keep_ref, got_ref, away, keep):
    away[...] = total_of(keep_ref[1], got_ref[1])
    keep[...] = total_of(keep_ref[0], got_ref[0])


def add_fourth(keep, got):
    half = like(keep.shape[1:], BF16)
    return call(add_fourth_kernel, "add_fourth", (keep, got), [half, half], 0.3)


def add_last_kernel(keep_ref, got_ref, out):
    out[...] = total_of(keep_ref[...], got_ref[...])


def add_last(keep, got):
    return call(add_last_kernel, "add_last", (keep, got), [like(keep.shape, BF16)], 0.3)[0]


def unpack_kernel(weights, near_ref, far_ref, *outs):
    _, chip, core = own_place()
    for weight, out in zip(weights, outs):
        for half, ref in enumerate((near_ref, far_ref)):
            for offset in range(4):
                at = aligned((chip ^ offset) * weight.rows, weight.rows, 16)
                for start, lane in weight.slots():
                    block = ref[offset, start : start + weight.rows, :]
                    out[at, aligned((core ^ half) * weight.half + lane, weight.lanes, 128)] = block.astype(F32)


def unpack(weights, near, far):
    return call(
        functools.partial(unpack_kernel, weights),
        "unpack_gradients",
        (near, far),
        [like((weight.shape[0] // 4, weight.shape[1]), F32) for weight in weights],
        2.0,
    )


def solution(mesh):
    replicas, shards = mesh.shape["rep"], mesh.shape["fsdp"]
    rep_pairs = lambda bits: [(i, i ^ bits) for i in range(replicas)]
    shard_pairs = lambda bits: [(i, i ^ bits) for i in range(shards)]
    plane = {"c": 1, "x": 2, "y": 4, "d": 6}

    def swap(values, way):
        return lax.ppermute(values, "rep", rep_pairs(plane[way]))

    def swap_shard(values, bits):
        return lax.ppermute(values, "fsdp", shard_pairs(bits))

    def swap_halves(halves, order="xy"):
        first, last = halves[:2]
        return first, swap(first, order[0]), last, swap(last, order[1])

    def swap_sums(sums, order):
        a_away, a_keep, b_away, b_keep = sums
        return a_keep, swap(a_away, order[0]), b_keep, swap(b_away, order[1])

    def over_planes(own):
        bit = 8
        while bit < replicas:
            own = total_of(own, lax.ppermute(own, "rep", rep_pairs(bit)))
            bit *= 2
        return own

    def on_device(
        hidden,
        segments,
        selected,
        w_query,
        w_key,
        w_value,
        w_out,
        w_up,
        w_down,
        w_router,
        gain_attn,
        gain_mlp,
        cotangent,
    ):
        LAST.clear()
        CALLS.clear()
        width = hidden.shape[2]
        seqs = hidden.shape[0]
        lanes = width // 2
        shard = lax.axis_index("fsdp")

        small, tall = w_query.shape[0] // 4, w_down.shape[0] // 4
        wide = w_up.shape[1] // 2 // lanes
        first_weights = [Weight(i * small, small, 1, lanes) for i in range(4)]
        up_at = Weight(0, small, wide, lanes, "columns")
        down_at = Weight(0, tall, 1, lanes, "rows")
        first_rows, second_rows = 4 * small, small * wide
        halved = lambda rows: [
            [(0, rows // 2, (0, 1)), (rows // 2, rows, (0, 2))],
            [(0, rows // 2, (2, 3)), (rows // 2, rows, (1, 3))],
        ]
        vectors = jnp.stack([w_router, gain_attn, gain_mlp])
        padded = jnp.pad(vectors, ((0, VECTOR_ROWS - 3), (0, lanes - vectors.shape[1])))

        first_own = pack((w_query, w_key, w_value, w_out), first_weights)
        first_second = swap_shard(first_own, 2)
        chosen, bias = choose(selected, segments)
        branch_grad = pick_rows(cotangent, chosen)
        first_pair = swap_shard(join_own(first_own, first_second), 1)
        second_own = pack((w_up,), (up_at,), (padded,))
        second_second = swap_shard(second_own, 2)
        picked = pick_rows(hidden, chosen)
        first = swap_halves(join_shards(first_pair, first_second, [first_rows // 2]))
        second_pair = swap_shard(join_own(second_own, second_second), 1)
        third_own = pack((w_down,), (down_at,))
        third_second = swap_shard(third_own, 2)
        *first, first_both = join_chips(*first)
        first = swap_halves(first, "yx")
        first_both_far = swap(first_both, "c")
        *second, others = join_shards(second_pair, second_second, [second_rows // 2, second_rows])
        second = swap_halves(second)
        third_pair = swap_shard(join_own(third_own, third_second), 1)
        vec = whole_vectors(padded, others, width)
        first_other = join_rows(first[1], first[3])
        first_other_far = swap(first_other, "c")
        *second, second_both = join_chips(*second)
        second = swap_halves(second, "yx")
        second_both_far = swap(second_both, "c")
        *qkv, full_out = assemble(
            (w_query, w_key, w_value, w_out),
            first_weights,
            halved(first_rows),
            (first_both, first_other, first_both_far, first_other_far),
        )
        normed, queries, keys, values = project(picked, vec, qkv)
        third = swap_halves(join_shards(third_pair, third_second, [tall // 2]))
        probs, attended = attend(bias, queries, keys, values)
        second_other = join_rows(second[1], second[3])
        second_other_far = swap(second_other, "c")
        *third, third_both = join_chips(*third)
        third = swap_halves(third, "yx")
        third_both_far = swap(third_both, "c")
        attn_out, normed_mlp, grad_mlp, gating = project_out(attended, full_out, picked, branch_grad, vec)
        up_near, up_far = assemble(
            (w_up,), (up_at,), halved(second_rows), (second_both, second_other, second_both_far, second_other_far)
        )
        act_far, slope_far, grad_far = project_up(normed_mlp, grad_mlp, up_far)
        act_near, slope_near, grad_near = project_up(normed_mlp, grad_mlp, up_near)

        down_keep, down_send = down_blocks(grad_near, grad_far)
        down_got = swap(down_send, "c")
        third_other = join_rows(third[1], third[3])
        third_other_far = swap(third_other, "c")
        down_near, down_far = assemble(
            (w_down,), (down_at,), halved(tall), (third_both, third_other, third_both_far, third_other_far)
        )
        mlp, grad_nm, up_send = down(up_at, act_far, slope_far, normed_mlp, grad_mlp, up_far, down_far)
        up_got = swap(up_send, "c")
        d_sums = swap_sums(add_first([(down_keep, down_got)], tall // 2), "xy")
        mlp, grad_nm, up_keep = down(
            up_at, act_near, slope_near, normed_mlp, grad_mlp, up_near, down_near, (mlp, grad_nm)
        )
        new_rows, grad_attn, grad_middle, grad_logit, gain_sums = branch(
            mlp, grad_nm, attn_out, picked, branch_grad, gating, vec
        )
        grad_attended, out_keep, out_send = out_back(first_weights[3], grad_attn, attended, full_out)
        out_got = swap(out_send, "c")
        d_sums = swap_sums(add_second(*d_sums), "yx")
        grads = []
        for seq in range(seqs):
            grads += attend_back(seq, grad_attended, queries, keys, values, probs)
            if seq == 0:
                u_sums = swap_sums(add_first([(up_keep, up_got), (out_keep, out_got)], 112), "xy")
            if seq == 1:
                d_away, d_keep = add_third(*d_sums)
                d_got = swap_shard(d_away, 1)
        first_keep, first_send = project_grads(first_weights[:3], normed, grads)
        first_got = swap(first_send, "c")
        d_away, d_keep = add_fourth(d_keep, d_got)
        d_got = swap_shard(d_away, 2)
        grad_rows, sums = project_back(
            grads, qkv, picked, grad_middle, branch_grad, grad_logit, vec, gain_sums
        )
        u_sums = swap_sums(add_second(*u_sums), "yx")
        d_own = over_planes(add_last(d_keep, d_got))
        f_sums = swap_sums(add_first([(first_keep, first_got)], 80, (sums, swap(sums, "c"))), "xy")
        out_hidden = place_rows(range(seqs), selected, new_rows, hidden)
        u_away, u_keep = add_third(*u_sums)
        u_got = swap_shard(u_away, 1)
        d_got = swap(d_own, "x")
        grad_hidden = place_rows(range(1), selected, grad_rows, cotangent)
        f_sums = swap_sums(add_second(*f_sums), "yx")
        d_pair = join(d_own, d_got)
        d_got = swap(d_pair, "y")
        u_away, u_keep = add_fourth(u_keep, u_got)
        u_got = swap_shard(u_away, 2)
        grad_hidden = place_rows(range(1, seqs), selected, grad_rows, cotangent, grad_hidden)
        f_away, f_keep = add_third(*f_sums)
        f_got = swap_shard(f_away, 1)
        d_near = join(d_pair, d_got).reshape(4, *d_own.shape)
        d_far = swap(d_near, "c")
        u_own = over_planes(add_last(u_keep, u_got))
        u_spread = [u_own] + [swap(u_own, way) for way in "xyd"]
        f_away, f_keep = add_fourth(f_keep, f_got)
        f_got = swap_shard(f_away, 2)
        (grad_down,) = unpack((Weight(0, tall, 1, lanes),), d_near, d_far)
        u_near = join(*u_spread)
        u_far = swap(u_near, "c")
        f_own = over_planes(add_last(f_keep, f_got))
        f_spread = [f_own] + [swap(f_own, way) for way in "xyd"]
        grad_up, grad_out = unpack(
            (Weight(0, small, wide, lanes), Weight(small * wide, small, 1, lanes)), u_near, u_far
        )
        f_near = join(*f_spread)
        grad_qkv = unpack(first_weights[:3], f_near, swap(f_near, "c"))
        sums = f_own[3 * small :].reshape(2, 8, lanes)[:, :3].swapaxes(0, 1).reshape(3, width).astype(F32)
        sums = lax.dynamic_slice(sums, (0, shard * w_router.shape[0]), (3, w_router.shape[0]))
        return (out_hidden, grad_hidden, *grad_qkv, grad_out, grad_up, grad_down, sums[0], sums[1], sums[2])

    placed = (
        P(("rep", "fsdp"), None, None),
        P(("rep", "fsdp"), None),
        P(("rep", "fsdp"), None),
        P("fsdp", None),
        P("fsdp", None),
        P("fsdp", None),
        P("fsdp", None),
        P("fsdp", None),
        P("fsdp", None),
        P("fsdp"),
        P("fsdp"),
        P("fsdp"),
        P(("rep", "fsdp"), None, None),
    )
    return jax.shard_map(
        on_device,
        mesh=mesh,
        in_specs=placed,
        out_specs=(
            P(("rep", "fsdp"), None, None),
            P(("rep", "fsdp"), None, None),
            P("fsdp", None),
            P("fsdp", None),
            P("fsdp", None),
            P("fsdp", None),
            P("fsdp", None),
            P("fsdp", None),
            P("fsdp"),
            P("fsdp"),
            P("fsdp"),
        ),
        check_vma=False,
    )
```

```python
import functools

import jax
import jax.numpy as jnp
from jax import lax
from jax.experimental import pallas as pl
from jax.experimental.pallas import tpu as pltpu
from jax.sharding import PartitionSpec as P

HEADS = 12
HEAD_DIM = 64
PAIR = 2 * HEAD_DIM
EPSILON = 1e-06
F32 = jnp.float32
BF16 = jnp.bfloat16
TILE = 256
LANES = 128
VECTOR_ROWS = 16
VMEM_BYTES = 10 * 1024 * 1024
SMALL_BYTES = 6 * 1024 * 1024
STREAM_BYTES = 28 * 1024 * 1024


def dot(left, right):
    return jnp.dot(left, right, preferred_element_type=F32)


def dot_nt(left, right):
    return lax.dot_general(left, right, (((1,), (1,)), ((), ())), preferred_element_type=F32)


def dot_tn(left, right):
    return lax.dot_general(left, right, (((0,), (0,)), ((), ())), preferred_element_type=F32)


def swap_bits(place):
    return ((place & 1) << 1) | (place >> 1)


def own_place():
    member = lax.axis_index("rep") & 7
    return lax.axis_index("fsdp"), member >> 1, member & 1


def micros(time):
    return pl.CostEstimate(flops=int(time * 1.1e9), bytes_accessed=0, transcendentals=0)


BESIDE = {
    "pack_blocks": (0.1, 0.3, 0.3),
    "choose": (0.3,),
    "pick_rows": (1.0, 3.0),
    "join_own": (0.1, 2.3, 4.3),
    "join_chips": (1.2, 0.1, 0.1),
    "cover": (9.5, 9.5, 11.0, 17.0, 9.5),
    "project": (1.0,),
    "attend": (2.4,),
    "project_out": (0.8,),
    "project_up": (2.0, 2.0),
    "down_and_back": (24.0, 12.0, 2.5, 1.0),
    "attend_back": (2.2, 0.5, 2.3),
    "project_gradients": (0.5,),
    "project_back": (1.0,),
    "place_rows": (5.2, 2.6, 2.6, 0.1),
    "add_last": (0.1, 0.1, 1.0),
    "unpack_gradients": (1.3, 2.0, 0.1),
}
CALLS = {}
LARGE = {"down_and_back", "project_back", "attend"}


def beside(name):
    number = CALLS.get(name, 0)
    CALLS[name] = number + 1
    times = BESIDE.get(name, (0.1,))
    return micros(times[min(number, len(times) - 1)])


def like(shape, dtype):
    return jax.ShapeDtypeStruct(shape, dtype)


def params(limit=VMEM_BYTES):
    return pltpu.CompilerParams(vmem_limit_bytes=limit)


ANYWHERE = pl.BlockSpec(memory_space=pl.ANY)
INSIDE = pl.BlockSpec(memory_space=pltpu.VMEM)
OUTSIDE = pl.BlockSpec(memory_space=pltpu.HBM)
LAST = []


def ordered(kernel, ins, in_specs, aliases=(), **options):
    before = tuple(LAST)

    def body(*refs):
        kernel(*refs[len(before) :])

    ins = [pltpu.with_memory_space_constraint(a, pltpu.HBM) if s is OUTSIDE else a for a, s in zip(ins, in_specs)]
    outs = pl.pallas_call(
        body,
        in_specs=[ANYWHERE] * len(before) + in_specs,
        input_output_aliases={len(before) + at: out for at, out in aliases},
        **options,
    )(*before, *ins)
    LAST[:] = [min(outs, key=lambda out: out.size)]
    return outs


def call(kernel, name, ins, outs, estimate, scratch=(), outside=0, aliases=(), outside_outs=0):
    return ordered(
        kernel,
        ins,
        [OUTSIDE] * outside + [INSIDE] * (len(ins) - outside),
        aliases,
        out_specs=[INSIDE] * (len(outs) - outside_outs) + [OUTSIDE] * outside_outs,
        out_shape=list(outs),
        scratch_shapes=list(scratch),
        compiler_params=params(VMEM_BYTES if name in LARGE else SMALL_BYTES),
        cost_estimate=beside(name),
        name=name,
    )


def choose_kernel(sel_from, seg_from, chosen_ref, bias_ref, sel_ref, seg_ref, sems):
    copies = [
        pltpu.make_async_copy(sel_from, sel_ref, sems.at[0]),
        pltpu.make_async_copy(seg_from, seg_ref, sems.at[1]),
    ]
    for copy in copies:
        copy.start()
    for copy in copies:
        copy.wait()
    seqs, keep, length = chosen_ref.shape
    square = (keep, keep)
    diagonal = lax.broadcasted_iota(jnp.int32, square, 0) == lax.broadcasted_iota(jnp.int32, square, 1)
    places = lax.broadcasted_iota(jnp.int32, (keep, length), 1)
    for seq in range(seqs):
        row = sel_ref[seq : seq + 1, :].astype(F32)
        column = jnp.sum(jnp.where(diagonal, row, 0.0), axis=1, keepdims=True)
        chosen = jnp.where(column.astype(jnp.int32) == places, 1.0, 0.0).astype(BF16)
        chosen_ref[seq] = chosen
        documents = jnp.broadcast_to(seg_ref[seq : seq + 1, :].astype(F32), (8, length)).astype(BF16)
        of_column = dot_nt(chosen, documents)[:, :1]
        of_row = jnp.sum(jnp.where(diagonal, of_column, 0.0), axis=0, keepdims=True)
        allowed = (row >= column) & (of_column == of_row)
        bias_ref[seq] = jnp.where(allowed, 0.0, -1e30).astype(BF16)


def choose(selected, segments):
    seqs, keep = selected.shape
    length = segments.shape[1]
    return ordered(
        choose_kernel,
        (selected, segments),
        [OUTSIDE] * 2,
        out_specs=[INSIDE] * 2,
        out_shape=[like((seqs, keep, length), BF16), like((seqs, keep, keep), BF16)],
        scratch_shapes=[
            pltpu.VMEM(selected.shape, selected.dtype),
            pltpu.VMEM(segments.shape, segments.dtype),
            pltpu.SemaphoreType.DMA((2,)),
        ],
        compiler_params=params(),
        cost_estimate=beside("choose"),
        name="choose_rows",
    )


def pick_kernel(rows_ref, chosen_ref, picked_ref, buffer, sems):
    seqs, keep, _ = chosen_ref.shape
    copies = [pltpu.make_async_copy(rows_ref.at[seq], buffer.at[seq], sems.at[seq]) for seq in range(seqs)]
    for copy in copies:
        copy.start()
    for seq, copy in enumerate(copies):
        copy.wait()
        picked_ref[seq * keep : (seq + 1) * keep, :] = dot(chosen_ref[seq], buffer[seq]).astype(BF16)


def pick_rows(rows, chosen):
    seqs, _, width = rows.shape
    return ordered(
        pick_kernel,
        (rows, chosen),
        [OUTSIDE, INSIDE],
        out_specs=[INSIDE],
        out_shape=[like((seqs * chosen.shape[1], width), BF16)],
        scratch_shapes=[pltpu.VMEM(rows.shape, BF16), pltpu.SemaphoreType.DMA((seqs,))],
        compiler_params=params(STREAM_BYTES),
        cost_estimate=beside("pick_rows"),
        name="pick_rows",
    )[0]


def place_kernel(seqs, sel_ref, new_ref, base_ref, *refs):
    out_ref, done_ref, buffer, wide_ref, in_sems, out_sems = refs[-6:]
    done_ref[...] = jnp.zeros_like(done_ref)
    length, width = base_ref.shape[1:]
    keep = sel_ref.shape[1]
    chunks = [(number, seq, part) for number, seq in enumerate(seqs) for part in tiles(length, length // 2)]
    copies = [
        pltpu.make_async_copy(base_ref.at[seq, part, :], buffer.at[number, part, :], in_sems.at[at])
        for at, (number, seq, part) in enumerate(chunks)
    ]
    for copy in copies:
        copy.start()
    for number, seq in enumerate(seqs):
        wide_ref[number, :, :width] = new_ref[seq * keep : (seq + 1) * keep, :]
        wide_ref[number, :, width:] = jnp.ones((keep, LANES), BF16)
    results = []
    for at, (number, seq, part) in enumerate(chunks):
        places = lax.broadcasted_iota(jnp.int32, (part.stop - part.start, keep), 0) + part.start
        hits = jnp.where(places == sel_ref[seq : seq + 1, :], 1.0, 0.0).astype(BF16)
        copies[at].wait()
        for row in range(0, part.stop - part.start, TILE):
            placed = dot(hits[row : row + TILE, :], wide_ref[number])
            new = placed[:, width:] > 0.0
            rows = slice(part.start + row, part.start + row + TILE)
            for lane in range(0, width, LANES):
                lanes = slice(lane, lane + LANES)
                base = buffer[number, rows, lanes].astype(F32)
                buffer[number, rows, lanes] = jnp.where(new, placed[:, lanes], base).astype(BF16)
        back = pltpu.make_async_copy(buffer.at[number, part, :], out_ref.at[seq, part, :], out_sems.at[at])
        back.start()
        results.append(back)
    for back in results:
        back.wait()


def place_rows(seqs, selected, new_rows, base, placed=None):
    _, length, width = base.shape
    earlier = () if placed is None else (placed,)
    return ordered(
        functools.partial(place_kernel, tuple(seqs)),
        (selected, new_rows, base, *earlier),
        [INSIDE, INSIDE, OUTSIDE] + [OUTSIDE] * len(earlier),
        aliases=[(3, 0)] if earlier else [],
        out_specs=[OUTSIDE, INSIDE],
        out_shape=[pltpu.HBM(base.shape, BF16), like((8, 128), F32)],
        scratch_shapes=[
            pltpu.VMEM((len(seqs), length, width), BF16),
            pltpu.VMEM((len(seqs), selected.shape[1], width + LANES), BF16),
        ]
        + [pltpu.SemaphoreType.DMA((2 * len(seqs),))] * 2,
        compiler_params=params(STREAM_BYTES),
        cost_estimate=beside("place_rows"),
        name="place_rows",
    )[0]


class Weight:
    def __init__(self, start, rows, columns, lanes, split=None, pieces=None):
        self.start, self.rows, self.columns, self.lanes, self.split = start, rows, columns, lanes, split
        self.parts = 1 if split is None else 2
        self.half = columns * lanes
        self.shape = (16 * rows, 2 * self.half)
        self.pieces = pieces or [(at, 0, rows, lane) for at, lane in self.slots()]

    def slots(self):
        return [(self.start + c * self.rows, c * self.lanes) for c in range(self.columns)]


def aligned(value, size, multiple):
    return pl.ds(pl.multiple_of(value, multiple), size)


def pack_kernel(weights, *refs):
    _, chip, core = own_place()
    *ins, out_ref, sem = refs
    for own, weight in zip(ins, weights):
        for start, lane in weight.slots():
            pltpu.make_async_copy(
                own.at[
                    aligned(chip * weight.rows, weight.rows, 16), aligned(core * weight.half + lane, weight.lanes, 128)
                ],
                out_ref.at[start : start + weight.rows, :],
                sem,
            ).start()
    for extra in ins[len(weights) :]:
        pltpu.make_async_copy(extra, out_ref.at[out_ref.shape[0] - extra.shape[0] :, :], sem).start()
    pltpu.make_async_copy(out_ref, out_ref, sem).wait()


def pack(owns, weights, extra=()):
    rows = sum(w.rows * w.columns for w in weights) + sum(e.shape[0] for e in extra)
    return call(
        functools.partial(pack_kernel, weights),
        "pack_blocks",
        (*owns, *extra),
        [like((rows, weights[0].lanes), BF16)],
        0.5,
        scratch=[pltpu.SemaphoreType.DMA],
        outside=len(owns) + len(extra),
    )[0]


def join_own_kernel(own_ref, second_ref, *refs):
    *held, out_ref, out_held = refs if len(refs) > 1 else (*refs, None)
    for ref in held:
        out_held[...] = ref[...]
    out_ref[0] = own_ref[...]
    out_ref[1] = second_ref[...]


def join_own(own, second, held=()):
    outs = [like((2, *own.shape), BF16)] + [like(a.shape, a.dtype) for a in held]
    outs = call(join_own_kernel, "join_own", (own, second, *held), outs, 0.2)
    return outs if held else outs[0]


def join_shards_kernel(count, pair_ref, second_ref, *refs):
    held, outs = refs[:count], refs[count:]
    for ref, out in zip(held, outs[len(outs) - count :]):
        out[...] = ref[...]
    start = 0
    for out in outs[: len(outs) - count]:
        rows = slice(start, start + out.shape[1])
        start = rows.stop
        out[0] = pair_ref[0, rows, :]
        out[1] = second_ref[rows, :]
        out[2] = pair_ref[1, rows, :]


def join_shards(pair, second, cuts, held=()):
    _, rows, lanes = pair.shape
    edges = [0, *cuts, rows]
    outs = [like((3, high - low, lanes), BF16) for low, high in zip(edges, edges[1:])]
    outs += [like(a.shape, a.dtype) for a in held]
    return call(functools.partial(join_shards_kernel, len(held)), "join_shards", (pair, second, *held), outs, 0.3)


def hold_kernel(*refs):
    count = len(refs) // 2
    for ref, out in zip(refs[:count], refs[count:]):
        out[...] = ref[...]


def hold(*arrays):
    return call(hold_kernel, "hold", arrays, [like(a.shape, a.dtype) for a in arrays], 0.2)


def cover_kernel(out_ref):
    out_ref[...] = jnp.zeros_like(out_ref)


def cover():
    call(cover_kernel, "cover", (), [like((8, 128), F32)], 0.1)


def join_chips_kernel(first_ref, first_got, last_ref, last_got, first_out, last_out, both_out):
    cut = first_ref.shape[1]
    for at, (first, last) in enumerate(((first_ref, last_ref), (first_got, last_got))):
        first_out[at] = first[...]
        last_out[at] = last[...]
        both_out[at, :, :cut, :] = first[...]
        both_out[at, :, cut:, :] = last[...]


def join_chips(first, first_got, last, last_got):
    count, cut, lanes = first.shape
    rows = last.shape[1]
    shapes = [(2, count, cut, lanes), (2, count, rows, lanes), (2, count, cut + rows, lanes)]
    return call(
        join_chips_kernel, "join_chips", (first, first_got, last, last_got), [like(s, BF16) for s in shapes], 0.5
    )


def vectors_kernel(own_ref, others_ref, out_ref):
    shard, _, _ = own_place()
    lanes = out_ref.shape[1] // 4
    pieces = []
    for ref in (own_ref, *[others_ref.at[other] for other in range(3)]):
        rows = ref[...].astype(F32)
        pieces.append(jnp.concatenate([rows[:1, :lanes], rows[:1, lanes:], rows[1:2, :lanes]], axis=0))
    out_ref[...] = jnp.zeros_like(out_ref)
    for place in range(4):
        value = pieces[3]
        for other in range(3):
            value = jnp.where((shard ^ place) == other, pieces[other], value)
        out_ref[:3, place * lanes : (place + 1) * lanes] = value


def whole_vectors(own, others, width):
    return call(vectors_kernel, "vectors", (own, others), [like((8, width), F32)], 0.2)[0]


def join_rows_kernel(*refs):
    *ins, out = refs
    start = 0
    for ref in ins:
        rows = ref.shape[-2]
        out[..., start : start + rows, :] = ref[...]
        start += rows


def join_rows(*arrays):
    shape = list(arrays[0].shape)
    shape[-2] = sum(a.shape[-2] for a in arrays)
    return call(join_rows_kernel, "join_rows", arrays, [like(shape, BF16)], 0.3)[0]


def join_kernel(*refs):
    *ins, out = refs
    for at, ref in enumerate(ins):
        out[at] = ref[...]


def join(*arrays):
    return call(join_kernel, "join", arrays, [like((len(arrays), *arrays[0].shape), BF16)], 0.2)[0]


def join_turned_kernel(pair_ref, got_ref, out):
    for y_bit in range(2):
        out[2 * y_bit] = pair_ref[y_bit]
        out[2 * y_bit + 1] = got_ref[y_bit]


def join_turned(pair, got):
    return call(join_turned_kernel, "join_turned", (pair, got), [like((4, *pair.shape[1:]), BF16)], 0.2)[0]


def assemble_kernel(weights, layout, *refs):
    shard, chip, core = own_place()
    count = len(layout)
    owns, refs = refs[: len(weights)], refs[len(weights) :]
    *refs, sems = refs
    pieces, outs = (refs[:count], refs[count : 2 * count]), list(refs[2 * count :])
    for number, (weight, own) in enumerate(zip(weights, owns)):
        shard_rows = own.shape[0]
        sem = sems.at[number]
        targets = [outs.pop(0) for _ in range(weight.parts)]

        def fill(place_of):
            copies = []
            if weight.split == "columns":
                for half in range(2):
                    out, row, _ = place_of(0, half)
                    lane = aligned((core ^ half) * weight.half, weight.half, 128)
                    copies.append(pltpu.make_async_copy(own.at[:, lane], out.at[row, :], sem.at[half]))
            else:
                out, row, _ = place_of(0, 0)
                copies.append(pltpu.make_async_copy(own, out.at[row, :], sem.at[0]))
            for copy in copies:
                copy.start()
            for half in range(2):
                for number, ranges in enumerate(layout):
                    ref = pieces[half][number]
                    for start, lane in weight.slots():
                        for low, high, chips in ranges:
                            lo, hi = max(start, low), min(start + weight.rows, high)
                            if lo >= hi:
                                continue
                            for at, offset in enumerate(chips):
                                for other in range(3):
                                    inner = (chip ^ offset) * weight.rows + (lo - start)
                                    out, row, lanes = place_of(other + 1, half, inner, hi - lo, lane, weight.lanes)
                                    out[row, lanes] = ref[at, other, lo:hi, :]
            for copy in copies:
                copy.wait()

        if weight.split == "columns":

            def place_of(other, half, inner=0, rows=shard_rows, lane=0, lanes=weight.half):
                return targets[half], aligned((shard ^ other) * shard_rows + inner, rows, 16), slice(lane, lane + lanes)

            fill(place_of)
        elif weight.split == "rows":
            for near in range(2):

                def place_of(other, half, inner=0, rows=shard_rows, lane=0, lanes=0):
                    row = ((shard ^ other) & 1) * shard_rows + inner
                    at = aligned((core ^ half) * weight.half + lane, lanes, 128) if lanes else slice(None)
                    return targets[near ^ (other >> 1)], aligned(row, rows, 16), at

                pl.when(((shard >> 1) ^ core) == near)(functools.partial(fill, place_of))
        else:

            def place_of(other, half, inner=0, rows=shard_rows, lane=0, lanes=0):
                at = aligned((core ^ half) * weight.half + lane, lanes, 128) if lanes else slice(None)
                return targets[0], aligned((shard ^ other) * shard_rows + inner, rows, 16), at

            fill(place_of)


def assemble(owns, weights, layout, pieces):
    outs = []
    for weight in weights:
        rows, columns = weight.shape
        if weight.split == "columns":
            outs += [like((rows, columns // 2), BF16)] * 2
        elif weight.split == "rows":
            outs += [like((rows // 2, columns), BF16)] * 2
        else:
            outs.append(like((rows, columns), BF16))
    return call(
        functools.partial(assemble_kernel, weights, layout),
        "assemble_weights",
        (*owns, *pieces),
        outs,
        0.3 * sum(w.columns * w.rows for w in weights) / 48,
        scratch=[pltpu.SemaphoreType.DMA((len(weights), 2))],
    )


def write_blocks(grad_ref, keep_ref, send_ref, start, rows):
    shard, chip, core = own_place()
    lanes = keep_ref.shape[-1]
    for x_bit in range(2):
        for y_bit in range(2):
            for place in range(4):
                row = (shard ^ swap_bits(place)) * (4 * rows) + (chip ^ (2 * y_bit + x_bit)) * rows
                for half, out in ((0, keep_ref), (1, send_ref)):
                    out[x_bit, y_bit, place, start : start + rows, :] = grad_ref[
                        aligned(row, rows, 16), aligned((core ^ half) * lanes, lanes, 128)
                    ].astype(BF16)


def tiles(size, step=TILE):
    return [slice(i, i + step) for i in range(0, size, step)]


def inverse_rms(values):
    return lax.rsqrt(jnp.mean(values * values, axis=-1, keepdims=True) + EPSILON)


def project_kernel(picked_ref, vec_ref, wq, wk, wv, normed_ref, q_ref, k_ref, v_ref):
    for at in tiles(picked_ref.shape[0]):
        values = picked_ref[at, :].astype(F32)
        normed_ref[at, :] = (values * inverse_rms(values) * vec_ref[1:2, :]).astype(BF16)
    q_ref[...] = dot(normed_ref[...], wq[...]).astype(BF16) * 0.125
    k_ref[...] = dot(normed_ref[...], wk[...]).astype(BF16)
    v_ref[...] = dot(normed_ref[...], wv[...]).astype(BF16)


def project(picked, vectors, weights):
    flat = like(picked.shape, BF16)
    return call(project_kernel, "project", (picked, vectors, *weights), [flat] * 4, 4.5)


def low_half_lanes(rows):
    return lax.broadcasted_iota(jnp.int32, (rows, PAIR), 1) < HEAD_DIM


def attend_kernel(count, bias_ref, q_ref, k_ref, v_ref, *refs):
    later, (att_ref, probs_out, *outs), (probs_ref, sems) = refs[:count], refs[count:-2], refs[-2:]
    seqs, keep, _ = bias_ref.shape
    low_half = low_half_lanes(keep)
    copies = [
        pltpu.make_async_copy(ref, out, sems.at[at]) for at, (ref, out) in enumerate(zip((q_ref, k_ref, v_ref, *later), outs))
    ]
    for copy in copies:
        copy.start()
    for seq in range(seqs):
        bias = bias_ref[seq].astype(F32)
        rows = slice(seq * keep, (seq + 1) * keep)
        for pair in range(HEADS // 2):
            lanes = slice(pair * PAIR, (pair + 1) * PAIR)
            queries, keys, values = q_ref[rows, lanes], k_ref[rows, lanes], v_ref[rows, lanes]
            results = []
            for half in range(2):
                mine = low_half if half == 0 else ~low_half
                scores = dot_nt(jnp.where(mine, keys, 0), queries) + bias
                exponent = jnp.exp(scores - jnp.max(scores, axis=0, keepdims=True))
                probs = (exponent * (1.0 / jnp.sum(exponent, axis=0, keepdims=True))).astype(BF16)
                probs_ref[seq, 2 * pair + half] = probs
                results.append(dot_tn(probs, values))
            att_ref[rows, lanes] = jnp.where(low_half, results[0], results[1]).astype(BF16)
        copy = pltpu.make_async_copy(probs_ref.at[seq], probs_out.at[seq], sems.at[len(outs) + seq])
        copy.start()
        copies.append(copy)
    for copy in copies:
        copy.wait()


def attend(bias, queries, keys, values, later):
    seqs, keep, _ = bias.shape
    shape = (seqs, HEADS, keep, keep)
    kept = (queries, keys, values, *later)
    return call(
        functools.partial(attend_kernel, len(later)),
        "attend",
        (bias, *kept),
        [like(queries.shape, BF16), pltpu.HBM(shape, BF16)] + [pltpu.HBM(a.shape, a.dtype) for a in kept],
        6.5,
        scratch=[pltpu.VMEM(shape, BF16), pltpu.SemaphoreType.DMA((len(kept) + seqs,))],
        outside_outs=1 + len(kept),
    )


def out_kernel(att_ref, wo_ref, picked_ref, gbr_ref, vec_ref, attn_ref, nm_ref, gmlp_ref, gating_ref):
    attn_ref[...] = dot(att_ref[...], wo_ref[...])
    for at in tiles(picked_ref.shape[0]):
        values = picked_ref[at, :].astype(F32)
        middle = values + attn_ref[at, :]
        nm_ref[at, :] = (middle * inverse_rms(middle) * vec_ref[2:3, :]).astype(BF16)
        logit = jnp.sum(values * vec_ref[0:1, :], axis=-1, keepdims=True)
        gating = 1.0 / (1.0 + jnp.exp(-logit))
        gating_ref[at, :] = gating
        gmlp_ref[at, :] = (gating * gbr_ref[at, :].astype(F32)).astype(BF16)


def project_out(attended, w_out, picked, branch_grad, vectors):
    flat = like(picked.shape, BF16)
    return call(
        out_kernel,
        "project_out",
        (attended, w_out, picked, branch_grad, vectors),
        [like(picked.shape, F32), flat, flat, like((picked.shape[0], 1), F32)],
        2.0,
    )


def gelu_parts(values):
    cdf = 0.5 * (1.0 + lax.erf(values * 0.7071067811865476))
    return values * cdf, cdf + values * (jnp.exp(-0.5 * values * values) * 0.3989422804014327)


def up_kernel(nm_ref, gmlp_ref, wu_ref, act_ref, slope_ref, grad_ref):
    tokens = nm_ref.shape[0]
    for columns in tiles(wu_ref.shape[1], wu_ref.shape[1] // 2):
        for at in tiles(tokens, 128):
            activated, slope = gelu_parts(dot(nm_ref[at, :], wu_ref[:, columns]))
            act_ref[at, columns] = activated.astype(BF16)
            slope_ref[at, columns] = slope.astype(BF16)
        grad_ref[columns, :] = dot_tn(act_ref[:, columns], gmlp_ref[...]).astype(BF16)


def project_up(normed, grad_mlp, w_up):
    tokens, width = normed.shape
    units = w_up.shape[1]
    wide = like((tokens, units), BF16)
    return call(
        up_kernel,
        "project_up",
        (normed, grad_mlp, w_up),
        [wide, wide, like((units, width), BF16)],
        6.0,
    )


def down_blocks_kernel(near_ref, far_ref, keep_ref, send_ref):
    shard, chip, core = own_place()
    rows, lanes = keep_ref.shape[-2:]
    shard_rows = 4 * rows

    def fill(near):
        for place in range(4):
            other = swap_bits(place)
            ref = (near_ref, far_ref)[near ^ (other >> 1)]
            for x_bit in range(2):
                for y_bit in range(2):
                    row = ((shard ^ other) & 1) * shard_rows + (chip ^ (2 * y_bit + x_bit)) * rows
                    for half, out in ((0, keep_ref), (1, send_ref)):
                        out[x_bit, y_bit, place] = ref[
                            aligned(row, rows, 16), aligned((core ^ half) * lanes, lanes, 128)
                        ]

    for near in range(2):
        pl.when(((shard >> 1) ^ core) == near)(functools.partial(fill, near))


def down_blocks(near, far):
    units, width = near.shape
    blocks = like((2, 2, 4, units // 8, width // 2), BF16)
    return call(down_blocks_kernel, "down_blocks", (near, far), [blocks, blocks], 0.7)


def norm_back(grad_normed, values, inverse, gain):
    scaled = grad_normed * gain
    grad_gain = jnp.sum(grad_normed * values * inverse, axis=0, keepdims=True)
    grad_values = inverse * scaled - values * (inverse * inverse * inverse) * jnp.mean(
        scaled * values, axis=-1, keepdims=True
    )
    return grad_values, grad_gain


def down_kernel(step, weight, act_ref, slope_ref, nm_ref, gmlp_ref, wu_ref, wd_ref, *refs):
    *starts, mlp_ref, gnm_ref, out_ref, grad_ref = refs
    shard, chip, core = own_place()
    block = wd_ref.shape[0] // 2
    rows, lanes = weight.rows, weight.lanes
    at = slice(step * block, (step + 1) * block)
    down = wd_ref[at, :]
    mlp = dot(act_ref[:, at], down)
    grad_before = (dot_nt(gmlp_ref[...], down) * slope_ref[:, at].astype(F32)).astype(BF16)
    grad_ref[...] = dot_tn(nm_ref[...], grad_before)
    grad_nm = dot_nt(grad_before, wu_ref[:, at])
    mlp_ref[...] = starts[0][...] + mlp if starts else mlp
    gnm_ref[...] = starts[1][...] + grad_nm if starts else grad_nm
    for x_bit in range(2):
        for y_bit in range(2):
            for place in range(4):
                row = (shard ^ swap_bits(place)) * (4 * rows) + (chip ^ (2 * y_bit + x_bit)) * rows
                for part in range(block // lanes):
                    out_ref[x_bit, y_bit, place, part * rows : (part + 1) * rows, :] = grad_ref[
                        aligned(row, rows, 16), part * lanes : (part + 1) * lanes
                    ].astype(BF16)


def down(step, weight, activated, slope, normed, grad_mlp, w_up, w_down, starts=()):
    tokens, width = normed.shape
    total = like((tokens, width), F32)
    return call(
        functools.partial(down_kernel, step, weight),
        "down_and_back",
        (activated, slope, normed, grad_mlp, w_up, w_down, *starts),
        [total, total, like((2, 2, 4, weight.rows * weight.columns // 2, weight.lanes), BF16)],
        4.2,
        scratch=[pltpu.VMEM((width, w_up.shape[1] // 2), F32)],
        aliases=[(6, 0), (7, 1)] if starts else [],
    )


def branch_kernel(
    mlp_ref, gnm_ref, attn_ref, picked_ref, gbr_ref, gating_ref, vec_ref, new_ref, gattn_ref, gmid_ref, glogit_ref, sum_ref
):
    total = jnp.zeros((1, vec_ref.shape[1]), F32)
    for at in tiles(picked_ref.shape[0]):
        attention = attn_ref[at, :]
        values = picked_ref[at, :].astype(F32)
        gating = gating_ref[at, :]
        branch_grad = gbr_ref[at, :].astype(F32)
        delta = attention + mlp_ref[at, :]
        new_ref[at, :] = (values + gating * delta).astype(BF16)
        grad_gating = jnp.sum(branch_grad * delta, axis=-1, keepdims=True)
        glogit_ref[at, :] = grad_gating * gating * (1.0 - gating)
        middle = values + attention
        grad_middle, grad_gain = norm_back(gnm_ref[at, :], middle, inverse_rms(middle), vec_ref[2:3, :])
        gmid_ref[at, :] = grad_middle
        gattn_ref[at, :] = (gating * branch_grad + grad_middle).astype(BF16)
        total = total + grad_gain
    sum_ref[...] = jnp.broadcast_to(total, sum_ref.shape)


def branch(mlp, grad_nm, attn_out, picked, branch_grad, gating, vectors):
    tokens, width = picked.shape
    return call(
        branch_kernel,
        "branch_and_norm_back",
        (mlp, grad_nm, attn_out, picked, branch_grad, gating, vectors),
        [
            like((tokens, width), BF16),
            like((tokens, width), BF16),
            like((tokens, width), F32),
            like((tokens, 1), F32),
            like((8, width), F32),
        ],
        2.0,
    )


def out_back_kernel(weight, gattn_ref, att_ref, wo_ref, gatt_ref, keep_ref, send_ref, grad_ref):
    grad_ref[...] = dot_tn(att_ref[...], gattn_ref[...])
    gatt_ref[...] = dot_nt(gattn_ref[...], wo_ref[...]).astype(BF16)
    write_blocks(grad_ref, keep_ref, send_ref, 0, weight.rows)


def out_back(weight, grad_attn, attended, w_out):
    blocks = like((2, 2, 4, weight.rows, weight.lanes), BF16)
    return call(
        functools.partial(out_back_kernel, weight),
        "project_out_back",
        (grad_attn, attended, w_out),
        [like(grad_attn.shape, BF16), blocks, blocks],
        2.5,
        scratch=[pltpu.VMEM(weight.shape, F32)],
    )


def attend_back_kernel(seq, gatt_ref, q_ref, k_ref, v_ref, probs_ref, gq_ref, gk_ref, gv_ref):
    keep = probs_ref.shape[2]
    low_half = low_half_lanes(keep)
    rows = slice(seq * keep, (seq + 1) * keep)
    for pair in range(HEADS // 2):
        lanes = slice(pair * PAIR, (pair + 1) * PAIR)
        queries, keys, values = q_ref[rows, lanes], k_ref[rows, lanes], v_ref[rows, lanes]
        grad_att = gatt_ref[rows, lanes]
        found = []
        for half in range(2):
            mine = low_half if half == 0 else ~low_half
            probs = probs_ref[seq, 2 * pair + half]
            wide = probs.astype(F32)
            weighted = wide * dot_nt(jnp.where(mine, values, 0), grad_att)
            scores = (weighted - wide * jnp.sum(weighted, axis=0, keepdims=True)).astype(BF16)
            found.append((dot_tn(scores, keys) * 0.125, dot(scores, queries), dot(probs, grad_att)))
        for out, first, second in zip((gq_ref, gk_ref, gv_ref), *found):
            out[:, lanes] = jnp.where(low_half, first, second).astype(BF16)


def attend_back(seq, grad_attended, queries, keys, values, probs):
    rows = like((probs.shape[2], queries.shape[1]), BF16)
    return call(
        functools.partial(attend_back_kernel, seq),
        "attend_back",
        (grad_attended, queries, keys, values, probs),
        [rows] * 3,
        4.0,
    )


def project_grads_kernel(weights, normed_ref, *refs):
    *grads, keep_ref, send_ref, grad_ref = refs
    for i, weight in enumerate(weights):
        grad_ref[...] = dot_tn(normed_ref[...], rows_of(grads, i))
        write_blocks(grad_ref, keep_ref, send_ref, weight.start, weight.rows)


def rows_of(grads, i):
    return jnp.concatenate([ref[...] for ref in grads[i::3]], axis=0)


def project_grads(weights, normed, grads):
    blocks = like((2, 2, 4, sum(w.rows for w in weights), weights[0].lanes), BF16)
    return call(
        functools.partial(project_grads_kernel, weights),
        "project_gradients",
        (normed, *grads),
        [blocks, blocks],
        4.0,
        scratch=[pltpu.VMEM(weights[0].shape, F32)],
    )


def project_back_kernel(count, *refs):
    grads, refs = refs[:count], refs[count:]
    wq, wk, wv, picked_ref, gmid_ref, gbr_ref, glogit_ref, vec_ref, middle_ref, new_ref, sum_ref, gn_ref = refs
    gn_ref[...] = sum(dot_nt(rows_of(grads, i), w[...]) for i, w in enumerate((wq, wk, wv)))
    router = jnp.zeros((1, vec_ref.shape[1]), F32)
    total = router
    for at in tiles(picked_ref.shape[0]):
        values = picked_ref[at, :].astype(F32)
        grad_picked, grad_gain = norm_back(gn_ref[at, :], values, inverse_rms(values), vec_ref[1:2, :])
        grad_logit = glogit_ref[at, :]
        new_ref[at, :] = (
            gbr_ref[at, :].astype(F32) + grad_logit * vec_ref[0:1, :] + (grad_picked + gmid_ref[at, :])
        ).astype(BF16)
        router = router + jnp.sum(grad_logit * values, axis=0, keepdims=True)
        total = total + grad_gain
    rows = jnp.concatenate([router, total, middle_ref[0:1, :], jnp.zeros((5, router.shape[1]), F32)], axis=0)
    lanes = sum_ref.shape[1]
    sum_ref[...] = jnp.concatenate([rows[:, :lanes], rows[:, lanes:]], axis=0).astype(BF16)


def project_back(grads, weights, picked, grad_middle, branch_grad, grad_logit, vectors, gain_sums):
    tokens, width = picked.shape
    return call(
        functools.partial(project_back_kernel, len(grads)),
        "project_back",
        (*grads, *weights, picked, grad_middle, branch_grad, grad_logit, vectors, gain_sums),
        [like((tokens, width), BF16), like((VECTOR_ROWS, width // 2), BF16)],
        5.0,
        scratch=[pltpu.VMEM((tokens, width), F32)],
    )


def total_of(left, right):
    return (left.astype(F32) + right.astype(F32)).astype(BF16)


def add_first_kernel(cut, parts, extra, *refs):
    *refs, a_away, a_keep, b_away, b_keep = refs
    start = 0

    def put(x_bit, y_bit, at, begin, value):
        low, high = begin, begin + value.shape[-2]
        if low < cut:
            out = a_away if x_bit else a_keep
            out[y_bit, at, low : min(high, cut), :] = value[: min(high, cut) - low]
        if high > cut:
            out = b_away if y_bit else b_keep
            out[x_bit, at, max(low, cut) - cut : high - cut, :] = value[max(low, cut) - low :]

    for number in range(parts):
        keep, got = refs[2 * number], refs[2 * number + 1]
        for x_bit in range(2):
            for y_bit in range(2):
                for at in range(keep.shape[2]):
                    put(x_bit, y_bit, at, start, total_of(keep[x_bit, y_bit, at], got[x_bit, y_bit, at]))
        start += keep.shape[3]
    if extra:
        value = total_of(refs[-2][...], refs[-1][...])
        for x_bit in range(2):
            for y_bit in range(2):
                for at in range(4):
                    put(x_bit, y_bit, at, start, value)


def add_first(pairs, cut, extra=()):
    lanes = pairs[0][0].shape[-1]
    rows = sum(keep.shape[3] for keep, _ in pairs) + (extra[0].shape[0] if extra else 0)
    out = lambda n: like((2, 4, n, lanes), BF16)
    return call(
        functools.partial(add_first_kernel, cut, len(pairs), bool(extra)),
        "add_first",
        [array for pair in pairs for array in pair] + list(extra),
        [out(cut), out(cut), out(rows - cut), out(rows - cut)],
        0.7,
    )


def add_second_kernel(*refs):
    *refs, a_away, a_keep, b_away, b_keep = refs
    for side, (away, keep) in enumerate(((a_away, a_keep), (b_away, b_keep))):
        start = 0
        for group in range(0, len(refs), 4):
            ref, got = refs[group + 2 * side : group + 2 * side + 2]
            rows = slice(start, start + ref.shape[2])
            start = rows.stop
            for at in range(ref.shape[1]):
                keep[at, rows, :] = total_of(ref[0, at], got[0, at])
                away[at, rows, :] = total_of(ref[1, at], got[1, at])


def add_second(*groups):
    sides = [sum(group[2 * side].shape[2] for group in groups) for side in range(2)]
    shards, lanes = groups[0][0].shape[1], groups[0][0].shape[3]
    outs = [like((shards, rows, lanes), BF16) for rows in sides for _ in range(2)]
    return call(add_second_kernel, "add_second", [a for group in groups for a in group], outs, 0.5)


def add_third_kernel(a_ref, a_got, b_ref, b_got, away, keep):
    cut = a_ref.shape[1]
    for out, first in ((away, 2), (keep, 0)):
        for at in range(2):
            out[at, :cut, :] = total_of(a_ref[first + at], a_got[first + at])
            out[at, cut:, :] = total_of(b_ref[first + at], b_got[first + at])


def add_third(a_keep, a_got, b_keep, b_got):
    half = like((2, a_keep.shape[1] + b_keep.shape[1], a_keep.shape[2]), BF16)
    return call(add_third_kernel, "add_third", (a_keep, a_got, b_keep, b_got), [half, half], 0.4)


def add_fourth_kernel(keep_ref, got_ref, away, keep):
    away[...] = total_of(keep_ref[1], got_ref[1])
    keep[...] = total_of(keep_ref[0], got_ref[0])


def add_fourth(keep, got):
    half = like(keep.shape[1:], BF16)
    return call(add_fourth_kernel, "add_fourth", (keep, got), [half, half], 0.3)


def add_last_kernel(keep_ref, got_ref, out):
    out[...] = total_of(keep_ref[...], got_ref[...])


def add_last(keep, got):
    return call(add_last_kernel, "add_last", (keep, got), [like(keep.shape, BF16)], 0.3)[0]


def unpack_kernel(weights, near_ref, far_ref, *refs):
    _, chip, core = own_place()
    count = len(weights)
    done_ref, *outs = refs[: count + 1]
    inner, sems = refs[count + 1 : -1], refs[-1]
    done_ref[...] = jnp.zeros_like(done_ref)
    copies = []
    for number, (weight, ref) in enumerate(zip(weights, inner)):
        for half, blocks in enumerate((near_ref, far_ref)):
            for offset in range(4):
                for start, inside, rows, lane in weight.pieces:
                    at = aligned((chip ^ offset) * weight.rows + inside, rows, 16)
                    block = blocks[offset, start : start + rows, :]
                    ref[at, aligned((core ^ half) * weight.half + lane, weight.lanes, 128)] = block.astype(F32)
        copy = pltpu.make_async_copy(ref, outs[number], sems.at[number])
        copy.start()
        copies.append(copy)
    for copy in copies:
        copy.wait()


def unpack(weights, near, far):
    shapes = [(weight.shape[0] // 4, weight.shape[1]) for weight in weights]
    return call(
        functools.partial(unpack_kernel, weights),
        "unpack_gradients",
        (near, far),
        [like((8, 128), F32)] + [pltpu.HBM(shape, F32) for shape in shapes],
        2.0,
        scratch=[pltpu.VMEM(shape, F32) for shape in shapes] + [pltpu.SemaphoreType.DMA((len(weights),))],
        outside_outs=len(weights),
    )[1:]


def solution(mesh):
    replicas, shards = mesh.shape["rep"], mesh.shape["fsdp"]
    rep_pairs = lambda bits: [(i, i ^ bits) for i in range(replicas)]
    shard_pairs = lambda bits: [(i, i ^ bits) for i in range(shards)]
    plane = {"c": 1, "x": 2, "y": 4, "d": 6}

    def swap(values, way):
        return lax.ppermute(values, "rep", rep_pairs(plane[way]))

    def swap_shard(values, bits):
        return lax.ppermute(values, "fsdp", shard_pairs(bits))

    def swap_halves(halves, order="xy"):
        first, last = halves[:2]
        return first, swap(first, order[0]), last, swap(last, order[1])

    def swap_sums(sums, order):
        a_away, a_keep, b_away, b_keep = sums
        return a_keep, swap(a_away, order[0]), b_keep, swap(b_away, order[1])

    def over_planes(own):
        bit = 8
        while bit < replicas:
            own = total_of(own, lax.ppermute(own, "rep", rep_pairs(bit)))
            bit *= 2
        return own

    def on_device(
        hidden,
        segments,
        selected,
        w_query,
        w_key,
        w_value,
        w_out,
        w_up,
        w_down,
        w_router,
        gain_attn,
        gain_mlp,
        cotangent,
    ):
        LAST.clear()
        CALLS.clear()
        width = hidden.shape[2]
        seqs = hidden.shape[0]
        lanes = width // 2
        shard = lax.axis_index("fsdp")

        small, tall = w_query.shape[0] // 4, w_down.shape[0] // 4
        wide = w_up.shape[1] // 2 // lanes
        first_weights = [Weight(i * small, small, 1, lanes) for i in range(4)]
        up_at = Weight(0, small, wide, lanes, "columns")
        down_at = Weight(0, tall, 1, lanes, "rows")
        first_rows, second_rows = 4 * small, small * wide
        halved = lambda rows: [
            [(0, rows // 2, (0, 1)), (rows // 2, rows, (0, 2))],
            [(0, rows // 2, (2, 3)), (rows // 2, rows, (1, 3))],
        ]
        vectors = jnp.concatenate([w_router, gain_attn, gain_mlp])
        padded = jnp.pad(vectors, (0, VECTOR_ROWS * lanes - vectors.shape[0])).reshape(VECTOR_ROWS, lanes)

        first_own = pack((w_query, w_key, w_value, w_out), first_weights)
        first_second = swap_shard(first_own, 2)
        chosen, bias = choose(selected, segments)
        picked = pick_rows(hidden, chosen)
        first_pair = swap_shard(join_own(first_own, first_second), 1)
        second_own = pack((w_up,), (up_at,), (padded,))
        second_second = swap_shard(second_own, 2)
        branch_grad = pick_rows(cotangent, chosen)
        third_own = pack((w_down,), (down_at,))
        first = swap_halves(join_shards(first_pair, first_second, [first_rows // 2]))
        second_pair, third_own = join_own(second_own, second_second, [third_own])
        second_pair = swap_shard(second_pair, 1)
        third_second = swap_shard(third_own, 2)
        *first, first_both = join_chips(*first)
        first = swap_halves(first, "yx")
        first_both_far = swap(first_both, "c")
        *second, others = join_shards(second_pair, second_second, [second_rows // 2, second_rows])
        second = swap_halves(second)
        vec = whole_vectors(padded, others, width)
        third_pair = swap_shard(join_own(third_own, third_second), 1)
        first_other = join_rows(first[1], first[3])
        first_other_far = swap(first_other, "c")
        *second, second_both = join_chips(*second)
        second = swap_halves(second, "yx")
        second_both_far = swap(second_both, "c")
        cover()
        *qkv, full_out = assemble(
            (w_query, w_key, w_value, w_out),
            first_weights,
            halved(first_rows),
            (first_both, first_other, first_both_far, first_other_far),
        )
        normed, queries, keys, values = project(picked, vec, qkv)
        third = swap_halves(join_shards(third_pair, third_second, [tall // 2]))
        attended, probs, queries, keys, values, normed, *qkv = attend(bias, queries, keys, values, (normed, *qkv))
        attn_out, normed_mlp, grad_mlp, gating = project_out(attended, full_out, picked, branch_grad, vec)
        second_other = join_rows(second[1], second[3])
        second_other_far = swap(second_other, "c")
        *third, third_both = join_chips(*third)
        third = swap_halves(third, "yx")
        third_both_far = swap(third_both, "c")
        cover()
        up_near, up_far = assemble(
            (w_up,), (up_at,), halved(second_rows), (second_both, second_other, second_both_far, second_other_far)
        )
        act_far, slope_far, grad_far = project_up(normed_mlp, grad_mlp, up_far)
        act_near, slope_near, grad_near = project_up(normed_mlp, grad_mlp, up_near)

        down_keep, down_send = down_blocks(grad_near, grad_far)
        down_got = swap(down_send, "c")
        third_other = join_rows(third[1], third[3])
        third_other_far = swap(third_other, "c")
        down_near, down_far = assemble(
            (w_down,), (down_at,), halved(tall), (third_both, third_other, third_both_far, third_other_far)
        )
        far, near = (act_far, slope_far, up_far, down_far), (act_near, slope_near, up_near, down_near)

        def down_step(half, step, carried=()):
            act, slope, w_in, w_back = half
            *carried, blocks = down(step, up_at, act, slope, normed_mlp, grad_mlp, w_in, w_back, carried)
            return carried, blocks

        carried, up_send = down_step(far, 0)
        up_got = swap(up_send, "c")
        d_sums = swap_sums(add_first([(down_keep, down_got)], tall // 2), "xy")
        carried, up_keep = down_step(near, 0, carried)
        u_first = swap_sums(add_first([(up_keep, up_got)], small), "xy")
        carried, up_send = down_step(far, 1, carried)
        up_got = swap(up_send, "c")
        carried, up_keep = down_step(near, 1, carried)
        new_rows, grad_attn, grad_middle, grad_logit, gain_sums = branch(
            *carried, attn_out, picked, branch_grad, gating, vec
        )
        d_sums = swap_sums(add_second(d_sums), "yx")
        u_first = tuple(hold(*u_first))
        grad_attended, out_keep, out_send = out_back(first_weights[3], grad_attn, attended, full_out)
        out_got = swap(out_send, "c")
        cover()
        u_last = swap_sums(add_first([(up_keep, up_got), (out_keep, out_got)], 64), "xy")
        grads = []
        for seq in range(seqs):
            grads += attend_back(seq, grad_attended, queries, keys, values, probs)
            if seq == seqs - 2:
                d_away, d_keep = add_third(*d_sums)
                d_got = swap_shard(d_away, 1)
        first_keep, first_send = project_grads(first_weights[:3], normed, grads)
        first_got = swap(first_send, "c")
        d_away, d_keep = add_fourth(d_keep, d_got)
        d_got = swap_shard(d_away, 2)
        u_sums = swap_sums(add_second(u_first, u_last), "yx")
        cover()
        grad_rows, sums = project_back(
            grads, qkv, picked, grad_middle, branch_grad, grad_logit, vec, gain_sums
        )
        f_sums = swap_sums(add_first([(first_keep, first_got)], 80, (sums, swap(sums, "c"))), "xy")
        u_away, u_keep = add_third(*u_sums)
        u_got = swap_shard(u_away, 1)
        out_hidden = place_rows(range(seqs), selected, new_rows, hidden)
        f_sums = swap_sums(add_second(f_sums), "yx")
        d_own = over_planes(add_last(d_keep, d_got))
        d_got = swap(d_own, "x")
        u_away, u_keep = add_fourth(u_keep, u_got)
        u_got = swap_shard(u_away, 2)
        grad_hidden = place_rows(range(1), selected, grad_rows, cotangent)
        d_pair = join(d_own, d_got)
        d_got = swap(d_pair, "y")
        f_away, f_keep = add_third(*f_sums)
        f_got = swap_shard(f_away, 1)
        u_own = over_planes(add_last(u_keep, u_got))
        u_spread = [u_own] + [swap(u_own, way) for way in "xyd"]
        grad_hidden = place_rows(range(1, 2), selected, grad_rows, cotangent, grad_hidden)
        f_away, f_keep = add_fourth(f_keep, f_got)
        f_got = swap_shard(f_away, 2)
        grad_hidden = place_rows(range(2, seqs), selected, grad_rows, cotangent, grad_hidden)
        d_near = join(d_pair, d_got).reshape(4, *d_own.shape)
        d_far = swap(d_near, "c")
        u_near = join(*u_spread)
        u_far = swap(u_near, "c")
        f_own = over_planes(add_last(f_keep, f_got))
        f_spread = [f_own] + [swap(f_own, way) for way in "xyd"]
        cover()
        (grad_down,) = unpack((Weight(0, tall, 1, lanes),), d_near, d_far)
        up_pieces = [
            (0, 0, small, 0),
            (2 * small + 16, 0, small, lanes),
            (small, 0, small, 2 * lanes),
            (2 * small, 0, 16, 3 * lanes),
            (3 * small + 16, 16, small - 16, 3 * lanes),
        ]
        grad_up, grad_out = unpack(
            (Weight(0, small, wide, lanes, pieces=up_pieces), Weight(4 * small, small, 1, lanes)), u_near, u_far
        )
        f_near = join(*f_spread)
        grad_qkv = unpack(first_weights[:3], f_near, swap(f_near, "c"))
        sums = f_own[3 * small :].reshape(2, 8, lanes)[:, :3].swapaxes(0, 1).reshape(3, width).astype(F32)
        sums = lax.dynamic_slice(sums, (0, shard * w_router.shape[0]), (3, w_router.shape[0]))
        return (out_hidden, grad_hidden, *grad_qkv, grad_out, grad_up, grad_down, sums[0], sums[1], sums[2])

    placed = (
        P(("rep", "fsdp"), None, None),
        P(("rep", "fsdp"), None),
        P(("rep", "fsdp"), None),
        P("fsdp", None),
        P("fsdp", None),
        P("fsdp", None),
        P("fsdp", None),
        P("fsdp", None),
        P("fsdp", None),
        P("fsdp"),
        P("fsdp"),
        P("fsdp"),
        P(("rep", "fsdp"), None, None),
    )
    return jax.shard_map(
        on_device,
        mesh=mesh,
        in_specs=placed,
        out_specs=(
            P(("rep", "fsdp"), None, None),
            P(("rep", "fsdp"), None, None),
            P("fsdp", None),
            P("fsdp", None),
            P("fsdp", None),
            P("fsdp", None),
            P("fsdp", None),
            P("fsdp", None),
            P("fsdp"),
            P("fsdp"),
            P("fsdp"),
        ),
        check_vma=False,
    )
```

```python
import functools

import jax
import jax.numpy as jnp
from jax import lax
from jax.experimental import pallas as pl
from jax.experimental.pallas import tpu as pltpu
from jax.sharding import PartitionSpec as P

HEADS = 12
HEAD_DIM = 64
PAIR = 2 * HEAD_DIM
EPSILON = 1e-06
F32 = jnp.float32
BF16 = jnp.bfloat16
TILE = 256
LANES = 128
VECTOR_ROWS = 16
VMEM_BYTES = 10 * 1024 * 1024
SMALL_BYTES = 6 * 1024 * 1024
STREAM_BYTES = 28 * 1024 * 1024


def dot(left, right):
    return jnp.dot(left, right, preferred_element_type=F32)


def dot_nt(left, right):
    return lax.dot_general(left, right, (((1,), (1,)), ((), ())), preferred_element_type=F32)


def dot_tn(left, right):
    return lax.dot_general(left, right, (((0,), (0,)), ((), ())), preferred_element_type=F32)


def swap_bits(place):
    return ((place & 1) << 1) | (place >> 1)


def own_place():
    member = lax.axis_index("rep") & 7
    return lax.axis_index("fsdp"), member >> 1, member & 1


def micros(time):
    return pl.CostEstimate(flops=int(time * 1.1e9), bytes_accessed=0, transcendentals=0)


BESIDE = {
    "pack_blocks": (0.1, 0.3, 0.3),
    "choose": (0.6,),
    "pick_rows": (1.0, 0.05),
    "join_three": (1.7,),
    "join_own": (2.3, 4.3),
    "join_chips": (1.2, 0.1, 0.1),
    "cover": (9.5, 9.5, 11.0, 17.0, 9.5),
    "project": (1.0,),
    "attend": (2.4,),
    "project_out": (0.8,),
    "project_up": (2.0, 2.0),
    "down_and_back": (24.0, 12.0, 2.5, 1.0),
    "attend_back": (2.2, 0.5, 2.3),
    "project_gradients": (0.5,),
    "project_back": (1.0,),
    "place_rows": (5.2, 2.6, 2.6, 0.1),
    "add_last": (0.1, 0.1, 1.0),
    "unpack_gradients": (1.3, 2.0, 0.1),
}
CALLS = {}
LARGE = {"down_and_back", "project_back", "attend"}


def beside(name):
    number = CALLS.get(name, 0)
    CALLS[name] = number + 1
    times = BESIDE.get(name, (0.1,))
    return micros(times[min(number, len(times) - 1)])


def like(shape, dtype):
    return jax.ShapeDtypeStruct(shape, dtype)


def params(limit=VMEM_BYTES):
    return pltpu.CompilerParams(vmem_limit_bytes=limit)


ANYWHERE = pl.BlockSpec(memory_space=pl.ANY)
INSIDE = pl.BlockSpec(memory_space=pltpu.VMEM)
OUTSIDE = pl.BlockSpec(memory_space=pltpu.HBM)
LAST = []


def ordered(kernel, ins, in_specs, aliases=(), **options):
    before = tuple(LAST)

    def body(*refs):
        kernel(*refs[len(before) :])

    ins = [pltpu.with_memory_space_constraint(a, pltpu.HBM) if s is OUTSIDE else a for a, s in zip(ins, in_specs)]
    outs = pl.pallas_call(
        body,
        in_specs=[ANYWHERE] * len(before) + in_specs,
        input_output_aliases={len(before) + at: out for at, out in aliases},
        **options,
    )(*before, *ins)
    LAST[:] = [min(outs, key=lambda out: out.size)]
    return outs


def call(kernel, name, ins, outs, estimate, scratch=(), outside=0, aliases=(), outside_outs=0):
    return ordered(
        kernel,
        ins,
        [OUTSIDE] * outside + [INSIDE] * (len(ins) - outside),
        aliases,
        out_specs=[INSIDE] * (len(outs) - outside_outs) + [OUTSIDE] * outside_outs,
        out_shape=list(outs),
        scratch_shapes=list(scratch),
        compiler_params=params(VMEM_BYTES if name in LARGE else SMALL_BYTES),
        cost_estimate=beside(name),
        name=name,
    )


def choose_kernel(sel_from, seg_from, chosen_ref, bias_ref, sel_ref, seg_ref, sems):
    copies = [
        pltpu.make_async_copy(sel_from, sel_ref, sems.at[0]),
        pltpu.make_async_copy(seg_from, seg_ref, sems.at[1]),
    ]
    for copy in copies:
        copy.start()
    for copy in copies:
        copy.wait()
    seqs, keep, length = chosen_ref.shape
    square = (keep, keep)
    diagonal = lax.broadcasted_iota(jnp.int32, square, 0) == lax.broadcasted_iota(jnp.int32, square, 1)
    places = lax.broadcasted_iota(jnp.int32, (keep, length), 1)
    for seq in range(seqs):
        row = sel_ref[seq : seq + 1, :].astype(F32)
        column = jnp.sum(jnp.where(diagonal, row, 0.0), axis=1, keepdims=True)
        chosen = jnp.where(column.astype(jnp.int32) == places, 1.0, 0.0).astype(BF16)
        chosen_ref[seq] = chosen
        documents = jnp.broadcast_to(seg_ref[seq : seq + 1, :].astype(F32), (8, length)).astype(BF16)
        of_column = dot_nt(chosen, documents)[:, :1]
        of_row = jnp.sum(jnp.where(diagonal, of_column, 0.0), axis=0, keepdims=True)
        allowed = (row >= column) & (of_column == of_row)
        bias_ref[seq] = jnp.where(allowed, 0.0, -1e30).astype(BF16)


def choose(selected, segments):
    seqs, keep = selected.shape
    length = segments.shape[1]
    return ordered(
        choose_kernel,
        (selected, segments),
        [OUTSIDE] * 2,
        out_specs=[INSIDE] * 2,
        out_shape=[like((seqs, keep, length), BF16), like((seqs, keep, keep), BF16)],
        scratch_shapes=[
            pltpu.VMEM(selected.shape, selected.dtype),
            pltpu.VMEM(segments.shape, segments.dtype),
            pltpu.SemaphoreType.DMA((2,)),
        ],
        compiler_params=params(),
        cost_estimate=beside("choose"),
        name="choose_rows",
    )


def pick_kernel(rows_ref, chosen_ref, picked_ref, buffer, sems):
    seqs, keep, _ = chosen_ref.shape
    copies = [pltpu.make_async_copy(rows_ref.at[seq], buffer.at[seq], sems.at[seq]) for seq in range(seqs)]
    for copy in copies:
        copy.start()
    for seq, copy in enumerate(copies):
        copy.wait()
        picked_ref[seq * keep : (seq + 1) * keep, :] = dot(chosen_ref[seq], buffer[seq]).astype(BF16)


def pick_rows(rows, chosen):
    seqs, _, width = rows.shape
    return ordered(
        pick_kernel,
        (rows, chosen),
        [OUTSIDE, INSIDE],
        out_specs=[INSIDE],
        out_shape=[like((seqs * chosen.shape[1], width), BF16)],
        scratch_shapes=[pltpu.VMEM(rows.shape, BF16), pltpu.SemaphoreType.DMA((seqs,))],
        compiler_params=params(STREAM_BYTES),
        cost_estimate=beside("pick_rows"),
        name="pick_rows",
    )[0]


def place_kernel(seqs, sel_ref, new_ref, base_ref, *refs):
    out_ref, done_ref, buffer, wide_ref, in_sems, out_sems = refs[-6:]
    done_ref[...] = jnp.zeros_like(done_ref)
    length, width = base_ref.shape[1:]
    keep = sel_ref.shape[1]
    chunks = [(number, seq, part) for number, seq in enumerate(seqs) for part in tiles(length, length // 2)]
    copies = [
        pltpu.make_async_copy(base_ref.at[seq, part, :], buffer.at[number, part, :], in_sems.at[at])
        for at, (number, seq, part) in enumerate(chunks)
    ]
    for copy in copies:
        copy.start()
    for number, seq in enumerate(seqs):
        wide_ref[number, :, :width] = new_ref[seq * keep : (seq + 1) * keep, :]
        wide_ref[number, :, width:] = jnp.ones((keep, LANES), BF16)
    results = []
    for at, (number, seq, part) in enumerate(chunks):
        places = lax.broadcasted_iota(jnp.int32, (part.stop - part.start, keep), 0) + part.start
        hits = jnp.where(places == sel_ref[seq : seq + 1, :], 1.0, 0.0).astype(BF16)
        copies[at].wait()
        for row in range(0, part.stop - part.start, TILE):
            placed = dot(hits[row : row + TILE, :], wide_ref[number])
            new = placed[:, width:] > 0.0
            rows = slice(part.start + row, part.start + row + TILE)
            for lane in range(0, width, LANES):
                lanes = slice(lane, lane + LANES)
                base = buffer[number, rows, lanes].astype(F32)
                buffer[number, rows, lanes] = jnp.where(new, placed[:, lanes], base).astype(BF16)
        back = pltpu.make_async_copy(buffer.at[number, part, :], out_ref.at[seq, part, :], out_sems.at[at])
        back.start()
        results.append(back)
    for back in results:
        back.wait()


def place_rows(seqs, selected, new_rows, base, placed=None):
    _, length, width = base.shape
    earlier = () if placed is None else (placed,)
    return ordered(
        functools.partial(place_kernel, tuple(seqs)),
        (selected, new_rows, base, *earlier),
        [INSIDE, INSIDE, OUTSIDE] + [OUTSIDE] * len(earlier),
        aliases=[(3, 0)] if earlier else [],
        out_specs=[OUTSIDE, INSIDE],
        out_shape=[pltpu.HBM(base.shape, BF16), like((8, 128), F32)],
        scratch_shapes=[
            pltpu.VMEM((len(seqs), length, width), BF16),
            pltpu.VMEM((len(seqs), selected.shape[1], width + LANES), BF16),
        ]
        + [pltpu.SemaphoreType.DMA((2 * len(seqs),))] * 2,
        compiler_params=params(STREAM_BYTES),
        cost_estimate=beside("place_rows"),
        name="place_rows",
    )[0]


class Weight:
    def __init__(self, start, rows, columns, lanes, split=None, pieces=None):
        self.start, self.rows, self.columns, self.lanes, self.split = start, rows, columns, lanes, split
        self.parts = 1 if split is None else 2
        self.half = columns * lanes
        self.shape = (16 * rows, 2 * self.half)
        self.pieces = pieces or [(at, 0, rows, lane) for at, lane in self.slots()]

    def slots(self):
        return [(self.start + c * self.rows, c * self.lanes) for c in range(self.columns)]


def aligned(value, size, multiple):
    return pl.ds(pl.multiple_of(value, multiple), size)


def pack_kernel(weights, *refs):
    _, chip, core = own_place()
    *ins, out_ref, sem = refs
    for own, weight in zip(ins, weights):
        for start, lane in weight.slots():
            pltpu.make_async_copy(
                own.at[
                    aligned(chip * weight.rows, weight.rows, 16), aligned(core * weight.half + lane, weight.lanes, 128)
                ],
                out_ref.at[start : start + weight.rows, :],
                sem,
            ).start()
    for extra in ins[len(weights) :]:
        pltpu.make_async_copy(extra, out_ref.at[out_ref.shape[0] - extra.shape[0] :, :], sem).start()
    pltpu.make_async_copy(out_ref, out_ref, sem).wait()


def pack(owns, weights, extra=()):
    rows = sum(w.rows * w.columns for w in weights) + sum(e.shape[0] for e in extra)
    return call(
        functools.partial(pack_kernel, weights),
        "pack_blocks",
        (*owns, *extra),
        [like((rows, weights[0].lanes), BF16)],
        0.5,
        scratch=[pltpu.SemaphoreType.DMA],
        outside=len(owns) + len(extra),
    )[0]


def join_own_kernel(own_ref, second_ref, *refs):
    *held, out_ref, out_held = refs if len(refs) > 1 else (*refs, None)
    for ref in held:
        out_held[...] = ref[...]
    out_ref[0] = own_ref[...]
    out_ref[1] = second_ref[...]


def join_own(own, second, held=()):
    outs = [like((2, *own.shape), BF16)] + [like(a.shape, a.dtype) for a in held]
    outs = call(join_own_kernel, "join_own", (own, second, *held), outs, 0.2)
    return outs if held else outs[0]


def join_shards_kernel(count, pair_ref, second_ref, *refs):
    held, outs = refs[:count], refs[count:]
    for ref, out in zip(held, outs[len(outs) - count :]):
        out[...] = ref[...]
    start = 0
    for out in outs[: len(outs) - count]:
        rows = slice(start, start + out.shape[1])
        start = rows.stop
        out[0] = pair_ref[0, rows, :]
        out[1] = second_ref[rows, :]
        out[2] = pair_ref[1, rows, :]


def join_shards(pair, second, cuts, held=()):
    _, rows, lanes = pair.shape
    edges = [0, *cuts, rows]
    outs = [like((3, high - low, lanes), BF16) for low, high in zip(edges, edges[1:])]
    outs += [like(a.shape, a.dtype) for a in held]
    return call(functools.partial(join_shards_kernel, len(held)), "join_shards", (pair, second, *held), outs, 0.3)


def hold_kernel(*refs):
    count = len(refs) // 2
    for ref, out in zip(refs[:count], refs[count:]):
        out[...] = ref[...]


def hold(*arrays):
    return call(hold_kernel, "hold", arrays, [like(a.shape, a.dtype) for a in arrays], 0.2)


def cover_kernel(out_ref):
    out_ref[...] = jnp.zeros_like(out_ref)


def cover():
    call(cover_kernel, "cover", (), [like((8, 128), F32)], 0.1)


def join_three_kernel(first_ref, second_ref, third_ref, *outs):
    start = 0
    for out in outs:
        rows = slice(start, start + out.shape[1])
        start = rows.stop
        for at, ref in enumerate((first_ref, second_ref, third_ref)):
            out[at] = ref[rows, :]


def join_three(pieces, cut):
    rows, lanes = pieces[0].shape
    outs = [like((3, cut, lanes), BF16), like((3, rows - cut, lanes), BF16)]
    return call(join_three_kernel, "join_three", pieces, outs, 0.3)


def join_chips_kernel(first_ref, first_got, last_ref, last_got, first_out, last_out, both_out):
    cut = first_ref.shape[1]
    for at, (first, last) in enumerate(((first_ref, last_ref), (first_got, last_got))):
        first_out[at] = first[...]
        last_out[at] = last[...]
        both_out[at, :, :cut, :] = first[...]
        both_out[at, :, cut:, :] = last[...]


def join_chips(first, first_got, last, last_got):
    count, cut, lanes = first.shape
    rows = last.shape[1]
    shapes = [(2, count, cut, lanes), (2, count, rows, lanes), (2, count, cut + rows, lanes)]
    return call(
        join_chips_kernel, "join_chips", (first, first_got, last, last_got), [like(s, BF16) for s in shapes], 0.5
    )


def vectors_kernel(own_ref, others_ref, out_ref):
    shard, _, _ = own_place()
    lanes = out_ref.shape[1] // 4
    pieces = []
    for ref in (own_ref, *[others_ref.at[other] for other in range(3)]):
        rows = ref[...].astype(F32)
        pieces.append(jnp.concatenate([rows[:1, :lanes], rows[:1, lanes:], rows[1:2, :lanes]], axis=0))
    out_ref[...] = jnp.zeros_like(out_ref)
    for place in range(4):
        value = pieces[3]
        for other in range(3):
            value = jnp.where((shard ^ place) == other, pieces[other], value)
        out_ref[:3, place * lanes : (place + 1) * lanes] = value


def whole_vectors(own, others, width):
    return call(vectors_kernel, "vectors", (own, others), [like((8, width), F32)], 0.2)[0]


def join_rows_kernel(*refs):
    *ins, out = refs
    start = 0
    for ref in ins:
        rows = ref.shape[-2]
        out[..., start : start + rows, :] = ref[...]
        start += rows


def join_rows(*arrays):
    shape = list(arrays[0].shape)
    shape[-2] = sum(a.shape[-2] for a in arrays)
    return call(join_rows_kernel, "join_rows", arrays, [like(shape, BF16)], 0.3)[0]


def join_kernel(*refs):
    *ins, out = refs
    for at, ref in enumerate(ins):
        out[at] = ref[...]


def join(*arrays):
    return call(join_kernel, "join", arrays, [like((len(arrays), *arrays[0].shape), BF16)], 0.2)[0]


def join_turned_kernel(pair_ref, got_ref, out):
    for y_bit in range(2):
        out[2 * y_bit] = pair_ref[y_bit]
        out[2 * y_bit + 1] = got_ref[y_bit]


def join_turned(pair, got):
    return call(join_turned_kernel, "join_turned", (pair, got), [like((4, *pair.shape[1:]), BF16)], 0.2)[0]


def assemble_kernel(weights, layout, *refs):
    shard, chip, core = own_place()
    count = len(layout)
    owns, refs = refs[: len(weights)], refs[len(weights) :]
    *refs, sems = refs
    pieces, outs = (refs[:count], refs[count : 2 * count]), list(refs[2 * count :])
    for number, (weight, own) in enumerate(zip(weights, owns)):
        shard_rows = own.shape[0]
        sem = sems.at[number]
        targets = [outs.pop(0) for _ in range(weight.parts)]

        def fill(place_of):
            copies = []
            if weight.split == "columns":
                for half in range(2):
                    out, row, _ = place_of(0, half)
                    lane = aligned((core ^ half) * weight.half, weight.half, 128)
                    copies.append(pltpu.make_async_copy(own.at[:, lane], out.at[row, :], sem.at[half]))
            else:
                out, row, _ = place_of(0, 0)
                copies.append(pltpu.make_async_copy(own, out.at[row, :], sem.at[0]))
            for copy in copies:
                copy.start()
            for half in range(2):
                for number, ranges in enumerate(layout):
                    ref = pieces[half][number]
                    for start, lane in weight.slots():
                        for low, high, chips in ranges:
                            lo, hi = max(start, low), min(start + weight.rows, high)
                            if lo >= hi:
                                continue
                            for at, offset in enumerate(chips):
                                for other in range(3):
                                    inner = (chip ^ offset) * weight.rows + (lo - start)
                                    out, row, lanes = place_of(other + 1, half, inner, hi - lo, lane, weight.lanes)
                                    out[row, lanes] = ref[at, other, lo:hi, :]
            for copy in copies:
                copy.wait()

        if weight.split == "columns":

            def place_of(other, half, inner=0, rows=shard_rows, lane=0, lanes=weight.half):
                return targets[half], aligned((shard ^ other) * shard_rows + inner, rows, 16), slice(lane, lane + lanes)

            fill(place_of)
        elif weight.split == "rows":
            for near in range(2):

                def place_of(other, half, inner=0, rows=shard_rows, lane=0, lanes=0):
                    row = ((shard ^ other) & 1) * shard_rows + inner
                    at = aligned((core ^ half) * weight.half + lane, lanes, 128) if lanes else slice(None)
                    return targets[near ^ (other >> 1)], aligned(row, rows, 16), at

                pl.when(((shard >> 1) ^ core) == near)(functools.partial(fill, place_of))
        else:

            def place_of(other, half, inner=0, rows=shard_rows, lane=0, lanes=0):
                at = aligned((core ^ half) * weight.half + lane, lanes, 128) if lanes else slice(None)
                return targets[0], aligned((shard ^ other) * shard_rows + inner, rows, 16), at

            fill(place_of)


def assemble(owns, weights, layout, pieces):
    outs = []
    for weight in weights:
        rows, columns = weight.shape
        if weight.split == "columns":
            outs += [like((rows, columns // 2), BF16)] * 2
        elif weight.split == "rows":
            outs += [like((rows // 2, columns), BF16)] * 2
        else:
            outs.append(like((rows, columns), BF16))
    return call(
        functools.partial(assemble_kernel, weights, layout),
        "assemble_weights",
        (*owns, *pieces),
        outs,
        0.3 * sum(w.columns * w.rows for w in weights) / 48,
        scratch=[pltpu.SemaphoreType.DMA((len(weights), 2))],
    )


def write_blocks(grad_ref, keep_ref, send_ref, start, rows):
    shard, chip, core = own_place()
    lanes = keep_ref.shape[-1]
    for x_bit in range(2):
        for y_bit in range(2):
            for place in range(4):
                row = (shard ^ swap_bits(place)) * (4 * rows) + (chip ^ (2 * y_bit + x_bit)) * rows
                for half, out in ((0, keep_ref), (1, send_ref)):
                    out[x_bit, y_bit, place, start : start + rows, :] = grad_ref[
                        aligned(row, rows, 16), aligned((core ^ half) * lanes, lanes, 128)
                    ].astype(BF16)


def tiles(size, step=TILE):
    return [slice(i, i + step) for i in range(0, size, step)]


def inverse_rms(values):
    return lax.rsqrt(jnp.mean(values * values, axis=-1, keepdims=True) + EPSILON)


def project_kernel(picked_ref, vec_ref, wq, wk, wv, normed_ref, q_ref, k_ref, v_ref):
    for at in tiles(picked_ref.shape[0]):
        values = picked_ref[at, :].astype(F32)
        normed_ref[at, :] = (values * inverse_rms(values) * vec_ref[1:2, :]).astype(BF16)
    q_ref[...] = dot(normed_ref[...], wq[...]).astype(BF16) * 0.125
    k_ref[...] = dot(normed_ref[...], wk[...]).astype(BF16)
    v_ref[...] = dot(normed_ref[...], wv[...]).astype(BF16)


def project(picked, vectors, weights):
    flat = like(picked.shape, BF16)
    return call(project_kernel, "project", (picked, vectors, *weights), [flat] * 4, 4.5)


def low_half_lanes(rows):
    return lax.broadcasted_iota(jnp.int32, (rows, PAIR), 1) < HEAD_DIM


def split_heads(low_half, values):
    return jnp.concatenate([jnp.where(low_half, values, 0), jnp.where(low_half, 0, values)], axis=0)


def join_heads(low_half, values):
    rows = low_half.shape[0]
    return jnp.where(low_half, values[:rows], values[rows:]).astype(BF16)


def attend_kernel(count, bias_ref, q_ref, k_ref, v_ref, *refs):
    later, (att_ref, probs_out, *outs), (probs_ref, sems) = refs[:count], refs[count:-2], refs[-2:]
    seqs, keep, _ = bias_ref.shape
    low_half = low_half_lanes(keep)
    copies = [
        pltpu.make_async_copy(ref, out, sems.at[at]) for at, (ref, out) in enumerate(zip((q_ref, k_ref, v_ref, *later), outs))
    ]
    for copy in copies:
        copy.start()
    for seq in range(seqs):
        bias = bias_ref[seq].astype(F32)
        rows = slice(seq * keep, (seq + 1) * keep)
        for pair in range(HEADS // 2):
            lanes = slice(pair * PAIR, (pair + 1) * PAIR)
            queries, keys, values = q_ref[rows, lanes], k_ref[rows, lanes], v_ref[rows, lanes]
            scores = dot_nt(split_heads(low_half, keys), queries)
            both = []
            for half in range(2):
                own = scores[half * keep : (half + 1) * keep] + bias
                exponent = jnp.exp(own - jnp.max(own, axis=0, keepdims=True))
                both.append((exponent * (1.0 / jnp.sum(exponent, axis=0, keepdims=True))).astype(BF16))
                probs_ref[seq, 2 * pair + half] = both[half]
            att_ref[rows, lanes] = join_heads(low_half, dot_tn(jnp.concatenate(both, axis=1), values))
        copy = pltpu.make_async_copy(probs_ref.at[seq], probs_out.at[seq], sems.at[len(outs) + seq])
        copy.start()
        copies.append(copy)
    for copy in copies:
        copy.wait()


def attend(bias, queries, keys, values, later):
    seqs, keep, _ = bias.shape
    shape = (seqs, HEADS, keep, keep)
    kept = (queries, keys, values, *later)
    return call(
        functools.partial(attend_kernel, len(later)),
        "attend",
        (bias, *kept),
        [like(queries.shape, BF16), pltpu.HBM(shape, BF16)] + [pltpu.HBM(a.shape, a.dtype) for a in kept],
        6.5,
        scratch=[pltpu.VMEM(shape, BF16), pltpu.SemaphoreType.DMA((len(kept) + seqs,))],
        outside_outs=1 + len(kept),
    )


def out_kernel(att_ref, wo_ref, picked_ref, gbr_ref, vec_ref, attn_ref, nm_ref, gmlp_ref, gating_ref):
    attn_ref[...] = dot(att_ref[...], wo_ref[...])
    for at in tiles(picked_ref.shape[0]):
        values = picked_ref[at, :].astype(F32)
        middle = values + attn_ref[at, :]
        nm_ref[at, :] = (middle * inverse_rms(middle) * vec_ref[2:3, :]).astype(BF16)
        logit = jnp.sum(values * vec_ref[0:1, :], axis=-1, keepdims=True)
        gating = 1.0 / (1.0 + jnp.exp(-logit))
        gating_ref[at, :] = gating
        gmlp_ref[at, :] = (gating * gbr_ref[at, :].astype(F32)).astype(BF16)


def project_out(attended, w_out, picked, branch_grad, vectors):
    flat = like(picked.shape, BF16)
    return call(
        out_kernel,
        "project_out",
        (attended, w_out, picked, branch_grad, vectors),
        [like(picked.shape, F32), flat, flat, like((picked.shape[0], 1), F32)],
        2.0,
    )


def gelu_parts(values):
    cdf = 0.5 * (1.0 + lax.erf(values * 0.7071067811865476))
    return values * cdf, cdf + values * (jnp.exp(-0.5 * values * values) * 0.3989422804014327)


def up_kernel(nm_ref, gmlp_ref, wu_ref, act_ref, slope_ref, grad_ref):
    tokens = nm_ref.shape[0]
    for columns in tiles(wu_ref.shape[1], wu_ref.shape[1] // 2):
        for at in tiles(tokens, 128):
            activated, slope = gelu_parts(dot(nm_ref[at, :], wu_ref[:, columns]))
            act_ref[at, columns] = activated.astype(BF16)
            slope_ref[at, columns] = slope.astype(BF16)
        grad_ref[columns, :] = dot_tn(act_ref[:, columns], gmlp_ref[...]).astype(BF16)


def project_up(normed, grad_mlp, w_up):
    tokens, width = normed.shape
    units = w_up.shape[1]
    wide = like((tokens, units), BF16)
    return call(
        up_kernel,
        "project_up",
        (normed, grad_mlp, w_up),
        [wide, wide, like((units, width), BF16)],
        6.0,
    )


def down_blocks_kernel(near_ref, far_ref, keep_ref, send_ref):
    shard, chip, core = own_place()
    rows, lanes = keep_ref.shape[-2:]
    shard_rows = 4 * rows

    def fill(near):
        for place in range(4):
            other = swap_bits(place)
            ref = (near_ref, far_ref)[near ^ (other >> 1)]
            for x_bit in range(2):
                for y_bit in range(2):
                    row = ((shard ^ other) & 1) * shard_rows + (chip ^ (2 * y_bit + x_bit)) * rows
                    for half, out in ((0, keep_ref), (1, send_ref)):
                        out[x_bit, y_bit, place] = ref[
                            aligned(row, rows, 16), aligned((core ^ half) * lanes, lanes, 128)
                        ]

    for near in range(2):
        pl.when(((shard >> 1) ^ core) == near)(functools.partial(fill, near))


def down_blocks(near, far):
    units, width = near.shape
    blocks = like((2, 2, 4, units // 8, width // 2), BF16)
    return call(down_blocks_kernel, "down_blocks", (near, far), [blocks, blocks], 0.7)


def norm_back(grad_normed, values, inverse, gain):
    scaled = grad_normed * gain
    grad_gain = jnp.sum(grad_normed * values * inverse, axis=0, keepdims=True)
    grad_values = inverse * scaled - values * (inverse * inverse * inverse) * jnp.mean(
        scaled * values, axis=-1, keepdims=True
    )
    return grad_values, grad_gain


def down_kernel(step, weight, act_ref, slope_ref, nm_ref, gmlp_ref, wu_ref, wd_ref, *refs):
    *starts, mlp_ref, gnm_ref, out_ref, grad_ref = refs
    shard, chip, core = own_place()
    block = wd_ref.shape[0] // 2
    rows, lanes = weight.rows, weight.lanes
    at = slice(step * block, (step + 1) * block)
    down = wd_ref[at, :]
    mlp = dot(act_ref[:, at], down)
    grad_before = (dot_nt(gmlp_ref[...], down) * slope_ref[:, at].astype(F32)).astype(BF16)
    grad_ref[...] = dot_tn(nm_ref[...], grad_before)
    grad_nm = dot_nt(grad_before, wu_ref[:, at])
    mlp_ref[...] = starts[0][...] + mlp if starts else mlp
    gnm_ref[...] = starts[1][...] + grad_nm if starts else grad_nm
    for x_bit in range(2):
        for y_bit in range(2):
            for place in range(4):
                row = (shard ^ swap_bits(place)) * (4 * rows) + (chip ^ (2 * y_bit + x_bit)) * rows
                for part in range(block // lanes):
                    out_ref[x_bit, y_bit, place, part * rows : (part + 1) * rows, :] = grad_ref[
                        aligned(row, rows, 16), part * lanes : (part + 1) * lanes
                    ].astype(BF16)


def down(step, weight, activated, slope, normed, grad_mlp, w_up, w_down, starts=()):
    tokens, width = normed.shape
    total = like((tokens, width), F32)
    return call(
        functools.partial(down_kernel, step, weight),
        "down_and_back",
        (activated, slope, normed, grad_mlp, w_up, w_down, *starts),
        [total, total, like((2, 2, 4, weight.rows * weight.columns // 2, weight.lanes), BF16)],
        4.2,
        scratch=[pltpu.VMEM((width, w_up.shape[1] // 2), F32)],
        aliases=[(6, 0), (7, 1)] if starts else [],
    )


def branch_kernel(
    mlp_ref, gnm_ref, attn_ref, picked_ref, gbr_ref, gating_ref, vec_ref, new_ref, gattn_ref, gmid_ref, glogit_ref, sum_ref
):
    total = jnp.zeros((1, vec_ref.shape[1]), F32)
    for at in tiles(picked_ref.shape[0]):
        attention = attn_ref[at, :]
        values = picked_ref[at, :].astype(F32)
        gating = gating_ref[at, :]
        branch_grad = gbr_ref[at, :].astype(F32)
        delta = attention + mlp_ref[at, :]
        new_ref[at, :] = (values + gating * delta).astype(BF16)
        grad_gating = jnp.sum(branch_grad * delta, axis=-1, keepdims=True)
        glogit_ref[at, :] = grad_gating * gating * (1.0 - gating)
        middle = values + attention
        grad_middle, grad_gain = norm_back(gnm_ref[at, :], middle, inverse_rms(middle), vec_ref[2:3, :])
        gmid_ref[at, :] = grad_middle
        gattn_ref[at, :] = (gating * branch_grad + grad_middle).astype(BF16)
        total = total + grad_gain
    sum_ref[...] = jnp.broadcast_to(total, sum_ref.shape)


def branch(mlp, grad_nm, attn_out, picked, branch_grad, gating, vectors):
    tokens, width = picked.shape
    return call(
        branch_kernel,
        "branch_and_norm_back",
        (mlp, grad_nm, attn_out, picked, branch_grad, gating, vectors),
        [
            like((tokens, width), BF16),
            like((tokens, width), BF16),
            like((tokens, width), F32),
            like((tokens, 1), F32),
            like((8, width), F32),
        ],
        2.0,
    )


def out_back_kernel(weight, gattn_ref, att_ref, wo_ref, gatt_ref, keep_ref, send_ref, grad_ref):
    grad_ref[...] = dot_tn(att_ref[...], gattn_ref[...])
    gatt_ref[...] = dot_nt(gattn_ref[...], wo_ref[...]).astype(BF16)
    write_blocks(grad_ref, keep_ref, send_ref, 0, weight.rows)


def out_back(weight, grad_attn, attended, w_out):
    blocks = like((2, 2, 4, weight.rows, weight.lanes), BF16)
    return call(
        functools.partial(out_back_kernel, weight),
        "project_out_back",
        (grad_attn, attended, w_out),
        [like(grad_attn.shape, BF16), blocks, blocks],
        2.5,
        scratch=[pltpu.VMEM(weight.shape, F32)],
    )


def attend_back_kernel(seq, gatt_ref, q_ref, k_ref, v_ref, probs_ref, gq_ref, gk_ref, gv_ref):
    keep = probs_ref.shape[2]
    low_half = low_half_lanes(keep)
    rows = slice(seq * keep, (seq + 1) * keep)
    for pair in range(HEADS // 2):
        lanes = slice(pair * PAIR, (pair + 1) * PAIR)
        queries, keys, values = q_ref[rows, lanes], k_ref[rows, lanes], v_ref[rows, lanes]
        grad_att = gatt_ref[rows, lanes]
        grad_probs = dot_nt(split_heads(low_half, values), grad_att)
        probs = [probs_ref[seq, 2 * pair + half] for half in range(2)]
        scores = []
        for half in range(2):
            wide = probs[half].astype(F32)
            weighted = wide * grad_probs[half * keep : (half + 1) * keep]
            scores.append((weighted - wide * jnp.sum(weighted, axis=0, keepdims=True)).astype(BF16))
        gq_ref[:, lanes] = join_heads(low_half, dot_tn(jnp.concatenate(scores, axis=1), keys) * 0.125)
        gk_ref[:, lanes] = join_heads(low_half, dot(jnp.concatenate(scores, axis=0), queries))
        gv_ref[:, lanes] = join_heads(low_half, dot(jnp.concatenate(probs, axis=0), grad_att))


def attend_back(seq, grad_attended, queries, keys, values, probs):
    rows = like((probs.shape[2], queries.shape[1]), BF16)
    return call(
        functools.partial(attend_back_kernel, seq),
        "attend_back",
        (grad_attended, queries, keys, values, probs),
        [rows] * 3,
        4.0,
    )


def project_grads_kernel(weights, normed_ref, *refs):
    *grads, keep_ref, send_ref, grad_ref = refs
    for i, weight in enumerate(weights):
        grad_ref[...] = dot_tn(normed_ref[...], rows_of(grads, i))
        write_blocks(grad_ref, keep_ref, send_ref, weight.start, weight.rows)


def rows_of(grads, i):
    return jnp.concatenate([ref[...] for ref in grads[i::3]], axis=0)


def project_grads(weights, normed, grads):
    blocks = like((2, 2, 4, sum(w.rows for w in weights), weights[0].lanes), BF16)
    return call(
        functools.partial(project_grads_kernel, weights),
        "project_gradients",
        (normed, *grads),
        [blocks, blocks],
        4.0,
        scratch=[pltpu.VMEM(weights[0].shape, F32)],
    )


def project_back_kernel(count, *refs):
    grads, refs = refs[:count], refs[count:]
    wq, wk, wv, picked_ref, gmid_ref, gbr_ref, glogit_ref, vec_ref, middle_ref, new_ref, sum_ref, gn_ref = refs
    gn_ref[...] = sum(dot_nt(rows_of(grads, i), w[...]) for i, w in enumerate((wq, wk, wv)))
    router = jnp.zeros((1, vec_ref.shape[1]), F32)
    total = router
    for at in tiles(picked_ref.shape[0]):
        values = picked_ref[at, :].astype(F32)
        grad_picked, grad_gain = norm_back(gn_ref[at, :], values, inverse_rms(values), vec_ref[1:2, :])
        grad_logit = glogit_ref[at, :]
        new_ref[at, :] = (
            gbr_ref[at, :].astype(F32) + grad_logit * vec_ref[0:1, :] + (grad_picked + gmid_ref[at, :])
        ).astype(BF16)
        router = router + jnp.sum(grad_logit * values, axis=0, keepdims=True)
        total = total + grad_gain
    rows = jnp.concatenate([router, total, middle_ref[0:1, :], jnp.zeros((5, router.shape[1]), F32)], axis=0)
    lanes = sum_ref.shape[1]
    sum_ref[...] = jnp.concatenate([rows[:, :lanes], rows[:, lanes:]], axis=0).astype(BF16)


def project_back(grads, weights, picked, grad_middle, branch_grad, grad_logit, vectors, gain_sums):
    tokens, width = picked.shape
    return call(
        functools.partial(project_back_kernel, len(grads)),
        "project_back",
        (*grads, *weights, picked, grad_middle, branch_grad, grad_logit, vectors, gain_sums),
        [like((tokens, width), BF16), like((VECTOR_ROWS, width // 2), BF16)],
        5.0,
        scratch=[pltpu.VMEM((tokens, width), F32)],
    )


def total_of(left, right):
    return (left.astype(F32) + right.astype(F32)).astype(BF16)


def add_first_kernel(cut, parts, extra, *refs):
    *refs, a_away, a_keep, b_away, b_keep = refs
    start = 0

    def put(x_bit, y_bit, at, begin, value):
        low, high = begin, begin + value.shape[-2]
        if low < cut:
            out = a_away if x_bit else a_keep
            out[y_bit, at, low : min(high, cut), :] = value[: min(high, cut) - low]
        if high > cut:
            out = b_away if y_bit else b_keep
            out[x_bit, at, max(low, cut) - cut : high - cut, :] = value[max(low, cut) - low :]

    for number in range(parts):
        keep, got = refs[2 * number], refs[2 * number + 1]
        for x_bit in range(2):
            for y_bit in range(2):
                for at in range(keep.shape[2]):
                    put(x_bit, y_bit, at, start, total_of(keep[x_bit, y_bit, at], got[x_bit, y_bit, at]))
        start += keep.shape[3]
    if extra:
        value = total_of(refs[-2][...], refs[-1][...])
        for x_bit in range(2):
            for y_bit in range(2):
                for at in range(4):
                    put(x_bit, y_bit, at, start, value)


def add_first(pairs, cut, extra=()):
    lanes = pairs[0][0].shape[-1]
    rows = sum(keep.shape[3] for keep, _ in pairs) + (extra[0].shape[0] if extra else 0)
    out = lambda n: like((2, 4, n, lanes), BF16)
    return call(
        functools.partial(add_first_kernel, cut, len(pairs), bool(extra)),
        "add_first",
        [array for pair in pairs for array in pair] + list(extra),
        [out(cut), out(cut), out(rows - cut), out(rows - cut)],
        0.7,
    )


def add_second_kernel(*refs):
    *refs, a_away, a_keep, b_away, b_keep = refs
    for side, (away, keep) in enumerate(((a_away, a_keep), (b_away, b_keep))):
        start = 0
        for group in range(0, len(refs), 4):
            ref, got = refs[group + 2 * side : group + 2 * side + 2]
            rows = slice(start, start + ref.shape[2])
            start = rows.stop
            for at in range(ref.shape[1]):
                keep[at, rows, :] = total_of(ref[0, at], got[0, at])
                away[at, rows, :] = total_of(ref[1, at], got[1, at])


def add_second(*groups):
    sides = [sum(group[2 * side].shape[2] for group in groups) for side in range(2)]
    shards, lanes = groups[0][0].shape[1], groups[0][0].shape[3]
    outs = [like((shards, rows, lanes), BF16) for rows in sides for _ in range(2)]
    return call(add_second_kernel, "add_second", [a for group in groups for a in group], outs, 0.5)


def add_third_kernel(a_ref, a_got, b_ref, b_got, away, keep):
    cut = a_ref.shape[1]
    for out, first in ((away, 2), (keep, 0)):
        for at in range(2):
            out[at, :cut, :] = total_of(a_ref[first + at], a_got[first + at])
            out[at, cut:, :] = total_of(b_ref[first + at], b_got[first + at])


def add_third(a_keep, a_got, b_keep, b_got):
    half = like((2, a_keep.shape[1] + b_keep.shape[1], a_keep.shape[2]), BF16)
    return call(add_third_kernel, "add_third", (a_keep, a_got, b_keep, b_got), [half, half], 0.4)


def add_fourth_kernel(keep_ref, got_ref, away, keep):
    away[...] = total_of(keep_ref[1], got_ref[1])
    keep[...] = total_of(keep_ref[0], got_ref[0])


def add_fourth(keep, got):
    half = like(keep.shape[1:], BF16)
    return call(add_fourth_kernel, "add_fourth", (keep, got), [half, half], 0.3)


def add_last_kernel(keep_ref, got_ref, out):
    out[...] = total_of(keep_ref[...], got_ref[...])


def add_last(keep, got):
    return call(add_last_kernel, "add_last", (keep, got), [like(keep.shape, BF16)], 0.3)[0]


def unpack_kernel(weights, near_ref, far_ref, *refs):
    _, chip, core = own_place()
    count = len(weights)
    done_ref, *outs = refs[: count + 1]
    inner, sems = refs[count + 1 : -1], refs[-1]
    done_ref[...] = jnp.zeros_like(done_ref)
    copies = []
    for number, (weight, ref) in enumerate(zip(weights, inner)):
        for half, blocks in enumerate((near_ref, far_ref)):
            for offset in range(4):
                for start, inside, rows, lane in weight.pieces:
                    at = aligned((chip ^ offset) * weight.rows + inside, rows, 16)
                    block = blocks[offset, start : start + rows, :]
                    ref[at, aligned((core ^ half) * weight.half + lane, weight.lanes, 128)] = block.astype(F32)
        copy = pltpu.make_async_copy(ref, outs[number], sems.at[number])
        copy.start()
        copies.append(copy)
    for copy in copies:
        copy.wait()


def unpack(weights, near, far):
    shapes = [(weight.shape[0] // 4, weight.shape[1]) for weight in weights]
    return call(
        functools.partial(unpack_kernel, weights),
        "unpack_gradients",
        (near, far),
        [like((8, 128), F32)] + [pltpu.HBM(shape, F32) for shape in shapes],
        2.0,
        scratch=[pltpu.VMEM(shape, F32) for shape in shapes] + [pltpu.SemaphoreType.DMA((len(weights),))],
        outside_outs=len(weights),
    )[1:]


def solution(mesh):
    replicas, shards = mesh.shape["rep"], mesh.shape["fsdp"]
    rep_pairs = lambda bits: [(i, i ^ bits) for i in range(replicas)]
    shard_pairs = lambda bits: [(i, i ^ bits) for i in range(shards)]
    plane = {"c": 1, "x": 2, "y": 4, "d": 6}

    def swap(values, way):
        return lax.ppermute(values, "rep", rep_pairs(plane[way]))

    def swap_shard(values, bits):
        return lax.ppermute(values, "fsdp", shard_pairs(bits))

    def swap_halves(halves, order="xy"):
        first, last = halves[:2]
        return first, swap(first, order[0]), last, swap(last, order[1])

    def swap_sums(sums, order):
        a_away, a_keep, b_away, b_keep = sums
        return a_keep, swap(a_away, order[0]), b_keep, swap(b_away, order[1])

    def over_planes(own):
        bit = 8
        while bit < replicas:
            own = total_of(own, lax.ppermute(own, "rep", rep_pairs(bit)))
            bit *= 2
        return own

    def on_device(
        hidden,
        segments,
        selected,
        w_query,
        w_key,
        w_value,
        w_out,
        w_up,
        w_down,
        w_router,
        gain_attn,
        gain_mlp,
        cotangent,
    ):
        LAST.clear()
        CALLS.clear()
        width = hidden.shape[2]
        seqs = hidden.shape[0]
        lanes = width // 2
        shard = lax.axis_index("fsdp")

        small, tall = w_query.shape[0] // 4, w_down.shape[0] // 4
        wide = w_up.shape[1] // 2 // lanes
        first_weights = [Weight(i * small, small, 1, lanes) for i in range(4)]
        up_at = Weight(0, small, wide, lanes, "columns")
        down_at = Weight(0, tall, 1, lanes, "rows")
        first_rows, second_rows = 4 * small, small * wide
        halved = lambda rows: [
            [(0, rows // 2, (0, 1)), (rows // 2, rows, (0, 2))],
            [(0, rows // 2, (2, 3)), (rows // 2, rows, (1, 3))],
        ]
        vectors = jnp.concatenate([w_router, gain_attn, gain_mlp])
        padded = jnp.pad(vectors, (0, VECTOR_ROWS * lanes - vectors.shape[0])).reshape(VECTOR_ROWS, lanes)

        first_own = pack((w_query, w_key, w_value, w_out), first_weights)
        first_pieces = [swap_shard(first_own, bits) for bits in (1, 2, 3)]
        chosen, bias = choose(selected, segments)
        picked = pick_rows(hidden, chosen)
        second_own = pack((w_up,), (up_at,), (padded,))
        second_second = swap_shard(second_own, 2)
        third_own = pack((w_down,), (down_at,))
        first = swap_halves(join_three(first_pieces, first_rows // 2))
        second_pair, third_own = join_own(second_own, second_second, [third_own])
        second_pair = swap_shard(second_pair, 1)
        third_second = swap_shard(third_own, 2)
        *first, first_both = join_chips(*first)
        first = swap_halves(first, "yx")
        first_both_far = swap(first_both, "c")
        branch_grad = pick_rows(cotangent, chosen)
        *second, others = join_shards(second_pair, second_second, [second_rows // 2, second_rows])
        second = swap_halves(second)
        vec = whole_vectors(padded, others, width)
        third_pair = swap_shard(join_own(third_own, third_second), 1)
        first_other = join_rows(first[1], first[3])
        first_other_far = swap(first_other, "c")
        *second, second_both = join_chips(*second)
        second = swap_halves(second, "yx")
        second_both_far = swap(second_both, "c")
        cover()
        *qkv, full_out = assemble(
            (w_query, w_key, w_value, w_out),
            first_weights,
            halved(first_rows),
            (first_both, first_other, first_both_far, first_other_far),
        )
        normed, queries, keys, values = project(picked, vec, qkv)
        third = swap_halves(join_shards(third_pair, third_second, [tall // 2]))
        attended, probs, queries, keys, values, normed, *qkv = attend(bias, queries, keys, values, (normed, *qkv))
        attn_out, normed_mlp, grad_mlp, gating = project_out(attended, full_out, picked, branch_grad, vec)
        second_other = join_rows(second[1], second[3])
        second_other_far = swap(second_other, "c")
        *third, third_both = join_chips(*third)
        third = swap_halves(third, "yx")
        third_both_far = swap(third_both, "c")
        cover()
        up_near, up_far = assemble(
            (w_up,), (up_at,), halved(second_rows), (second_both, second_other, second_both_far, second_other_far)
        )
        act_far, slope_far, grad_far = project_up(normed_mlp, grad_mlp, up_far)
        act_near, slope_near, grad_near = project_up(normed_mlp, grad_mlp, up_near)

        down_keep, down_send = down_blocks(grad_near, grad_far)
        down_got = swap(down_send, "c")
        third_other = join_rows(third[1], third[3])
        third_other_far = swap(third_other, "c")
        down_near, down_far = assemble(
            (w_down,), (down_at,), halved(tall), (third_both, third_other, third_both_far, third_other_far)
        )
        far, near = (act_far, slope_far, up_far, down_far), (act_near, slope_near, up_near, down_near)

        def down_step(half, step, carried=()):
            act, slope, w_in, w_back = half
            *carried, blocks = down(step, up_at, act, slope, normed_mlp, grad_mlp, w_in, w_back, carried)
            return carried, blocks

        carried, up_send = down_step(far, 0)
        up_got = swap(up_send, "c")
        d_sums = swap_sums(add_first([(down_keep, down_got)], tall // 2), "xy")
        carried, up_keep = down_step(near, 0, carried)
        u_first = swap_sums(add_first([(up_keep, up_got)], small), "xy")
        carried, up_send = down_step(far, 1, carried)
        up_got = swap(up_send, "c")
        carried, up_keep = down_step(near, 1, carried)
        new_rows, grad_attn, grad_middle, grad_logit, gain_sums = branch(
            *carried, attn_out, picked, branch_grad, gating, vec
        )
        d_sums = swap_sums(add_second(d_sums), "yx")
        u_first = tuple(hold(*u_first))
        grad_attended, out_keep, out_send = out_back(first_weights[3], grad_attn, attended, full_out)
        out_got = swap(out_send, "c")
        cover()
        u_last = swap_sums(add_first([(up_keep, up_got), (out_keep, out_got)], 64), "xy")
        grads = []
        for seq in range(seqs):
            grads += attend_back(seq, grad_attended, queries, keys, values, probs)
            if seq == seqs - 2:
                d_away, d_keep = add_third(*d_sums)
                d_got = swap_shard(d_away, 1)
        first_keep, first_send = project_grads(first_weights[:3], normed, grads)
        first_got = swap(first_send, "c")
        d_away, d_keep = add_fourth(d_keep, d_got)
        d_got = swap_shard(d_away, 2)
        u_sums = swap_sums(add_second(u_first, u_last), "yx")
        cover()
        grad_rows, sums = project_back(
            grads, qkv, picked, grad_middle, branch_grad, grad_logit, vec, gain_sums
        )
        f_sums = swap_sums(add_first([(first_keep, first_got)], 80, (sums, swap(sums, "c"))), "xy")
        u_away, u_keep = add_third(*u_sums)
        u_got = swap_shard(u_away, 1)
        out_hidden = place_rows(range(seqs), selected, new_rows, hidden)
        f_sums = swap_sums(add_second(f_sums), "yx")
        d_own = over_planes(add_last(d_keep, d_got))
        d_got = swap(d_own, "x")
        u_away, u_keep = add_fourth(u_keep, u_got)
        u_got = swap_shard(u_away, 2)
        grad_hidden = place_rows(range(1), selected, grad_rows, cotangent)
        d_pair = join(d_own, d_got)
        d_got = swap(d_pair, "y")
        f_away, f_keep = add_third(*f_sums)
        f_got = swap_shard(f_away, 1)
        u_own = over_planes(add_last(u_keep, u_got))
        u_spread = [u_own] + [swap(u_own, way) for way in "xyd"]
        grad_hidden = place_rows(range(1, 2), selected, grad_rows, cotangent, grad_hidden)
        f_away, f_keep = add_fourth(f_keep, f_got)
        f_got = swap_shard(f_away, 2)
        grad_hidden = place_rows(range(2, seqs), selected, grad_rows, cotangent, grad_hidden)
        d_near = join(d_pair, d_got).reshape(4, *d_own.shape)
        d_far = swap(d_near, "c")
        u_near = join(*u_spread)
        u_far = swap(u_near, "c")
        f_own = over_planes(add_last(f_keep, f_got))
        f_spread = [f_own] + [swap(f_own, way) for way in "xyd"]
        cover()
        (grad_down,) = unpack((Weight(0, tall, 1, lanes),), d_near, d_far)
        up_pieces = [
            (0, 0, small, 0),
            (2 * small + 16, 0, small, lanes),
            (small, 0, small, 2 * lanes),
            (2 * small, 0, 16, 3 * lanes),
            (3 * small + 16, 16, small - 16, 3 * lanes),
        ]
        grad_up, grad_out = unpack(
            (Weight(0, small, wide, lanes, pieces=up_pieces), Weight(4 * small, small, 1, lanes)), u_near, u_far
        )
        f_near = join(*f_spread)
        grad_qkv = unpack(first_weights[:3], f_near, swap(f_near, "c"))
        sums = f_own[3 * small :].reshape(2, 8, lanes)[:, :3].swapaxes(0, 1).reshape(3, width).astype(F32)
        sums = lax.dynamic_slice(sums, (0, shard * w_router.shape[0]), (3, w_router.shape[0]))
        return (out_hidden, grad_hidden, *grad_qkv, grad_out, grad_up, grad_down, sums[0], sums[1], sums[2])

    placed = (
        P(("rep", "fsdp"), None, None),
        P(("rep", "fsdp"), None),
        P(("rep", "fsdp"), None),
        P("fsdp", None),
        P("fsdp", None),
        P("fsdp", None),
        P("fsdp", None),
        P("fsdp", None),
        P("fsdp", None),
        P("fsdp"),
        P("fsdp"),
        P("fsdp"),
        P(("rep", "fsdp"), None, None),
    )
    return jax.shard_map(
        on_device,
        mesh=mesh,
        in_specs=placed,
        out_specs=(
            P(("rep", "fsdp"), None, None),
            P(("rep", "fsdp"), None, None),
            P("fsdp", None),
            P("fsdp", None),
            P("fsdp", None),
            P("fsdp", None),
            P("fsdp", None),
            P("fsdp", None),
            P("fsdp"),
            P("fsdp"),
            P("fsdp"),
        ),
        check_vma=False,
    )
```

```python
import functools

import jax
import jax.numpy as jnp
from jax import lax
from jax.experimental import pallas as pl
from jax.experimental.pallas import tpu as pltpu
from jax.sharding import PartitionSpec as P

HEADS = 12
HEAD_DIM = 64
PAIR = 2 * HEAD_DIM
EPSILON = 1e-06
F32 = jnp.float32
BF16 = jnp.bfloat16
TILE = 256
LANES = 128
VECTOR_ROWS = 16
VMEM_BYTES = 9 * 1024 * 1024
SMALL_BYTES = 6 * 1024 * 1024
STREAM_BYTES = 16 * 1024 * 1024


def dot(left, right):
    return jnp.dot(left, right, preferred_element_type=F32)


def dot_nt(left, right):
    return lax.dot_general(left, right, (((1,), (1,)), ((), ())), preferred_element_type=F32)


def dot_tn(left, right):
    return lax.dot_general(left, right, (((0,), (0,)), ((), ())), preferred_element_type=F32)


def swap_bits(place):
    return ((place & 1) << 1) | (place >> 1)


def own_place():
    member = lax.axis_index("rep") & 7
    return lax.axis_index("fsdp"), member >> 1, member & 1


def micros(time):
    return pl.CostEstimate(flops=int(time * 1.1e9), bytes_accessed=0, transcendentals=0)


BESIDE = {
    "pack_blocks": (0.1, 0.3, 0.3),
    "choose": (0.6,),
    "pick_rows": (1.0, 0.05),
    "join_three": (1.7,),
    "join_own": (2.3, 4.3),
    "join_chips": (1.2, 0.1, 0.1),
    "cover": (9.5, 9.5, 11.0, 17.0, 9.5),
    "project": (1.0,),
    "attend": (2.4,),
    "project_out": (0.8,),
    "project_up": (2.0, 2.0),
    "down_and_back": (24.0, 12.0, 2.5, 1.0),
    "attend_back": (2.2, 0.5, 2.3),
    "project_gradients": (0.5,),
    "project_back": (1.0,),
    "place_rows": (5.2, 2.2, 2.6, 0.1),
    "add_last": (0.1, 0.1, 1.0),
    "unpack_gradients": (1.3, 2.0, 0.1),
}
CALLS = {}
LARGE = {"down_and_back", "project_back", "attend"}


def beside(name):
    number = CALLS.get(name, 0)
    CALLS[name] = number + 1
    times = BESIDE.get(name, (0.1,))
    return micros(times[min(number, len(times) - 1)])


def like(shape, dtype):
    return jax.ShapeDtypeStruct(shape, dtype)


def params(limit=VMEM_BYTES):
    return pltpu.CompilerParams(vmem_limit_bytes=limit)


ANYWHERE = pl.BlockSpec(memory_space=pl.ANY)
INSIDE = pl.BlockSpec(memory_space=pltpu.VMEM)
OUTSIDE = pl.BlockSpec(memory_space=pltpu.HBM)
LAST = []


def ordered(kernel, ins, in_specs, aliases=(), **options):
    before = tuple(LAST)

    def body(*refs):
        kernel(*refs[len(before) :])

    ins = [pltpu.with_memory_space_constraint(a, pltpu.HBM) if s is OUTSIDE else a for a, s in zip(ins, in_specs)]
    outs = pl.pallas_call(
        body,
        in_specs=[ANYWHERE] * len(before) + in_specs,
        input_output_aliases={len(before) + at: out for at, out in aliases},
        **options,
    )(*before, *ins)
    LAST[:] = [min(outs, key=lambda out: out.size)]
    return outs


def call(kernel, name, ins, outs, estimate, scratch=(), outside=0, aliases=(), outside_outs=0):
    return ordered(
        kernel,
        ins,
        [OUTSIDE] * outside + [INSIDE] * (len(ins) - outside),
        aliases,
        out_specs=[INSIDE] * (len(outs) - outside_outs) + [OUTSIDE] * outside_outs,
        out_shape=list(outs),
        scratch_shapes=list(scratch),
        compiler_params=params(VMEM_BYTES if name in LARGE else SMALL_BYTES),
        cost_estimate=beside(name),
        name=name,
    )


def choose_kernel(sel_from, seg_from, chosen_ref, bias_ref, sel_ref, seg_ref, sems):
    copies = [
        pltpu.make_async_copy(sel_from, sel_ref, sems.at[0]),
        pltpu.make_async_copy(seg_from, seg_ref, sems.at[1]),
    ]
    for copy in copies:
        copy.start()
    for copy in copies:
        copy.wait()
    seqs, keep, length = chosen_ref.shape
    square = (keep, keep)
    diagonal = lax.broadcasted_iota(jnp.int32, square, 0) == lax.broadcasted_iota(jnp.int32, square, 1)
    places = lax.broadcasted_iota(jnp.int32, (keep, length), 1)
    for seq in range(seqs):
        row = sel_ref[seq : seq + 1, :].astype(F32)
        column = jnp.sum(jnp.where(diagonal, row, 0.0), axis=1, keepdims=True)
        chosen = jnp.where(column.astype(jnp.int32) == places, 1.0, 0.0).astype(BF16)
        chosen_ref[seq] = chosen
        documents = jnp.broadcast_to(seg_ref[seq : seq + 1, :].astype(F32), (8, length)).astype(BF16)
        of_column = dot_nt(chosen, documents)[:, :1]
        of_row = jnp.sum(jnp.where(diagonal, of_column, 0.0), axis=0, keepdims=True)
        allowed = (row >= column) & (of_column == of_row)
        bias_ref[seq] = jnp.where(allowed, 0.0, -1e30).astype(BF16)


def choose(selected, segments):
    seqs, keep = selected.shape
    length = segments.shape[1]
    return ordered(
        choose_kernel,
        (selected, segments),
        [OUTSIDE] * 2,
        out_specs=[INSIDE] * 2,
        out_shape=[like((seqs, keep, length), BF16), like((seqs, keep, keep), BF16)],
        scratch_shapes=[
            pltpu.VMEM(selected.shape, selected.dtype),
            pltpu.VMEM(segments.shape, segments.dtype),
            pltpu.SemaphoreType.DMA((2,)),
        ],
        compiler_params=params(),
        cost_estimate=beside("choose"),
        name="choose_rows",
    )


def pick_kernel(rows_ref, chosen_ref, picked_ref, buffer, sems):
    seqs, keep, _ = chosen_ref.shape
    copies = [pltpu.make_async_copy(rows_ref.at[seq], buffer.at[seq], sems.at[seq]) for seq in range(seqs)]
    for copy in copies:
        copy.start()
    for seq, copy in enumerate(copies):
        copy.wait()
        picked_ref[seq * keep : (seq + 1) * keep, :] = dot(chosen_ref[seq], buffer[seq]).astype(BF16)


def pick_rows(rows, chosen):
    seqs, _, width = rows.shape
    return ordered(
        pick_kernel,
        (rows, chosen),
        [OUTSIDE, INSIDE],
        out_specs=[INSIDE],
        out_shape=[like((seqs * chosen.shape[1], width), BF16)],
        scratch_shapes=[pltpu.VMEM(rows.shape, BF16), pltpu.SemaphoreType.DMA((seqs,))],
        compiler_params=params(STREAM_BYTES),
        cost_estimate=beside("pick_rows"),
        name="pick_rows",
    )[0]


def place_kernel(seqs, sel_ref, new_ref, base_ref, *refs):
    out_ref, done_ref, buffer, wide_ref, in_sems, out_sems = refs[-6:]
    done_ref[...] = jnp.zeros_like(done_ref)
    length, width = base_ref.shape[1:]
    keep = sel_ref.shape[1]
    chunks = [(number, seq, part) for number, seq in enumerate(seqs) for part in tiles(length, length // 2)]
    copies = [
        pltpu.make_async_copy(base_ref.at[seq, part, :], buffer.at[number, part, :], in_sems.at[at])
        for at, (number, seq, part) in enumerate(chunks)
    ]
    for copy in copies:
        copy.start()
    for number, seq in enumerate(seqs):
        wide_ref[number, :, :width] = new_ref[seq * keep : (seq + 1) * keep, :]
        wide_ref[number, :, width:] = jnp.ones((keep, LANES), BF16)
    results = []
    for at, (number, seq, part) in enumerate(chunks):
        places = lax.broadcasted_iota(jnp.int32, (part.stop - part.start, keep), 0) + part.start
        hits = jnp.where(places == sel_ref[seq : seq + 1, :], 1.0, 0.0).astype(BF16)
        copies[at].wait()
        for row in range(0, part.stop - part.start, TILE):
            placed = dot(hits[row : row + TILE, :], wide_ref[number])
            new = placed[:, width:] > 0.0
            rows = slice(part.start + row, part.start + row + TILE)
            for lane in range(0, width, LANES):
                lanes = slice(lane, lane + LANES)
                base = buffer[number, rows, lanes].astype(F32)
                buffer[number, rows, lanes] = jnp.where(new, placed[:, lanes], base).astype(BF16)
        back = pltpu.make_async_copy(buffer.at[number, part, :], out_ref.at[seq, part, :], out_sems.at[at])
        back.start()
        results.append(back)
    for back in results:
        back.wait()


def place_rows(seqs, selected, new_rows, base, placed=None):
    _, length, width = base.shape
    earlier = () if placed is None else (placed,)
    return ordered(
        functools.partial(place_kernel, tuple(seqs)),
        (selected, new_rows, base, *earlier),
        [INSIDE, INSIDE, OUTSIDE] + [OUTSIDE] * len(earlier),
        aliases=[(3, 0)] if earlier else [],
        out_specs=[OUTSIDE, INSIDE],
        out_shape=[pltpu.HBM(base.shape, BF16), like((8, 128), F32)],
        scratch_shapes=[
            pltpu.VMEM((len(seqs), length, width), BF16),
            pltpu.VMEM((len(seqs), selected.shape[1], width + LANES), BF16),
        ]
        + [pltpu.SemaphoreType.DMA((2 * len(seqs),))] * 2,
        compiler_params=params(STREAM_BYTES),
        cost_estimate=beside("place_rows"),
        name="place_rows",
    )[0]


class Weight:
    def __init__(self, start, rows, columns, lanes, split=None, pieces=None):
        self.start, self.rows, self.columns, self.lanes, self.split = start, rows, columns, lanes, split
        self.parts = 1 if split is None else 2
        self.half = columns * lanes
        self.shape = (16 * rows, 2 * self.half)
        self.pieces = pieces or [(at, 0, rows, lane) for at, lane in self.slots()]

    def slots(self):
        return [(self.start + c * self.rows, c * self.lanes) for c in range(self.columns)]


def aligned(value, size, multiple):
    return pl.ds(pl.multiple_of(value, multiple), size)


def pack_kernel(weights, *refs):
    _, chip, core = own_place()
    *ins, out_ref, sem = refs
    for own, weight in zip(ins, weights):
        for start, lane in weight.slots():
            pltpu.make_async_copy(
                own.at[
                    aligned(chip * weight.rows, weight.rows, 16), aligned(core * weight.half + lane, weight.lanes, 128)
                ],
                out_ref.at[start : start + weight.rows, :],
                sem,
            ).start()
    for extra in ins[len(weights) :]:
        pltpu.make_async_copy(extra, out_ref.at[out_ref.shape[0] - extra.shape[0] :, :], sem).start()
    pltpu.make_async_copy(out_ref, out_ref, sem).wait()


def pack(owns, weights, extra=()):
    rows = sum(w.rows * w.columns for w in weights) + sum(e.shape[0] for e in extra)
    return call(
        functools.partial(pack_kernel, weights),
        "pack_blocks",
        (*owns, *extra),
        [like((rows, weights[0].lanes), BF16)],
        0.5,
        scratch=[pltpu.SemaphoreType.DMA],
        outside=len(owns) + len(extra),
    )[0]


def join_own_kernel(own_ref, second_ref, *refs):
    *held, out_ref, out_held = refs if len(refs) > 1 else (*refs, None)
    for ref in held:
        out_held[...] = ref[...]
    out_ref[0] = own_ref[...]
    out_ref[1] = second_ref[...]


def join_own(own, second, held=()):
    outs = [like((2, *own.shape), BF16)] + [like(a.shape, a.dtype) for a in held]
    outs = call(join_own_kernel, "join_own", (own, second, *held), outs, 0.2)
    return outs if held else outs[0]


def join_shards_kernel(count, pair_ref, second_ref, *refs):
    held, outs = refs[:count], refs[count:]
    for ref, out in zip(held, outs[len(outs) - count :]):
        out[...] = ref[...]
    start = 0
    for out in outs[: len(outs) - count]:
        rows = slice(start, start + out.shape[1])
        start = rows.stop
        out[0] = pair_ref[0, rows, :]
        out[1] = second_ref[rows, :]
        out[2] = pair_ref[1, rows, :]


def join_shards(pair, second, cuts, held=()):
    _, rows, lanes = pair.shape
    edges = [0, *cuts, rows]
    outs = [like((3, high - low, lanes), BF16) for low, high in zip(edges, edges[1:])]
    outs += [like(a.shape, a.dtype) for a in held]
    return call(functools.partial(join_shards_kernel, len(held)), "join_shards", (pair, second, *held), outs, 0.3)


def hold_kernel(*refs):
    count = len(refs) // 2
    for ref, out in zip(refs[:count], refs[count:]):
        out[...] = ref[...]


def hold(*arrays):
    return call(hold_kernel, "hold", arrays, [like(a.shape, a.dtype) for a in arrays], 0.2)


def cover_kernel(out_ref):
    out_ref[...] = jnp.zeros_like(out_ref)


def cover():
    call(cover_kernel, "cover", (), [like((8, 128), F32)], 0.1)


def join_three_kernel(first_ref, second_ref, third_ref, *outs):
    start = 0
    for out in outs:
        rows = slice(start, start + out.shape[1])
        start = rows.stop
        for at, ref in enumerate((first_ref, second_ref, third_ref)):
            out[at] = ref[rows, :]


def join_three(pieces, cut):
    rows, lanes = pieces[0].shape
    outs = [like((3, cut, lanes), BF16), like((3, rows - cut, lanes), BF16)]
    return call(join_three_kernel, "join_three", pieces, outs, 0.3)


def join_chips_kernel(first_ref, first_got, last_ref, last_got, first_out, last_out, both_out):
    cut = first_ref.shape[1]
    for at, (first, last) in enumerate(((first_ref, last_ref), (first_got, last_got))):
        first_out[at] = first[...]
        last_out[at] = last[...]
        both_out[at, :, :cut, :] = first[...]
        both_out[at, :, cut:, :] = last[...]


def join_chips(first, first_got, last, last_got):
    count, cut, lanes = first.shape
    rows = last.shape[1]
    shapes = [(2, count, cut, lanes), (2, count, rows, lanes), (2, count, cut + rows, lanes)]
    return call(
        join_chips_kernel, "join_chips", (first, first_got, last, last_got), [like(s, BF16) for s in shapes], 0.5
    )


def vectors_kernel(own_ref, others_ref, out_ref):
    shard, _, _ = own_place()
    lanes = out_ref.shape[1] // 4
    pieces = []
    for ref in (own_ref, *[others_ref.at[other] for other in range(3)]):
        rows = ref[...].astype(F32)
        pieces.append(jnp.concatenate([rows[:1, :lanes], rows[:1, lanes:], rows[1:2, :lanes]], axis=0))
    out_ref[...] = jnp.zeros_like(out_ref)
    for place in range(4):
        value = pieces[3]
        for other in range(3):
            value = jnp.where((shard ^ place) == other, pieces[other], value)
        out_ref[:3, place * lanes : (place + 1) * lanes] = value


def whole_vectors(own, others, width):
    return call(vectors_kernel, "vectors", (own, others), [like((8, width), F32)], 0.2)[0]


def join_rows_kernel(*refs):
    *ins, out = refs
    start = 0
    for ref in ins:
        rows = ref.shape[-2]
        out[..., start : start + rows, :] = ref[...]
        start += rows


def join_rows(*arrays):
    shape = list(arrays[0].shape)
    shape[-2] = sum(a.shape[-2] for a in arrays)
    return call(join_rows_kernel, "join_rows", arrays, [like(shape, BF16)], 0.3)[0]


def join_kernel(*refs):
    *ins, out = refs
    for at, ref in enumerate(ins):
        out[at] = ref[...]


def join(*arrays):
    return call(join_kernel, "join", arrays, [like((len(arrays), *arrays[0].shape), BF16)], 0.2)[0]


def join_turned_kernel(pair_ref, got_ref, out):
    for y_bit in range(2):
        out[2 * y_bit] = pair_ref[y_bit]
        out[2 * y_bit + 1] = got_ref[y_bit]


def join_turned(pair, got):
    return call(join_turned_kernel, "join_turned", (pair, got), [like((4, *pair.shape[1:]), BF16)], 0.2)[0]


def assemble_kernel(weights, layout, *refs):
    shard, chip, core = own_place()
    count = len(layout)
    owns, refs = refs[: len(weights)], refs[len(weights) :]
    *refs, sems = refs
    pieces, outs = (refs[:count], refs[count : 2 * count]), list(refs[2 * count :])
    for number, (weight, own) in enumerate(zip(weights, owns)):
        shard_rows = own.shape[0]
        sem = sems.at[number]
        targets = [outs.pop(0) for _ in range(weight.parts)]

        def fill(place_of):
            copies = []
            if weight.split == "columns":
                for half in range(2):
                    out, row, _ = place_of(0, half)
                    lane = aligned((core ^ half) * weight.half, weight.half, 128)
                    copies.append(pltpu.make_async_copy(own.at[:, lane], out.at[row, :], sem.at[half]))
            else:
                out, row, _ = place_of(0, 0)
                copies.append(pltpu.make_async_copy(own, out.at[row, :], sem.at[0]))
            for copy in copies:
                copy.start()
            for half in range(2):
                for number, ranges in enumerate(layout):
                    ref = pieces[half][number]
                    for start, lane in weight.slots():
                        for low, high, chips in ranges:
                            lo, hi = max(start, low), min(start + weight.rows, high)
                            if lo >= hi:
                                continue
                            for at, offset in enumerate(chips):
                                for other in range(3):
                                    inner = (chip ^ offset) * weight.rows + (lo - start)
                                    out, row, lanes = place_of(other + 1, half, inner, hi - lo, lane, weight.lanes)
                                    out[row, lanes] = ref[at, other, lo:hi, :]
            for copy in copies:
                copy.wait()

        if weight.split == "columns":

            def place_of(other, half, inner=0, rows=shard_rows, lane=0, lanes=weight.half):
                return targets[half], aligned((shard ^ other) * shard_rows + inner, rows, 16), slice(lane, lane + lanes)

            fill(place_of)
        elif weight.split == "rows":
            for near in range(2):

                def place_of(other, half, inner=0, rows=shard_rows, lane=0, lanes=0):
                    row = ((shard ^ other) & 1) * shard_rows + inner
                    at = aligned((core ^ half) * weight.half + lane, lanes, 128) if lanes else slice(None)
                    return targets[near ^ (other >> 1)], aligned(row, rows, 16), at

                pl.when(((shard >> 1) ^ core) == near)(functools.partial(fill, place_of))
        else:

            def place_of(other, half, inner=0, rows=shard_rows, lane=0, lanes=0):
                at = aligned((core ^ half) * weight.half + lane, lanes, 128) if lanes else slice(None)
                return targets[0], aligned((shard ^ other) * shard_rows + inner, rows, 16), at

            fill(place_of)


def assemble(owns, weights, layout, pieces):
    outs = []
    for weight in weights:
        rows, columns = weight.shape
        if weight.split == "columns":
            outs += [like((rows, columns // 2), BF16)] * 2
        elif weight.split == "rows":
            outs += [like((rows // 2, columns), BF16)] * 2
        else:
            outs.append(like((rows, columns), BF16))
    return call(
        functools.partial(assemble_kernel, weights, layout),
        "assemble_weights",
        (*owns, *pieces),
        outs,
        0.3 * sum(w.columns * w.rows for w in weights) / 48,
        scratch=[pltpu.SemaphoreType.DMA((len(weights), 2))],
    )


def write_blocks(grad_ref, keep_ref, send_ref, start, rows):
    shard, chip, core = own_place()
    lanes = keep_ref.shape[-1]
    for x_bit in range(2):
        for y_bit in range(2):
            for place in range(4):
                row = (shard ^ swap_bits(place)) * (4 * rows) + (chip ^ (2 * y_bit + x_bit)) * rows
                for half, out in ((0, keep_ref), (1, send_ref)):
                    out[x_bit, y_bit, place, start : start + rows, :] = grad_ref[
                        aligned(row, rows, 16), aligned((core ^ half) * lanes, lanes, 128)
                    ].astype(BF16)


def tiles(size, step=TILE):
    return [slice(i, i + step) for i in range(0, size, step)]


def inverse_rms(values):
    return lax.rsqrt(jnp.mean(values * values, axis=-1, keepdims=True) + EPSILON)


def project_kernel(picked_ref, vec_ref, wq, wk, wv, normed_ref, q_ref, k_ref, v_ref):
    for at in tiles(picked_ref.shape[0]):
        values = picked_ref[at, :].astype(F32)
        normed_ref[at, :] = (values * inverse_rms(values) * vec_ref[1:2, :]).astype(BF16)
    q_ref[...] = dot(normed_ref[...], wq[...]).astype(BF16) * 0.125
    k_ref[...] = dot(normed_ref[...], wk[...]).astype(BF16)
    v_ref[...] = dot(normed_ref[...], wv[...]).astype(BF16)


def project(picked, vectors, weights):
    flat = like(picked.shape, BF16)
    return call(project_kernel, "project", (picked, vectors, *weights), [flat] * 4, 4.5)


def low_half_lanes(rows):
    return lax.broadcasted_iota(jnp.int32, (rows, PAIR), 1) < HEAD_DIM


def split_heads(low_half, values):
    return jnp.concatenate([jnp.where(low_half, values, 0), jnp.where(low_half, 0, values)], axis=0)


def join_heads(low_half, values):
    rows = low_half.shape[0]
    return jnp.where(low_half, values[:rows], values[rows:]).astype(BF16)


def attend_kernel(count, bias_ref, q_ref, k_ref, v_ref, *refs):
    later, (att_ref, probs_out, *outs), (probs_ref, sems) = refs[:count], refs[count:-2], refs[-2:]
    seqs, keep, _ = bias_ref.shape
    low_half = low_half_lanes(keep)
    copies = [
        pltpu.make_async_copy(ref, out, sems.at[at]) for at, (ref, out) in enumerate(zip((q_ref, k_ref, v_ref, *later), outs))
    ]
    for copy in copies:
        copy.start()
    for seq in range(seqs):
        bias = bias_ref[seq].astype(F32)
        rows = slice(seq * keep, (seq + 1) * keep)
        for pair in range(HEADS // 2):
            lanes = slice(pair * PAIR, (pair + 1) * PAIR)
            queries, keys, values = q_ref[rows, lanes], k_ref[rows, lanes], v_ref[rows, lanes]
            scores = dot_nt(split_heads(low_half, keys), queries)
            both = []
            for half in range(2):
                own = scores[half * keep : (half + 1) * keep] + bias
                exponent = jnp.exp(own - jnp.max(own, axis=0, keepdims=True))
                both.append((exponent * (1.0 / jnp.sum(exponent, axis=0, keepdims=True))).astype(BF16))
                probs_ref[seq, 2 * pair + half] = both[half]
            att_ref[rows, lanes] = join_heads(low_half, dot_tn(jnp.concatenate(both, axis=1), values))
        copy = pltpu.make_async_copy(probs_ref.at[seq], probs_out.at[seq], sems.at[len(outs) + seq])
        copy.start()
        copies.append(copy)
    for copy in copies:
        copy.wait()


def attend(bias, queries, keys, values, later):
    seqs, keep, _ = bias.shape
    shape = (seqs, HEADS, keep, keep)
    kept = (queries, keys, values, *later)
    return call(
        functools.partial(attend_kernel, len(later)),
        "attend",
        (bias, *kept),
        [like(queries.shape, BF16), pltpu.HBM(shape, BF16)] + [pltpu.HBM(a.shape, a.dtype) for a in kept],
        6.5,
        scratch=[pltpu.VMEM(shape, BF16), pltpu.SemaphoreType.DMA((len(kept) + seqs,))],
        outside_outs=1 + len(kept),
    )


def out_kernel(att_ref, wo_ref, picked_ref, gbr_ref, vec_ref, attn_ref, nm_ref, gmlp_ref, gating_ref):
    attn_ref[...] = dot(att_ref[...], wo_ref[...])
    for at in tiles(picked_ref.shape[0]):
        values = picked_ref[at, :].astype(F32)
        middle = values + attn_ref[at, :]
        nm_ref[at, :] = (middle * inverse_rms(middle) * vec_ref[2:3, :]).astype(BF16)
        logit = jnp.sum(values * vec_ref[0:1, :], axis=-1, keepdims=True)
        gating = 1.0 / (1.0 + jnp.exp(-logit))
        gating_ref[at, :] = gating
        gmlp_ref[at, :] = (gating * gbr_ref[at, :].astype(F32)).astype(BF16)


def project_out(attended, w_out, picked, branch_grad, vectors):
    flat = like(picked.shape, BF16)
    return call(
        out_kernel,
        "project_out",
        (attended, w_out, picked, branch_grad, vectors),
        [like(picked.shape, F32), flat, flat, like((picked.shape[0], 1), F32)],
        2.0,
    )


def gelu_parts(values):
    cdf = 0.5 * (1.0 + lax.erf(values * 0.7071067811865476))
    return values * cdf, cdf + values * (jnp.exp(-0.5 * values * values) * 0.3989422804014327)


def up_kernel(nm_ref, gmlp_ref, wu_ref, act_ref, slope_ref, grad_ref):
    tokens = nm_ref.shape[0]
    for columns in tiles(wu_ref.shape[1], wu_ref.shape[1] // 2):
        for at in tiles(tokens, 128):
            activated, slope = gelu_parts(dot(nm_ref[at, :], wu_ref[:, columns]))
            act_ref[at, columns] = activated.astype(BF16)
            slope_ref[at, columns] = slope.astype(BF16)
        grad_ref[columns, :] = dot_tn(act_ref[:, columns], gmlp_ref[...]).astype(BF16)


def project_up(normed, grad_mlp, w_up):
    tokens, width = normed.shape
    units = w_up.shape[1]
    wide = like((tokens, units), BF16)
    return call(
        up_kernel,
        "project_up",
        (normed, grad_mlp, w_up),
        [wide, wide, like((units, width), BF16)],
        6.0,
    )


def down_blocks_kernel(near_ref, far_ref, keep_ref, send_ref):
    shard, chip, core = own_place()
    rows, lanes = keep_ref.shape[-2:]
    shard_rows = 4 * rows

    def fill(near):
        for place in range(4):
            other = swap_bits(place)
            ref = (near_ref, far_ref)[near ^ (other >> 1)]
            for x_bit in range(2):
                for y_bit in range(2):
                    row = ((shard ^ other) & 1) * shard_rows + (chip ^ (2 * y_bit + x_bit)) * rows
                    for half, out in ((0, keep_ref), (1, send_ref)):
                        out[x_bit, y_bit, place] = ref[
                            aligned(row, rows, 16), aligned((core ^ half) * lanes, lanes, 128)
                        ]

    for near in range(2):
        pl.when(((shard >> 1) ^ core) == near)(functools.partial(fill, near))


def down_blocks(near, far):
    units, width = near.shape
    blocks = like((2, 2, 4, units // 8, width // 2), BF16)
    return call(down_blocks_kernel, "down_blocks", (near, far), [blocks, blocks], 0.7)


def norm_back(grad_normed, values, inverse, gain):
    scaled = grad_normed * gain
    grad_gain = jnp.sum(grad_normed * values * inverse, axis=0, keepdims=True)
    grad_values = inverse * scaled - values * (inverse * inverse * inverse) * jnp.mean(
        scaled * values, axis=-1, keepdims=True
    )
    return grad_values, grad_gain


def down_kernel(step, weight, act_ref, slope_ref, nm_ref, gmlp_ref, wu_ref, wd_ref, *refs):
    *starts, mlp_ref, gnm_ref, out_ref, grad_ref = refs
    shard, chip, core = own_place()
    block = wd_ref.shape[0] // 2
    rows, lanes = weight.rows, weight.lanes
    at = slice(step * block, (step + 1) * block)
    down = wd_ref[at, :]
    mlp = dot(act_ref[:, at], down)
    grad_before = (dot_nt(gmlp_ref[...], down) * slope_ref[:, at].astype(F32)).astype(BF16)
    grad_ref[...] = dot_tn(nm_ref[...], grad_before)
    grad_nm = dot_nt(grad_before, wu_ref[:, at])
    mlp_ref[...] = starts[0][...] + mlp if starts else mlp
    gnm_ref[...] = starts[1][...] + grad_nm if starts else grad_nm
    for x_bit in range(2):
        for y_bit in range(2):
            for place in range(4):
                row = (shard ^ swap_bits(place)) * (4 * rows) + (chip ^ (2 * y_bit + x_bit)) * rows
                for part in range(block // lanes):
                    out_ref[x_bit, y_bit, place, part * rows : (part + 1) * rows, :] = grad_ref[
                        aligned(row, rows, 16), part * lanes : (part + 1) * lanes
                    ].astype(BF16)


def down(step, weight, activated, slope, normed, grad_mlp, w_up, w_down, starts=()):
    tokens, width = normed.shape
    total = like((tokens, width), F32)
    return call(
        functools.partial(down_kernel, step, weight),
        "down_and_back",
        (activated, slope, normed, grad_mlp, w_up, w_down, *starts),
        [total, total, like((2, 2, 4, weight.rows * weight.columns // 2, weight.lanes), BF16)],
        4.2,
        scratch=[pltpu.VMEM((width, w_up.shape[1] // 2), F32)],
        aliases=[(6, 0), (7, 1)] if starts else [],
    )


def branch_kernel(
    mlp_ref, gnm_ref, attn_ref, picked_ref, gbr_ref, gating_ref, vec_ref, new_ref, gattn_ref, gmid_ref, glogit_ref, sum_ref
):
    total = jnp.zeros((1, vec_ref.shape[1]), F32)
    for at in tiles(picked_ref.shape[0]):
        attention = attn_ref[at, :]
        values = picked_ref[at, :].astype(F32)
        gating = gating_ref[at, :]
        branch_grad = gbr_ref[at, :].astype(F32)
        delta = attention + mlp_ref[at, :]
        new_ref[at, :] = (values + gating * delta).astype(BF16)
        grad_gating = jnp.sum(branch_grad * delta, axis=-1, keepdims=True)
        glogit_ref[at, :] = grad_gating * gating * (1.0 - gating)
        middle = values + attention
        grad_middle, grad_gain = norm_back(gnm_ref[at, :], middle, inverse_rms(middle), vec_ref[2:3, :])
        gmid_ref[at, :] = grad_middle
        gattn_ref[at, :] = (gating * branch_grad + grad_middle).astype(BF16)
        total = total + grad_gain
    sum_ref[...] = jnp.broadcast_to(total, sum_ref.shape)


def branch(mlp, grad_nm, attn_out, picked, branch_grad, gating, vectors):
    tokens, width = picked.shape
    return call(
        branch_kernel,
        "branch_and_norm_back",
        (mlp, grad_nm, attn_out, picked, branch_grad, gating, vectors),
        [
            like((tokens, width), BF16),
            like((tokens, width), BF16),
            like((tokens, width), F32),
            like((tokens, 1), F32),
            like((8, width), F32),
        ],
        2.0,
    )


def out_back_kernel(weight, gattn_ref, att_ref, wo_ref, gatt_ref, keep_ref, send_ref, grad_ref):
    grad_ref[...] = dot_tn(att_ref[...], gattn_ref[...])
    gatt_ref[...] = dot_nt(gattn_ref[...], wo_ref[...]).astype(BF16)
    write_blocks(grad_ref, keep_ref, send_ref, 0, weight.rows)


def out_back(weight, grad_attn, attended, w_out):
    blocks = like((2, 2, 4, weight.rows, weight.lanes), BF16)
    return call(
        functools.partial(out_back_kernel, weight),
        "project_out_back",
        (grad_attn, attended, w_out),
        [like(grad_attn.shape, BF16), blocks, blocks],
        2.5,
        scratch=[pltpu.VMEM(weight.shape, F32)],
    )


def attend_back_kernel(seq, gatt_ref, q_ref, k_ref, v_ref, probs_ref, gq_ref, gk_ref, gv_ref):
    keep = probs_ref.shape[2]
    low_half = low_half_lanes(keep)
    rows = slice(seq * keep, (seq + 1) * keep)
    for pair in range(HEADS // 2):
        lanes = slice(pair * PAIR, (pair + 1) * PAIR)
        queries, keys, values = q_ref[rows, lanes], k_ref[rows, lanes], v_ref[rows, lanes]
        grad_att = gatt_ref[rows, lanes]
        grad_probs = dot_nt(split_heads(low_half, values), grad_att)
        probs = [probs_ref[seq, 2 * pair + half] for half in range(2)]
        scores = []
        for half in range(2):
            wide = probs[half].astype(F32)
            weighted = wide * grad_probs[half * keep : (half + 1) * keep]
            scores.append((weighted - wide * jnp.sum(weighted, axis=0, keepdims=True)).astype(BF16))
        gq_ref[:, lanes] = join_heads(low_half, dot_tn(jnp.concatenate(scores, axis=1), keys) * 0.125)
        gk_ref[:, lanes] = join_heads(low_half, dot(jnp.concatenate(scores, axis=0), queries))
        gv_ref[:, lanes] = join_heads(low_half, dot(jnp.concatenate(probs, axis=0), grad_att))


def attend_back(seq, grad_attended, queries, keys, values, probs):
    rows = like((probs.shape[2], queries.shape[1]), BF16)
    return call(
        functools.partial(attend_back_kernel, seq),
        "attend_back",
        (grad_attended, queries, keys, values, probs),
        [rows] * 3,
        4.0,
    )


def project_grads_kernel(weights, normed_ref, *refs):
    *grads, keep_ref, send_ref, grad_ref = refs
    for i, weight in enumerate(weights):
        grad_ref[...] = dot_tn(normed_ref[...], rows_of(grads, i))
        write_blocks(grad_ref, keep_ref, send_ref, weight.start, weight.rows)


def rows_of(grads, i):
    return jnp.concatenate([ref[...] for ref in grads[i::3]], axis=0)


def project_grads(weights, normed, grads):
    blocks = like((2, 2, 4, sum(w.rows for w in weights), weights[0].lanes), BF16)
    return call(
        functools.partial(project_grads_kernel, weights),
        "project_gradients",
        (normed, *grads),
        [blocks, blocks],
        4.0,
        scratch=[pltpu.VMEM(weights[0].shape, F32)],
    )


def project_back_kernel(count, *refs):
    grads, refs = refs[:count], refs[count:]
    wq, wk, wv, picked_ref, gmid_ref, gbr_ref, glogit_ref, vec_ref, middle_ref, new_ref, sum_ref, gn_ref = refs
    gn_ref[...] = sum(dot_nt(rows_of(grads, i), w[...]) for i, w in enumerate((wq, wk, wv)))
    router = jnp.zeros((1, vec_ref.shape[1]), F32)
    total = router
    for at in tiles(picked_ref.shape[0]):
        values = picked_ref[at, :].astype(F32)
        grad_picked, grad_gain = norm_back(gn_ref[at, :], values, inverse_rms(values), vec_ref[1:2, :])
        grad_logit = glogit_ref[at, :]
        new_ref[at, :] = (
            gbr_ref[at, :].astype(F32) + grad_logit * vec_ref[0:1, :] + (grad_picked + gmid_ref[at, :])
        ).astype(BF16)
        router = router + jnp.sum(grad_logit * values, axis=0, keepdims=True)
        total = total + grad_gain
    rows = jnp.concatenate([router, total, middle_ref[0:1, :], jnp.zeros((5, router.shape[1]), F32)], axis=0)
    lanes = sum_ref.shape[1]
    sum_ref[...] = jnp.concatenate([rows[:, :lanes], rows[:, lanes:]], axis=0).astype(BF16)


def project_back(grads, weights, picked, grad_middle, branch_grad, grad_logit, vectors, gain_sums):
    tokens, width = picked.shape
    return call(
        functools.partial(project_back_kernel, len(grads)),
        "project_back",
        (*grads, *weights, picked, grad_middle, branch_grad, grad_logit, vectors, gain_sums),
        [like((tokens, width), BF16), like((VECTOR_ROWS, width // 2), BF16)],
        5.0,
        scratch=[pltpu.VMEM((tokens, width), F32)],
    )


def total_of(left, right):
    return (left.astype(F32) + right.astype(F32)).astype(BF16)


def add_first_kernel(cut, parts, extra, *refs):
    *refs, a_away, a_keep, b_away, b_keep = refs
    start = 0

    def put(x_bit, y_bit, at, begin, value):
        low, high = begin, begin + value.shape[-2]
        if low < cut:
            out = a_away if x_bit else a_keep
            out[y_bit, at, low : min(high, cut), :] = value[: min(high, cut) - low]
        if high > cut:
            out = b_away if y_bit else b_keep
            out[x_bit, at, max(low, cut) - cut : high - cut, :] = value[max(low, cut) - low :]

    for number in range(parts):
        keep, got = refs[2 * number], refs[2 * number + 1]
        for x_bit in range(2):
            for y_bit in range(2):
                for at in range(keep.shape[2]):
                    put(x_bit, y_bit, at, start, total_of(keep[x_bit, y_bit, at], got[x_bit, y_bit, at]))
        start += keep.shape[3]
    if extra:
        value = total_of(refs[-2][...], refs[-1][...])
        for x_bit in range(2):
            for y_bit in range(2):
                for at in range(4):
                    put(x_bit, y_bit, at, start, value)


def add_first(pairs, cut, extra=()):
    lanes = pairs[0][0].shape[-1]
    rows = sum(keep.shape[3] for keep, _ in pairs) + (extra[0].shape[0] if extra else 0)
    out = lambda n: like((2, 4, n, lanes), BF16)
    return call(
        functools.partial(add_first_kernel, cut, len(pairs), bool(extra)),
        "add_first",
        [array for pair in pairs for array in pair] + list(extra),
        [out(cut), out(cut), out(rows - cut), out(rows - cut)],
        0.7,
    )


def add_second_kernel(*refs):
    *refs, a_away, a_keep, b_away, b_keep = refs
    for side, (away, keep) in enumerate(((a_away, a_keep), (b_away, b_keep))):
        start = 0
        for group in range(0, len(refs), 4):
            ref, got = refs[group + 2 * side : group + 2 * side + 2]
            rows = slice(start, start + ref.shape[2])
            start = rows.stop
            for at in range(ref.shape[1]):
                keep[at, rows, :] = total_of(ref[0, at], got[0, at])
                away[at, rows, :] = total_of(ref[1, at], got[1, at])


def add_second(*groups):
    sides = [sum(group[2 * side].shape[2] for group in groups) for side in range(2)]
    shards, lanes = groups[0][0].shape[1], groups[0][0].shape[3]
    outs = [like((shards, rows, lanes), BF16) for rows in sides for _ in range(2)]
    return call(add_second_kernel, "add_second", [a for group in groups for a in group], outs, 0.5)


def add_third_kernel(a_ref, a_got, b_ref, b_got, away, keep):
    cut = a_ref.shape[1]
    for out, first in ((away, 2), (keep, 0)):
        for at in range(2):
            out[at, :cut, :] = total_of(a_ref[first + at], a_got[first + at])
            out[at, cut:, :] = total_of(b_ref[first + at], b_got[first + at])


def add_third(a_keep, a_got, b_keep, b_got):
    half = like((2, a_keep.shape[1] + b_keep.shape[1], a_keep.shape[2]), BF16)
    return call(add_third_kernel, "add_third", (a_keep, a_got, b_keep, b_got), [half, half], 0.4)


def add_fourth_kernel(keep_ref, got_ref, away, keep):
    away[...] = total_of(keep_ref[1], got_ref[1])
    keep[...] = total_of(keep_ref[0], got_ref[0])


def add_fourth(keep, got):
    half = like(keep.shape[1:], BF16)
    return call(add_fourth_kernel, "add_fourth", (keep, got), [half, half], 0.3)


def add_last_kernel(keep_ref, got_ref, out):
    out[...] = total_of(keep_ref[...], got_ref[...])


def add_last(keep, got):
    return call(add_last_kernel, "add_last", (keep, got), [like(keep.shape, BF16)], 0.3)[0]


def unpack_kernel(weights, near_ref, far_ref, *refs):
    _, chip, core = own_place()
    count = len(weights)
    done_ref, *outs = refs[: count + 1]
    inner, sems = refs[count + 1 : -1], refs[-1]
    done_ref[...] = jnp.zeros_like(done_ref)
    copies = []
    for number, (weight, ref) in enumerate(zip(weights, inner)):
        for half, blocks in enumerate((near_ref, far_ref)):
            for offset in range(4):
                for start, inside, rows, lane in weight.pieces:
                    at = aligned((chip ^ offset) * weight.rows + inside, rows, 16)
                    block = blocks[offset, start : start + rows, :]
                    ref[at, aligned((core ^ half) * weight.half + lane, weight.lanes, 128)] = block.astype(F32)
        copy = pltpu.make_async_copy(ref, outs[number], sems.at[number])
        copy.start()
        copies.append(copy)
    for copy in copies:
        copy.wait()


def unpack(weights, near, far):
    shapes = [(weight.shape[0] // 4, weight.shape[1]) for weight in weights]
    return call(
        functools.partial(unpack_kernel, weights),
        "unpack_gradients",
        (near, far),
        [like((8, 128), F32)] + [pltpu.HBM(shape, F32) for shape in shapes],
        2.0,
        scratch=[pltpu.VMEM(shape, F32) for shape in shapes] + [pltpu.SemaphoreType.DMA((len(weights),))],
        outside_outs=len(weights),
    )[1:]


def solution(mesh):
    replicas, shards = mesh.shape["rep"], mesh.shape["fsdp"]
    rep_pairs = lambda bits: [(i, i ^ bits) for i in range(replicas)]
    shard_pairs = lambda bits: [(i, i ^ bits) for i in range(shards)]
    plane = {"c": 1, "x": 2, "y": 4, "d": 6}

    def swap(values, way):
        return lax.ppermute(values, "rep", rep_pairs(plane[way]))

    def swap_shard(values, bits):
        return lax.ppermute(values, "fsdp", shard_pairs(bits))

    def swap_halves(halves, order="xy"):
        first, last = halves[:2]
        return first, swap(first, order[0]), last, swap(last, order[1])

    def swap_sums(sums, order):
        a_away, a_keep, b_away, b_keep = sums
        return a_keep, swap(a_away, order[0]), b_keep, swap(b_away, order[1])

    def over_planes(own):
        bit = 8
        while bit < replicas:
            own = total_of(own, lax.ppermute(own, "rep", rep_pairs(bit)))
            bit *= 2
        return own

    def on_device(
        hidden,
        segments,
        selected,
        w_query,
        w_key,
        w_value,
        w_out,
        w_up,
        w_down,
        w_router,
        gain_attn,
        gain_mlp,
        cotangent,
    ):
        LAST.clear()
        CALLS.clear()
        width = hidden.shape[2]
        seqs = hidden.shape[0]
        lanes = width // 2
        shard = lax.axis_index("fsdp")

        small, tall = w_query.shape[0] // 4, w_down.shape[0] // 4
        wide = w_up.shape[1] // 2 // lanes
        first_weights = [Weight(i * small, small, 1, lanes) for i in range(4)]
        up_at = Weight(0, small, wide, lanes, "columns")
        down_at = Weight(0, tall, 1, lanes, "rows")
        first_rows, second_rows = 4 * small, small * wide
        halved = lambda rows: [
            [(0, rows // 2, (0, 1)), (rows // 2, rows, (0, 2))],
            [(0, rows // 2, (2, 3)), (rows // 2, rows, (1, 3))],
        ]
        vectors = jnp.concatenate([w_router, gain_attn, gain_mlp])
        padded = jnp.pad(vectors, (0, VECTOR_ROWS * lanes - vectors.shape[0])).reshape(VECTOR_ROWS, lanes)

        first_own = pack((w_query, w_key, w_value, w_out), first_weights)
        first_pieces = [swap_shard(first_own, bits) for bits in (1, 2, 3)]
        chosen, bias = choose(selected, segments)
        picked = pick_rows(hidden, chosen)
        second_own = pack((w_up,), (up_at,), (padded,))
        second_second = swap_shard(second_own, 2)
        third_own = pack((w_down,), (down_at,))
        first = swap_halves(join_three(first_pieces, first_rows // 2))
        second_pair, third_own = join_own(second_own, second_second, [third_own])
        second_pair = swap_shard(second_pair, 1)
        third_second = swap_shard(third_own, 2)
        *first, first_both = join_chips(*first)
        first = swap_halves(first, "yx")
        first_both_far = swap(first_both, "c")
        branch_grad = pick_rows(cotangent, chosen)
        *second, others = join_shards(second_pair, second_second, [second_rows // 2, second_rows])
        second = swap_halves(second)
        vec = whole_vectors(padded, others, width)
        third_pair = swap_shard(join_own(third_own, third_second), 1)
        first_other = join_rows(first[1], first[3])
        first_other_far = swap(first_other, "c")
        *second, second_both = join_chips(*second)
        second = swap_halves(second, "yx")
        second_both_far = swap(second_both, "c")
        cover()
        *qkv, full_out = assemble(
            (w_query, w_key, w_value, w_out),
            first_weights,
            halved(first_rows),
            (first_both, first_other, first_both_far, first_other_far),
        )
        normed, queries, keys, values = project(picked, vec, qkv)
        third = swap_halves(join_shards(third_pair, third_second, [tall // 2]))
        attended, probs, queries, keys, values, normed, *qkv = attend(bias, queries, keys, values, (normed, *qkv))
        attn_out, normed_mlp, grad_mlp, gating = project_out(attended, full_out, picked, branch_grad, vec)
        second_other = join_rows(second[1], second[3])
        second_other_far = swap(second_other, "c")
        *third, third_both = join_chips(*third)
        third = swap_halves(third, "yx")
        third_both_far = swap(third_both, "c")
        cover()
        up_near, up_far = assemble(
            (w_up,), (up_at,), halved(second_rows), (second_both, second_other, second_both_far, second_other_far)
        )
        act_far, slope_far, grad_far = project_up(normed_mlp, grad_mlp, up_far)
        act_near, slope_near, grad_near = project_up(normed_mlp, grad_mlp, up_near)

        down_keep, down_send = down_blocks(grad_near, grad_far)
        down_got = swap(down_send, "c")
        third_other = join_rows(third[1], third[3])
        third_other_far = swap(third_other, "c")
        down_near, down_far = assemble(
            (w_down,), (down_at,), halved(tall), (third_both, third_other, third_both_far, third_other_far)
        )
        far, near = (act_far, slope_far, up_far, down_far), (act_near, slope_near, up_near, down_near)

        def down_step(half, step, carried=()):
            act, slope, w_in, w_back = half
            *carried, blocks = down(step, up_at, act, slope, normed_mlp, grad_mlp, w_in, w_back, carried)
            return carried, blocks

        carried, up_send = down_step(far, 0)
        up_got = swap(up_send, "c")
        d_sums = swap_sums(add_first([(down_keep, down_got)], tall // 2), "xy")
        carried, up_keep = down_step(near, 0, carried)
        u_first = swap_sums(add_first([(up_keep, up_got)], small), "xy")
        carried, up_send = down_step(far, 1, carried)
        up_got = swap(up_send, "c")
        carried, up_keep = down_step(near, 1, carried)
        new_rows, grad_attn, grad_middle, grad_logit, gain_sums = branch(
            *carried, attn_out, picked, branch_grad, gating, vec
        )
        d_sums = swap_sums(add_second(d_sums), "yx")
        u_first = tuple(hold(*u_first))
        grad_attended, out_keep, out_send = out_back(first_weights[3], grad_attn, attended, full_out)
        out_got = swap(out_send, "c")
        cover()
        u_last = swap_sums(add_first([(up_keep, up_got), (out_keep, out_got)], 64), "xy")
        grads = []
        for seq in range(seqs):
            grads += attend_back(seq, grad_attended, queries, keys, values, probs)
            if seq == seqs - 2:
                d_away, d_keep = add_third(*d_sums)
                d_got = swap_shard(d_away, 1)
        first_keep, first_send = project_grads(first_weights[:3], normed, grads)
        first_got = swap(first_send, "c")
        d_away, d_keep = add_fourth(d_keep, d_got)
        u_sums = swap_sums(add_second(u_first, u_last), "yx")
        cover()
        grad_rows, sums = project_back(
            grads, qkv, picked, grad_middle, branch_grad, grad_logit, vec, gain_sums
        )
        f_sums = swap_sums(add_first([(first_keep, first_got)], 80, (sums, swap(sums, "c"))), "xy")
        (d_away,) = hold(d_away)
        d_got = swap_shard(d_away, 2)
        u_away, u_keep = add_third(*u_sums)
        u_got = swap_shard(u_away, 1)
        out_hidden = place_rows(range(seqs), selected, new_rows, hidden)
        f_sums = swap_sums(add_second(f_sums), "yx")
        u_away, u_keep = add_fourth(u_keep, u_got)
        u_got = swap_shard(u_away, 2)
        d_own = over_planes(add_last(d_keep, d_got))
        d_got = swap(d_own, "x")
        grad_hidden = place_rows(range(1), selected, grad_rows, cotangent)
        f_away, f_keep = add_third(*f_sums)
        f_got = swap_shard(f_away, 1)
        d_pair = join(d_own, d_got)
        d_got = swap(d_pair, "y")
        u_own = over_planes(add_last(u_keep, u_got))
        u_spread = [u_own] + [swap(u_own, way) for way in "xyd"]
        grad_hidden = place_rows(range(1, 2), selected, grad_rows, cotangent, grad_hidden)
        f_away, f_keep = add_fourth(f_keep, f_got)
        f_got = swap_shard(f_away, 2)
        grad_hidden = place_rows(range(2, seqs), selected, grad_rows, cotangent, grad_hidden)
        d_near = join(d_pair, d_got).reshape(4, *d_own.shape)
        d_far = swap(d_near, "c")
        u_near = join(*u_spread)
        u_far = swap(u_near, "c")
        f_own = over_planes(add_last(f_keep, f_got))
        f_spread = [f_own] + [swap(f_own, way) for way in "xyd"]
        cover()
        (grad_down,) = unpack((Weight(0, tall, 1, lanes),), d_near, d_far)
        up_pieces = [
            (0, 0, small, 0),
            (2 * small + 16, 0, small, lanes),
            (small, 0, small, 2 * lanes),
            (2 * small, 0, 16, 3 * lanes),
            (3 * small + 16, 16, small - 16, 3 * lanes),
        ]
        grad_up, grad_out = unpack(
            (Weight(0, small, wide, lanes, pieces=up_pieces), Weight(4 * small, small, 1, lanes)), u_near, u_far
        )
        f_near = join(*f_spread)
        grad_qkv = unpack(first_weights[:3], f_near, swap(f_near, "c"))
        sums = f_own[3 * small :].reshape(2, 8, lanes)[:, :3].swapaxes(0, 1).reshape(3, width).astype(F32)
        sums = lax.dynamic_slice(sums, (0, shard * w_router.shape[0]), (3, w_router.shape[0]))
        return (out_hidden, grad_hidden, *grad_qkv, grad_out, grad_up, grad_down, sums[0], sums[1], sums[2])

    placed = (
        P(("rep", "fsdp"), None, None),
        P(("rep", "fsdp"), None),
        P(("rep", "fsdp"), None),
        P("fsdp", None),
        P("fsdp", None),
        P("fsdp", None),
        P("fsdp", None),
        P("fsdp", None),
        P("fsdp", None),
        P("fsdp"),
        P("fsdp"),
        P("fsdp"),
        P(("rep", "fsdp"), None, None),
    )
    return jax.shard_map(
        on_device,
        mesh=mesh,
        in_specs=placed,
        out_specs=(
            P(("rep", "fsdp"), None, None),
            P(("rep", "fsdp"), None, None),
            P("fsdp", None),
            P("fsdp", None),
            P("fsdp", None),
            P("fsdp", None),
            P("fsdp", None),
            P("fsdp", None),
            P("fsdp"),
            P("fsdp"),
            P("fsdp"),
        ),
        check_vma=False,
    )
```

```python
import functools

import jax
import jax.numpy as jnp
from jax import lax
from jax.experimental import pallas as pl
from jax.experimental.pallas import tpu as pltpu
from jax.sharding import PartitionSpec as P

HEADS = 12
HEAD_DIM = 64
PAIR = 2 * HEAD_DIM
EPSILON = 1e-06
F32 = jnp.float32
BF16 = jnp.bfloat16
TILE = 256
LANES = 128
VECTOR_ROWS = 16
VMEM_BYTES = 9 * 1024 * 1024
SMALL_BYTES = 6 * 1024 * 1024
STREAM_BYTES = 16 * 1024 * 1024


def dot(left, right):
    return jnp.dot(left, right, preferred_element_type=F32)


def dot_nt(left, right):
    return lax.dot_general(left, right, (((1,), (1,)), ((), ())), preferred_element_type=F32)


def dot_tn(left, right):
    return lax.dot_general(left, right, (((0,), (0,)), ((), ())), preferred_element_type=F32)


def swap_bits(place):
    return ((place & 1) << 1) | (place >> 1)


def own_place():
    member = lax.axis_index("rep") & 7
    return lax.axis_index("fsdp"), member >> 1, member & 1


def micros(time):
    return pl.CostEstimate(flops=int(time * 1.1e9), bytes_accessed=0, transcendentals=0)


BESIDE = {
    "pack_blocks": (0.1, 0.3, 0.3),
    "choose": (0.6,),
    "pick_rows": (1.0, 0.05),
    "join_three": (1.7,),
    "join_own": (2.3, 4.3),
    "join_chips": (1.2, 0.1, 0.1),
    "cover": (9.5, 9.5, 11.0, 17.0, 9.5),
    "project": (1.0,),
    "attend": (2.4,),
    "project_out": (0.8,),
    "project_up": (2.0, 2.0),
    "down_and_back": (24.0, 12.0, 2.5, 1.0),
    "attend_back": (2.2, 0.5, 2.3),
    "project_gradients": (0.5,),
    "project_back": (1.0,),
    "place_rows": (5.2, 2.2, 2.6, 0.1),
    "add_last": (0.1, 0.1, 1.0),
    "unpack_gradients": (1.3, 2.0, 0.1),
}
CALLS = {}
LARGE = {"down_and_back", "project_back", "attend"}


def beside(name):
    number = CALLS.get(name, 0)
    CALLS[name] = number + 1
    times = BESIDE.get(name, (0.1,))
    return micros(times[min(number, len(times) - 1)])


def like(shape, dtype):
    return jax.ShapeDtypeStruct(shape, dtype)


def params(limit=VMEM_BYTES):
    return pltpu.CompilerParams(vmem_limit_bytes=limit)


ANYWHERE = pl.BlockSpec(memory_space=pl.ANY)
INSIDE = pl.BlockSpec(memory_space=pltpu.VMEM)
OUTSIDE = pl.BlockSpec(memory_space=pltpu.HBM)
LAST = []


def ordered(kernel, ins, in_specs, aliases=(), **options):
    before = tuple(LAST)

    def body(*refs):
        kernel(*refs[len(before) :])

    ins = [pltpu.with_memory_space_constraint(a, pltpu.HBM) if s is OUTSIDE else a for a, s in zip(ins, in_specs)]
    outs = pl.pallas_call(
        body,
        in_specs=[ANYWHERE] * len(before) + in_specs,
        input_output_aliases={len(before) + at: out for at, out in aliases},
        **options,
    )(*before, *ins)
    LAST[:] = [min(outs, key=lambda out: out.size)]
    return outs


def call(kernel, name, ins, outs, estimate, scratch=(), outside=0, aliases=(), outside_outs=0):
    return ordered(
        kernel,
        ins,
        [OUTSIDE] * outside + [INSIDE] * (len(ins) - outside),
        aliases,
        out_specs=[INSIDE] * (len(outs) - outside_outs) + [OUTSIDE] * outside_outs,
        out_shape=list(outs),
        scratch_shapes=list(scratch),
        compiler_params=params(VMEM_BYTES if name in LARGE else SMALL_BYTES),
        cost_estimate=beside(name),
        name=name,
    )


def choose_kernel(sel_from, seg_from, chosen_ref, bias_ref, sel_ref, seg_ref, sems):
    copies = [
        pltpu.make_async_copy(sel_from, sel_ref, sems.at[0]),
        pltpu.make_async_copy(seg_from, seg_ref, sems.at[1]),
    ]
    for copy in copies:
        copy.start()
    for copy in copies:
        copy.wait()
    seqs, keep, length = chosen_ref.shape
    square = (keep, keep)
    diagonal = lax.broadcasted_iota(jnp.int32, square, 0) == lax.broadcasted_iota(jnp.int32, square, 1)
    places = lax.broadcasted_iota(jnp.int32, (keep, length), 1)
    for seq in range(seqs):
        row = sel_ref[seq : seq + 1, :].astype(F32)
        column = jnp.sum(jnp.where(diagonal, row, 0.0), axis=1, keepdims=True)
        chosen = jnp.where(column.astype(jnp.int32) == places, 1.0, 0.0).astype(BF16)
        chosen_ref[seq] = chosen
        documents = jnp.broadcast_to(seg_ref[seq : seq + 1, :].astype(F32), (8, length)).astype(BF16)
        of_column = dot_nt(chosen, documents)[:, :1]
        of_row = jnp.sum(jnp.where(diagonal, of_column, 0.0), axis=0, keepdims=True)
        allowed = (row >= column) & (of_column == of_row)
        bias_ref[seq] = jnp.where(allowed, 0.0, -1e30).astype(BF16)


def choose(selected, segments):
    seqs, keep = selected.shape
    length = segments.shape[1]
    return ordered(
        choose_kernel,
        (selected, segments),
        [OUTSIDE] * 2,
        out_specs=[INSIDE] * 2,
        out_shape=[like((seqs, keep, length), BF16), like((seqs, keep, keep), BF16)],
        scratch_shapes=[
            pltpu.VMEM(selected.shape, selected.dtype),
            pltpu.VMEM(segments.shape, segments.dtype),
            pltpu.SemaphoreType.DMA((2,)),
        ],
        compiler_params=params(),
        cost_estimate=beside("choose"),
        name="choose_rows",
    )


def pick_kernel(rows_ref, chosen_ref, picked_ref, buffer, sems):
    seqs, keep, _ = chosen_ref.shape
    copies = [pltpu.make_async_copy(rows_ref.at[seq], buffer.at[seq], sems.at[seq]) for seq in range(seqs)]
    for copy in copies:
        copy.start()
    for seq, copy in enumerate(copies):
        copy.wait()
        picked_ref[seq * keep : (seq + 1) * keep, :] = dot(chosen_ref[seq], buffer[seq]).astype(BF16)


def pick_rows(rows, chosen):
    seqs, _, width = rows.shape
    return ordered(
        pick_kernel,
        (rows, chosen),
        [OUTSIDE, INSIDE],
        out_specs=[INSIDE],
        out_shape=[like((seqs * chosen.shape[1], width), BF16)],
        scratch_shapes=[pltpu.VMEM(rows.shape, BF16), pltpu.SemaphoreType.DMA((seqs,))],
        compiler_params=params(STREAM_BYTES),
        cost_estimate=beside("pick_rows"),
        name="pick_rows",
    )[0]


def place_kernel(seqs, sel_ref, new_ref, base_ref, *refs):
    out_ref, done_ref, buffer, wide_ref, in_sems, out_sems = refs[-6:]
    done_ref[...] = jnp.zeros_like(done_ref)
    length, width = base_ref.shape[1:]
    keep = sel_ref.shape[1]
    chunks = [(number, seq, part) for number, seq in enumerate(seqs) for part in tiles(length, length // 2)]
    copies = [
        pltpu.make_async_copy(base_ref.at[seq, part, :], buffer.at[number, part, :], in_sems.at[at])
        for at, (number, seq, part) in enumerate(chunks)
    ]
    for copy in copies:
        copy.start()
    for number, seq in enumerate(seqs):
        wide_ref[number, :, :width] = new_ref[seq * keep : (seq + 1) * keep, :]
        wide_ref[number, :, width:] = jnp.ones((keep, LANES), BF16)
    results = []
    for at, (number, seq, part) in enumerate(chunks):
        places = lax.broadcasted_iota(jnp.int32, (part.stop - part.start, keep), 0) + part.start
        hits = jnp.where(places == sel_ref[seq : seq + 1, :], 1.0, 0.0).astype(BF16)
        copies[at].wait()
        for row in range(0, part.stop - part.start, TILE):
            placed = dot(hits[row : row + TILE, :], wide_ref[number])
            new = placed[:, width:] > 0.0
            rows = slice(part.start + row, part.start + row + TILE)
            for lane in range(0, width, LANES):
                lanes = slice(lane, lane + LANES)
                base = buffer[number, rows, lanes].astype(F32)
                buffer[number, rows, lanes] = jnp.where(new, placed[:, lanes], base).astype(BF16)
        back = pltpu.make_async_copy(buffer.at[number, part, :], out_ref.at[seq, part, :], out_sems.at[at])
        back.start()
        results.append(back)
    for back in results:
        back.wait()


def place_rows(seqs, selected, new_rows, base, placed=None):
    _, length, width = base.shape
    earlier = () if placed is None else (placed,)
    return ordered(
        functools.partial(place_kernel, tuple(seqs)),
        (selected, new_rows, base, *earlier),
        [INSIDE, INSIDE, OUTSIDE] + [OUTSIDE] * len(earlier),
        aliases=[(3, 0)] if earlier else [],
        out_specs=[OUTSIDE, INSIDE],
        out_shape=[pltpu.HBM(base.shape, BF16), like((8, 128), F32)],
        scratch_shapes=[
            pltpu.VMEM((len(seqs), length, width), BF16),
            pltpu.VMEM((len(seqs), selected.shape[1], width + LANES), BF16),
        ]
        + [pltpu.SemaphoreType.DMA((2 * len(seqs),))] * 2,
        compiler_params=params(STREAM_BYTES),
        cost_estimate=beside("place_rows"),
        name="place_rows",
    )[0]


class Weight:
    def __init__(self, start, rows, columns, lanes, split=None, pieces=None):
        self.start, self.rows, self.columns, self.lanes, self.split = start, rows, columns, lanes, split
        self.parts = 1 if split is None else 2
        self.half = columns * lanes
        self.shape = (16 * rows, 2 * self.half)
        self.pieces = pieces or [(at, 0, rows, lane) for at, lane in self.slots()]

    def slots(self):
        return [(self.start + c * self.rows, c * self.lanes) for c in range(self.columns)]


def aligned(value, size, multiple):
    return pl.ds(pl.multiple_of(value, multiple), size)


def pack_kernel(weights, *refs):
    _, chip, core = own_place()
    *ins, out_ref, sem = refs
    for own, weight in zip(ins, weights):
        for start, lane in weight.slots():
            pltpu.make_async_copy(
                own.at[
                    aligned(chip * weight.rows, weight.rows, 16), aligned(core * weight.half + lane, weight.lanes, 128)
                ],
                out_ref.at[start : start + weight.rows, :],
                sem,
            ).start()
    for extra in ins[len(weights) :]:
        pltpu.make_async_copy(extra, out_ref.at[out_ref.shape[0] - extra.shape[0] :, :], sem).start()
    pltpu.make_async_copy(out_ref, out_ref, sem).wait()


def pack(owns, weights, extra=()):
    rows = sum(w.rows * w.columns for w in weights) + sum(e.shape[0] for e in extra)
    return call(
        functools.partial(pack_kernel, weights),
        "pack_blocks",
        (*owns, *extra),
        [like((rows, weights[0].lanes), BF16)],
        0.5,
        scratch=[pltpu.SemaphoreType.DMA],
        outside=len(owns) + len(extra),
    )[0]


def join_own_kernel(own_ref, second_ref, *refs):
    *held, out_ref, out_held = refs if len(refs) > 1 else (*refs, None)
    for ref in held:
        out_held[...] = ref[...]
    out_ref[0] = own_ref[...]
    out_ref[1] = second_ref[...]


def join_own(own, second, held=()):
    outs = [like((2, *own.shape), BF16)] + [like(a.shape, a.dtype) for a in held]
    outs = call(join_own_kernel, "join_own", (own, second, *held), outs, 0.2)
    return outs if held else outs[0]


def join_shards_kernel(count, pair_ref, second_ref, *refs):
    held, outs = refs[:count], refs[count:]
    for ref, out in zip(held, outs[len(outs) - count :]):
        out[...] = ref[...]
    start = 0
    for out in outs[: len(outs) - count]:
        rows = slice(start, start + out.shape[1])
        start = rows.stop
        out[0] = pair_ref[0, rows, :]
        out[1] = second_ref[rows, :]
        out[2] = pair_ref[1, rows, :]


def join_shards(pair, second, cuts, held=()):
    _, rows, lanes = pair.shape
    edges = [0, *cuts, rows]
    outs = [like((3, high - low, lanes), BF16) for low, high in zip(edges, edges[1:])]
    outs += [like(a.shape, a.dtype) for a in held]
    return call(functools.partial(join_shards_kernel, len(held)), "join_shards", (pair, second, *held), outs, 0.3)


def hold_kernel(*refs):
    count = len(refs) // 2
    for ref, out in zip(refs[:count], refs[count:]):
        out[...] = ref[...]


def hold(*arrays):
    return call(hold_kernel, "hold", arrays, [like(a.shape, a.dtype) for a in arrays], 0.2)


def cover_kernel(out_ref):
    out_ref[...] = jnp.zeros_like(out_ref)


def cover():
    call(cover_kernel, "cover", (), [like((8, 128), F32)], 0.1)


def join_three_kernel(first_ref, second_ref, third_ref, *outs):
    start = 0
    for out in outs:
        rows = slice(start, start + out.shape[1])
        start = rows.stop
        for at, ref in enumerate((first_ref, second_ref, third_ref)):
            out[at] = ref[rows, :]


def join_three(pieces, cut):
    rows, lanes = pieces[0].shape
    outs = [like((3, cut, lanes), BF16), like((3, rows - cut, lanes), BF16)]
    return call(join_three_kernel, "join_three", pieces, outs, 0.3)


def join_chips_kernel(first_ref, first_got, last_ref, last_got, first_out, last_out, both_out):
    cut = first_ref.shape[1]
    for at, (first, last) in enumerate(((first_ref, last_ref), (first_got, last_got))):
        first_out[at] = first[...]
        last_out[at] = last[...]
        both_out[at, :, :cut, :] = first[...]
        both_out[at, :, cut:, :] = last[...]


def join_chips(first, first_got, last, last_got):
    count, cut, lanes = first.shape
    rows = last.shape[1]
    shapes = [(2, count, cut, lanes), (2, count, rows, lanes), (2, count, cut + rows, lanes)]
    return call(
        join_chips_kernel, "join_chips", (first, first_got, last, last_got), [like(s, BF16) for s in shapes], 0.5
    )


def vectors_kernel(own_ref, others_ref, out_ref):
    shard, _, _ = own_place()
    lanes = out_ref.shape[1] // 4
    pieces = []
    for ref in (own_ref, *[others_ref.at[other] for other in range(3)]):
        rows = ref[...].astype(F32)
        pieces.append(jnp.concatenate([rows[:1, :lanes], rows[:1, lanes:], rows[1:2, :lanes]], axis=0))
    out_ref[...] = jnp.zeros_like(out_ref)
    for place in range(4):
        value = pieces[3]
        for other in range(3):
            value = jnp.where((shard ^ place) == other, pieces[other], value)
        out_ref[:3, place * lanes : (place + 1) * lanes] = value


def whole_vectors(own, others, width):
    return call(vectors_kernel, "vectors", (own, others), [like((8, width), F32)], 0.2)[0]


def join_rows_kernel(*refs):
    *ins, out = refs
    start = 0
    for ref in ins:
        rows = ref.shape[-2]
        out[..., start : start + rows, :] = ref[...]
        start += rows


def join_rows(*arrays):
    shape = list(arrays[0].shape)
    shape[-2] = sum(a.shape[-2] for a in arrays)
    return call(join_rows_kernel, "join_rows", arrays, [like(shape, BF16)], 0.3)[0]


def join_kernel(*refs):
    *ins, out = refs
    for at, ref in enumerate(ins):
        out[at] = ref[...]


def join(*arrays):
    return call(join_kernel, "join", arrays, [like((len(arrays), *arrays[0].shape), BF16)], 0.2)[0]


def join_turned_kernel(pair_ref, got_ref, out):
    for y_bit in range(2):
        out[2 * y_bit] = pair_ref[y_bit]
        out[2 * y_bit + 1] = got_ref[y_bit]


def join_turned(pair, got):
    return call(join_turned_kernel, "join_turned", (pair, got), [like((4, *pair.shape[1:]), BF16)], 0.2)[0]


def assemble_kernel(weights, layout, *refs):
    shard, chip, core = own_place()
    count = len(layout)
    owns, refs = refs[: len(weights)], refs[len(weights) :]
    *refs, sems = refs
    pieces, outs = (refs[:count], refs[count : 2 * count]), list(refs[2 * count :])
    for number, (weight, own) in enumerate(zip(weights, owns)):
        shard_rows = own.shape[0]
        sem = sems.at[number]
        targets = [outs.pop(0) for _ in range(weight.parts)]

        def fill(place_of):
            copies = []
            if weight.split == "columns":
                for half in range(2):
                    out, row, _ = place_of(0, half)
                    lane = aligned((core ^ half) * weight.half, weight.half, 128)
                    copies.append(pltpu.make_async_copy(own.at[:, lane], out.at[row, :], sem.at[half]))
            else:
                out, row, _ = place_of(0, 0)
                copies.append(pltpu.make_async_copy(own, out.at[row, :], sem.at[0]))
            for copy in copies:
                copy.start()
            for half in range(2):
                for number, ranges in enumerate(layout):
                    ref = pieces[half][number]
                    for start, lane in weight.slots():
                        for low, high, chips in ranges:
                            lo, hi = max(start, low), min(start + weight.rows, high)
                            if lo >= hi:
                                continue
                            for at, offset in enumerate(chips):
                                for other in range(3):
                                    inner = (chip ^ offset) * weight.rows + (lo - start)
                                    out, row, lanes = place_of(other + 1, half, inner, hi - lo, lane, weight.lanes)
                                    out[row, lanes] = ref[at, other, lo:hi, :]
            for copy in copies:
                copy.wait()

        if weight.split == "columns":

            def place_of(other, half, inner=0, rows=shard_rows, lane=0, lanes=weight.half):
                return targets[half], aligned((shard ^ other) * shard_rows + inner, rows, 16), slice(lane, lane + lanes)

            fill(place_of)
        elif weight.split == "rows":
            for near in range(2):

                def place_of(other, half, inner=0, rows=shard_rows, lane=0, lanes=0):
                    row = ((shard ^ other) & 1) * shard_rows + inner
                    at = aligned((core ^ half) * weight.half + lane, lanes, 128) if lanes else slice(None)
                    return targets[near ^ (other >> 1)], aligned(row, rows, 16), at

                pl.when(((shard >> 1) ^ core) == near)(functools.partial(fill, place_of))
        else:

            def place_of(other, half, inner=0, rows=shard_rows, lane=0, lanes=0):
                at = aligned((core ^ half) * weight.half + lane, lanes, 128) if lanes else slice(None)
                return targets[0], aligned((shard ^ other) * shard_rows + inner, rows, 16), at

            fill(place_of)


def assemble(owns, weights, layout, pieces):
    outs = []
    for weight in weights:
        rows, columns = weight.shape
        if weight.split == "columns":
            outs += [like((rows, columns // 2), BF16)] * 2
        elif weight.split == "rows":
            outs += [like((rows // 2, columns), BF16)] * 2
        else:
            outs.append(like((rows, columns), BF16))
    return call(
        functools.partial(assemble_kernel, weights, layout),
        "assemble_weights",
        (*owns, *pieces),
        outs,
        0.3 * sum(w.columns * w.rows for w in weights) / 48,
        scratch=[pltpu.SemaphoreType.DMA((len(weights), 2))],
    )


def write_blocks(grad_ref, keep_ref, send_ref, start, rows):
    shard, chip, core = own_place()
    lanes = keep_ref.shape[-1]
    for x_bit in range(2):
        for y_bit in range(2):
            for place in range(4):
                row = (shard ^ swap_bits(place)) * (4 * rows) + (chip ^ (2 * y_bit + x_bit)) * rows
                for half, out in ((0, keep_ref), (1, send_ref)):
                    out[x_bit, y_bit, place, start : start + rows, :] = grad_ref[
                        aligned(row, rows, 16), aligned((core ^ half) * lanes, lanes, 128)
                    ].astype(BF16)


def tiles(size, step=TILE):
    return [slice(i, i + step) for i in range(0, size, step)]


def inverse_rms(values):
    return lax.rsqrt(jnp.mean(values * values, axis=-1, keepdims=True) + EPSILON)


def project_kernel(picked_ref, vec_ref, wq, wk, wv, normed_ref, q_ref, k_ref, v_ref):
    for at in tiles(picked_ref.shape[0]):
        values = picked_ref[at, :].astype(F32)
        normed_ref[at, :] = (values * inverse_rms(values) * vec_ref[1:2, :]).astype(BF16)
    q_ref[...] = dot(normed_ref[...], wq[...]).astype(BF16) * 0.125
    k_ref[...] = dot(normed_ref[...], wk[...]).astype(BF16)
    v_ref[...] = dot(normed_ref[...], wv[...]).astype(BF16)


def project(picked, vectors, weights):
    flat = like(picked.shape, BF16)
    return call(project_kernel, "project", (picked, vectors, *weights), [flat] * 4, 4.5)


def low_half_lanes(rows):
    return lax.broadcasted_iota(jnp.int32, (rows, PAIR), 1) < HEAD_DIM


def split_heads(low_half, values):
    return jnp.concatenate([jnp.where(low_half, values, 0), jnp.where(low_half, 0, values)], axis=0)


def join_heads(low_half, values):
    rows = low_half.shape[0]
    return jnp.where(low_half, values[:rows], values[rows:]).astype(BF16)


def attend_kernel(count, bias_ref, q_ref, k_ref, v_ref, *refs):
    later, (att_ref, probs_out, *outs), (probs_ref, sems) = refs[:count], refs[count:-2], refs[-2:]
    seqs, keep, _ = bias_ref.shape
    low_half = low_half_lanes(keep)
    copies = [
        pltpu.make_async_copy(ref, out, sems.at[at]) for at, (ref, out) in enumerate(zip((q_ref, k_ref, v_ref, *later), outs))
    ]
    for copy in copies:
        copy.start()
    for seq in range(seqs):
        bias = bias_ref[seq].astype(F32)
        rows = slice(seq * keep, (seq + 1) * keep)
        for pair in range(HEADS // 2):
            lanes = slice(pair * PAIR, (pair + 1) * PAIR)
            queries, keys, values = q_ref[rows, lanes], k_ref[rows, lanes], v_ref[rows, lanes]
            scores = dot_nt(split_heads(low_half, keys), queries)
            both = []
            for half in range(2):
                own = scores[half * keep : (half + 1) * keep] + bias
                exponent = jnp.exp(own - jnp.max(own, axis=0, keepdims=True))
                both.append((exponent * (1.0 / jnp.sum(exponent, axis=0, keepdims=True))).astype(BF16))
                probs_ref[seq, 2 * pair + half] = both[half]
            att_ref[rows, lanes] = join_heads(low_half, dot_tn(jnp.concatenate(both, axis=1), values))
        copy = pltpu.make_async_copy(probs_ref.at[seq], probs_out.at[seq], sems.at[len(outs) + seq])
        copy.start()
        copies.append(copy)
    for copy in copies:
        copy.wait()


def attend(bias, queries, keys, values, later):
    seqs, keep, _ = bias.shape
    shape = (seqs, HEADS, keep, keep)
    kept = (queries, keys, values, *later)
    return call(
        functools.partial(attend_kernel, len(later)),
        "attend",
        (bias, *kept),
        [like(queries.shape, BF16), pltpu.HBM(shape, BF16)] + [pltpu.HBM(a.shape, a.dtype) for a in kept],
        6.5,
        scratch=[pltpu.VMEM(shape, BF16), pltpu.SemaphoreType.DMA((len(kept) + seqs,))],
        outside_outs=1 + len(kept),
    )


def out_kernel(att_ref, wo_ref, picked_ref, gbr_ref, vec_ref, attn_ref, nm_ref, gmlp_ref, gating_ref):
    attn_ref[...] = dot(att_ref[...], wo_ref[...])
    for at in tiles(picked_ref.shape[0]):
        values = picked_ref[at, :].astype(F32)
        middle = values + attn_ref[at, :]
        nm_ref[at, :] = (middle * inverse_rms(middle) * vec_ref[2:3, :]).astype(BF16)
        logit = jnp.sum(values * vec_ref[0:1, :], axis=-1, keepdims=True)
        gating = 1.0 / (1.0 + jnp.exp(-logit))
        gating_ref[at, :] = gating
        gmlp_ref[at, :] = (gating * gbr_ref[at, :].astype(F32)).astype(BF16)


def project_out(attended, w_out, picked, branch_grad, vectors):
    flat = like(picked.shape, BF16)
    return call(
        out_kernel,
        "project_out",
        (attended, w_out, picked, branch_grad, vectors),
        [like(picked.shape, F32), flat, flat, like((picked.shape[0], 1), F32)],
        2.0,
    )


def gelu_parts(values):
    cdf = 0.5 * (1.0 + lax.erf(values * 0.7071067811865476))
    return values * cdf, cdf + values * (jnp.exp(-0.5 * values * values) * 0.3989422804014327)


def up_kernel(nm_ref, gmlp_ref, wu_ref, act_ref, slope_ref, grad_ref):
    tokens = nm_ref.shape[0]
    for columns in tiles(wu_ref.shape[1], wu_ref.shape[1] // 2):
        for at in tiles(tokens, 128):
            activated, slope = gelu_parts(dot(nm_ref[at, :], wu_ref[:, columns]))
            act_ref[at, columns] = activated.astype(BF16)
            slope_ref[at, columns] = slope.astype(BF16)
        grad_ref[columns, :] = dot_tn(act_ref[:, columns], gmlp_ref[...]).astype(BF16)


def project_up(normed, grad_mlp, w_up):
    tokens, width = normed.shape
    units = w_up.shape[1]
    wide = like((tokens, units), BF16)
    return call(
        up_kernel,
        "project_up",
        (normed, grad_mlp, w_up),
        [wide, wide, like((units, width), BF16)],
        6.0,
    )


def down_blocks_kernel(near_ref, far_ref, keep_ref, send_ref):
    shard, chip, core = own_place()
    rows, lanes = keep_ref.shape[-2:]
    shard_rows = 4 * rows

    def fill(near):
        for place in range(4):
            other = swap_bits(place)
            ref = (near_ref, far_ref)[near ^ (other >> 1)]
            for x_bit in range(2):
                for y_bit in range(2):
                    row = ((shard ^ other) & 1) * shard_rows + (chip ^ (2 * y_bit + x_bit)) * rows
                    for half, out in ((0, keep_ref), (1, send_ref)):
                        out[x_bit, y_bit, place] = ref[
                            aligned(row, rows, 16), aligned((core ^ half) * lanes, lanes, 128)
                        ]

    for near in range(2):
        pl.when(((shard >> 1) ^ core) == near)(functools.partial(fill, near))


def down_blocks(near, far):
    units, width = near.shape
    blocks = like((2, 2, 4, units // 8, width // 2), BF16)
    return call(down_blocks_kernel, "down_blocks", (near, far), [blocks, blocks], 0.7)


def norm_back(grad_normed, values, inverse, gain):
    scaled = grad_normed * gain
    grad_gain = jnp.sum(grad_normed * values * inverse, axis=0, keepdims=True)
    grad_values = inverse * scaled - values * (inverse * inverse * inverse) * jnp.mean(
        scaled * values, axis=-1, keepdims=True
    )
    return grad_values, grad_gain


def down_kernel(step, weight, act_ref, slope_ref, nm_ref, gmlp_ref, wu_ref, wd_ref, *refs):
    *starts, mlp_ref, gnm_ref, out_ref, grad_ref = refs
    shard, chip, core = own_place()
    block = wd_ref.shape[0] // 2
    rows, lanes = weight.rows, weight.lanes
    at = slice(step * block, (step + 1) * block)
    down = wd_ref[at, :]
    mlp = dot(act_ref[:, at], down)
    grad_before = (dot_nt(gmlp_ref[...], down) * slope_ref[:, at].astype(F32)).astype(BF16)
    grad_ref[...] = dot_tn(nm_ref[...], grad_before)
    grad_nm = dot_nt(grad_before, wu_ref[:, at])
    mlp_ref[...] = starts[0][...] + mlp if starts else mlp
    gnm_ref[...] = starts[1][...] + grad_nm if starts else grad_nm
    for x_bit in range(2):
        for y_bit in range(2):
            for place in range(4):
                row = (shard ^ swap_bits(place)) * (4 * rows) + (chip ^ (2 * y_bit + x_bit)) * rows
                for part in range(block // lanes):
                    out_ref[x_bit, y_bit, place, part * rows : (part + 1) * rows, :] = grad_ref[
                        aligned(row, rows, 16), part * lanes : (part + 1) * lanes
                    ].astype(BF16)


def down(step, weight, activated, slope, normed, grad_mlp, w_up, w_down, starts=()):
    tokens, width = normed.shape
    total = like((tokens, width), F32)
    return call(
        functools.partial(down_kernel, step, weight),
        "down_and_back",
        (activated, slope, normed, grad_mlp, w_up, w_down, *starts),
        [total, total, like((2, 2, 4, weight.rows * weight.columns // 2, weight.lanes), BF16)],
        4.2,
        scratch=[pltpu.VMEM((width, w_up.shape[1] // 2), F32)],
        aliases=[(6, 0), (7, 1)] if starts else [],
    )


def branch_kernel(
    mlp_ref, gnm_ref, attn_ref, picked_ref, gbr_ref, gating_ref, vec_ref, new_ref, gattn_ref, gmid_ref, glogit_ref, sum_ref
):
    total = jnp.zeros((1, vec_ref.shape[1]), F32)
    for at in tiles(picked_ref.shape[0]):
        attention = attn_ref[at, :]
        values = picked_ref[at, :].astype(F32)
        gating = gating_ref[at, :]
        branch_grad = gbr_ref[at, :].astype(F32)
        delta = attention + mlp_ref[at, :]
        new_ref[at, :] = (values + gating * delta).astype(BF16)
        grad_gating = jnp.sum(branch_grad * delta, axis=-1, keepdims=True)
        glogit_ref[at, :] = grad_gating * gating * (1.0 - gating)
        middle = values + attention
        grad_middle, grad_gain = norm_back(gnm_ref[at, :], middle, inverse_rms(middle), vec_ref[2:3, :])
        gmid_ref[at, :] = grad_middle
        gattn_ref[at, :] = (gating * branch_grad + grad_middle).astype(BF16)
        total = total + grad_gain
    sum_ref[...] = jnp.broadcast_to(total, sum_ref.shape)


def branch(mlp, grad_nm, attn_out, picked, branch_grad, gating, vectors):
    tokens, width = picked.shape
    return call(
        branch_kernel,
        "branch_and_norm_back",
        (mlp, grad_nm, attn_out, picked, branch_grad, gating, vectors),
        [
            like((tokens, width), BF16),
            like((tokens, width), BF16),
            like((tokens, width), F32),
            like((tokens, 1), F32),
            like((8, width), F32),
        ],
        2.0,
    )


def out_back_kernel(weight, gattn_ref, att_ref, wo_ref, gatt_ref, keep_ref, send_ref, grad_ref):
    grad_ref[...] = dot_tn(att_ref[...], gattn_ref[...])
    gatt_ref[...] = dot_nt(gattn_ref[...], wo_ref[...]).astype(BF16)
    write_blocks(grad_ref, keep_ref, send_ref, 0, weight.rows)


def out_back(weight, grad_attn, attended, w_out):
    blocks = like((2, 2, 4, weight.rows, weight.lanes), BF16)
    return call(
        functools.partial(out_back_kernel, weight),
        "project_out_back",
        (grad_attn, attended, w_out),
        [like(grad_attn.shape, BF16), blocks, blocks],
        2.5,
        scratch=[pltpu.VMEM(weight.shape, F32)],
    )


def attend_back_kernel(seq, gatt_ref, q_ref, k_ref, v_ref, probs_ref, gq_ref, gk_ref, gv_ref):
    keep = probs_ref.shape[2]
    low_half = low_half_lanes(keep)
    rows = slice(seq * keep, (seq + 1) * keep)
    for pair in range(HEADS // 2):
        lanes = slice(pair * PAIR, (pair + 1) * PAIR)
        queries, keys, values = q_ref[rows, lanes], k_ref[rows, lanes], v_ref[rows, lanes]
        grad_att = gatt_ref[rows, lanes]
        grad_probs = dot_nt(split_heads(low_half, values), grad_att)
        probs = [probs_ref[seq, 2 * pair + half] for half in range(2)]
        scores = []
        for half in range(2):
            wide = probs[half].astype(F32)
            weighted = wide * grad_probs[half * keep : (half + 1) * keep]
            scores.append((weighted - wide * jnp.sum(weighted, axis=0, keepdims=True)).astype(BF16))
        gq_ref[:, lanes] = join_heads(low_half, dot_tn(jnp.concatenate(scores, axis=1), keys) * 0.125)
        gk_ref[:, lanes] = join_heads(low_half, dot(jnp.concatenate(scores, axis=0), queries))
        gv_ref[:, lanes] = join_heads(low_half, dot(jnp.concatenate(probs, axis=0), grad_att))


def attend_back(seq, grad_attended, queries, keys, values, probs):
    rows = like((probs.shape[2], queries.shape[1]), BF16)
    return call(
        functools.partial(attend_back_kernel, seq),
        "attend_back",
        (grad_attended, queries, keys, values, probs),
        [rows] * 3,
        4.0,
    )


def project_grads_kernel(weights, normed_ref, *refs):
    *grads, keep_ref, send_ref, grad_ref = refs
    for i, weight in enumerate(weights):
        grad_ref[...] = dot_tn(normed_ref[...], rows_of(grads, i))
        write_blocks(grad_ref, keep_ref, send_ref, weight.start, weight.rows)


def rows_of(grads, i):
    return jnp.concatenate([ref[...] for ref in grads[i::3]], axis=0)


def project_grads(weights, normed, grads):
    blocks = like((2, 2, 4, sum(w.rows for w in weights), weights[0].lanes), BF16)
    return call(
        functools.partial(project_grads_kernel, weights),
        "project_gradients",
        (normed, *grads),
        [blocks, blocks],
        4.0,
        scratch=[pltpu.VMEM(weights[0].shape, F32)],
    )


def project_back_kernel(count, *refs):
    grads, refs = refs[:count], refs[count:]
    wq, wk, wv, picked_ref, gmid_ref, gbr_ref, glogit_ref, vec_ref, middle_ref, new_ref, sum_ref, gn_ref = refs
    gn_ref[...] = sum(dot_nt(rows_of(grads, i), w[...]) for i, w in enumerate((wq, wk, wv)))
    router = jnp.zeros((1, vec_ref.shape[1]), F32)
    total = router
    for at in tiles(picked_ref.shape[0]):
        values = picked_ref[at, :].astype(F32)
        grad_picked, grad_gain = norm_back(gn_ref[at, :], values, inverse_rms(values), vec_ref[1:2, :])
        grad_logit = glogit_ref[at, :]
        new_ref[at, :] = (
            gbr_ref[at, :].astype(F32) + grad_logit * vec_ref[0:1, :] + (grad_picked + gmid_ref[at, :])
        ).astype(BF16)
        router = router + jnp.sum(grad_logit * values, axis=0, keepdims=True)
        total = total + grad_gain
    rows = jnp.concatenate([router, total, middle_ref[0:1, :], jnp.zeros((5, router.shape[1]), F32)], axis=0)
    lanes = sum_ref.shape[1]
    sum_ref[...] = jnp.concatenate([rows[:, :lanes], rows[:, lanes:]], axis=0).astype(BF16)


def project_back(grads, weights, picked, grad_middle, branch_grad, grad_logit, vectors, gain_sums):
    tokens, width = picked.shape
    return call(
        functools.partial(project_back_kernel, len(grads)),
        "project_back",
        (*grads, *weights, picked, grad_middle, branch_grad, grad_logit, vectors, gain_sums),
        [like((tokens, width), BF16), like((VECTOR_ROWS, width // 2), BF16)],
        5.0,
        scratch=[pltpu.VMEM((tokens, width), F32)],
    )


def total_of(left, right):
    return (left.astype(F32) + right.astype(F32)).astype(BF16)


def add_first_kernel(cut, parts, extra, *refs):
    *refs, a_away, a_keep, b_away, b_keep = refs
    start = 0

    def put(x_bit, y_bit, at, begin, value):
        low, high = begin, begin + value.shape[-2]
        if low < cut:
            out = a_away if x_bit else a_keep
            out[y_bit, at, low : min(high, cut), :] = value[: min(high, cut) - low]
        if high > cut:
            out = b_away if y_bit else b_keep
            out[x_bit, at, max(low, cut) - cut : high - cut, :] = value[max(low, cut) - low :]

    for number in range(parts):
        keep, got = refs[2 * number], refs[2 * number + 1]
        for x_bit in range(2):
            for y_bit in range(2):
                for at in range(keep.shape[2]):
                    put(x_bit, y_bit, at, start, total_of(keep[x_bit, y_bit, at], got[x_bit, y_bit, at]))
        start += keep.shape[3]
    if extra:
        value = total_of(refs[-2][...], refs[-1][...])
        for x_bit in range(2):
            for y_bit in range(2):
                for at in range(4):
                    put(x_bit, y_bit, at, start, value)


def add_first(pairs, cut, extra=()):
    lanes = pairs[0][0].shape[-1]
    rows = sum(keep.shape[3] for keep, _ in pairs) + (extra[0].shape[0] if extra else 0)
    out = lambda n: like((2, 4, n, lanes), BF16)
    return call(
        functools.partial(add_first_kernel, cut, len(pairs), bool(extra)),
        "add_first",
        [array for pair in pairs for array in pair] + list(extra),
        [out(cut), out(cut), out(rows - cut), out(rows - cut)],
        0.7,
    )


def add_second_kernel(*refs):
    *refs, a_away, a_keep, b_away, b_keep = refs
    for side, (away, keep) in enumerate(((a_away, a_keep), (b_away, b_keep))):
        start = 0
        for group in range(0, len(refs), 4):
            ref, got = refs[group + 2 * side : group + 2 * side + 2]
            rows = slice(start, start + ref.shape[2])
            start = rows.stop
            for at in range(ref.shape[1]):
                keep[at, rows, :] = total_of(ref[0, at], got[0, at])
                away[at, rows, :] = total_of(ref[1, at], got[1, at])


def add_second(*groups):
    sides = [sum(group[2 * side].shape[2] for group in groups) for side in range(2)]
    shards, lanes = groups[0][0].shape[1], groups[0][0].shape[3]
    outs = [like((shards, rows, lanes), BF16) for rows in sides for _ in range(2)]
    return call(add_second_kernel, "add_second", [a for group in groups for a in group], outs, 0.5)


def add_third_kernel(a_ref, a_got, b_ref, b_got, away, keep):
    cut = a_ref.shape[1]
    for out, first in ((away, 2), (keep, 0)):
        for at in range(2):
            out[at, :cut, :] = total_of(a_ref[first + at], a_got[first + at])
            out[at, cut:, :] = total_of(b_ref[first + at], b_got[first + at])


def add_third(a_keep, a_got, b_keep, b_got):
    half = like((2, a_keep.shape[1] + b_keep.shape[1], a_keep.shape[2]), BF16)
    return call(add_third_kernel, "add_third", (a_keep, a_got, b_keep, b_got), [half, half], 0.4)


def add_fourth_kernel(keep_ref, got_ref, away, keep):
    away[...] = total_of(keep_ref[1], got_ref[1])
    keep[...] = total_of(keep_ref[0], got_ref[0])


def add_fourth(keep, got):
    half = like(keep.shape[1:], BF16)
    return call(add_fourth_kernel, "add_fourth", (keep, got), [half, half], 0.3)


def add_last_kernel(keep_ref, got_ref, out):
    out[...] = total_of(keep_ref[...], got_ref[...])


def add_last(keep, got):
    return call(add_last_kernel, "add_last", (keep, got), [like(keep.shape, BF16)], 0.3)[0]


def unpack_kernel(weights, near_ref, far_ref, *refs):
    _, chip, core = own_place()
    count = len(weights)
    done_ref, *outs = refs[: count + 1]
    inner, sems = refs[count + 1 : -1], refs[-1]
    done_ref[...] = jnp.zeros_like(done_ref)
    copies = []
    for number, (weight, ref) in enumerate(zip(weights, inner)):
        for half, blocks in enumerate((near_ref, far_ref)):
            for offset in range(4):
                for start, inside, rows, lane in weight.pieces:
                    at = aligned((chip ^ offset) * weight.rows + inside, rows, 16)
                    block = blocks[offset, start : start + rows, :]
                    ref[at, aligned((core ^ half) * weight.half + lane, weight.lanes, 128)] = block.astype(F32)
        copy = pltpu.make_async_copy(ref, outs[number], sems.at[number])
        copy.start()
        copies.append(copy)
    for copy in copies:
        copy.wait()


def unpack(weights, near, far):
    shapes = [(weight.shape[0] // 4, weight.shape[1]) for weight in weights]
    return call(
        functools.partial(unpack_kernel, weights),
        "unpack_gradients",
        (near, far),
        [like((8, 128), F32)] + [pltpu.HBM(shape, F32) for shape in shapes],
        2.0,
        scratch=[pltpu.VMEM(shape, F32) for shape in shapes] + [pltpu.SemaphoreType.DMA((len(weights),))],
        outside_outs=len(weights),
    )[1:]


def solution(mesh):
    replicas, shards = mesh.shape["rep"], mesh.shape["fsdp"]
    rep_pairs = lambda bits: [(i, i ^ bits) for i in range(replicas)]
    shard_pairs = lambda bits: [(i, i ^ bits) for i in range(shards)]
    plane = {"c": 1, "x": 2, "y": 4, "d": 6}

    def swap(values, way):
        return lax.ppermute(values, "rep", rep_pairs(plane[way]))

    def swap_shard(values, bits):
        return lax.ppermute(values, "fsdp", shard_pairs(bits))

    def swap_halves(halves, order="xy"):
        first, last = halves[:2]
        return first, swap(first, order[0]), last, swap(last, order[1])

    def swap_sums(sums, order):
        a_away, a_keep, b_away, b_keep = sums
        return a_keep, swap(a_away, order[0]), b_keep, swap(b_away, order[1])

    def over_planes(own):
        bit = 8
        while bit < replicas:
            own = total_of(own, lax.ppermute(own, "rep", rep_pairs(bit)))
            bit *= 2
        return own

    def on_device(
        hidden,
        segments,
        selected,
        w_query,
        w_key,
        w_value,
        w_out,
        w_up,
        w_down,
        w_router,
        gain_attn,
        gain_mlp,
        cotangent,
    ):
        LAST.clear()
        CALLS.clear()
        width = hidden.shape[2]
        seqs = hidden.shape[0]
        lanes = width // 2
        shard = lax.axis_index("fsdp")

        small, tall = w_query.shape[0] // 4, w_down.shape[0] // 4
        wide = w_up.shape[1] // 2 // lanes
        first_weights = [Weight(i * small, small, 1, lanes) for i in range(4)]
        up_at = Weight(0, small, wide, lanes, "columns")
        down_at = Weight(0, tall, 1, lanes, "rows")
        first_rows, second_rows = 4 * small, small * wide
        halved = lambda rows: [
            [(0, rows // 2, (0, 1)), (rows // 2, rows, (0, 2))],
            [(0, rows // 2, (2, 3)), (rows // 2, rows, (1, 3))],
        ]
        vectors = jnp.concatenate([w_router, gain_attn, gain_mlp])
        padded = jnp.pad(vectors, (0, VECTOR_ROWS * lanes - vectors.shape[0])).reshape(VECTOR_ROWS, lanes)

        first_own = pack((w_query, w_key, w_value, w_out), first_weights)
        first_pieces = [swap_shard(first_own, bits) for bits in (1, 2, 3)]
        chosen, bias = choose(selected, segments)
        picked = pick_rows(hidden, chosen)
        second_own = pack((w_up,), (up_at,), (padded,))
        second_second = swap_shard(second_own, 2)
        first = swap_halves(join_three(first_pieces, first_rows // 2))
        third_own = pack((w_down,), (down_at,))
        second_pair, third_own = join_own(second_own, second_second, [third_own])
        second_pair = swap_shard(second_pair, 1)
        third_second = swap_shard(third_own, 2)
        *first, first_both = join_chips(*first)
        first = swap_halves(first, "yx")
        first_both_far = swap(first_both, "c")
        branch_grad = pick_rows(cotangent, chosen)
        *second, others = join_shards(second_pair, second_second, [second_rows // 2, second_rows])
        second = swap_halves(second)
        vec = whole_vectors(padded, others, width)
        third_pair = swap_shard(join_own(third_own, third_second), 1)
        first_other = join_rows(first[1], first[3])
        first_other_far = swap(first_other, "c")
        *second, second_both = join_chips(*second)
        second = swap_halves(second, "yx")
        second_both_far = swap(second_both, "c")
        cover()
        *qkv, full_out = assemble(
            (w_query, w_key, w_value, w_out),
            first_weights,
            halved(first_rows),
            (first_both, first_other, first_both_far, first_other_far),
        )
        normed, queries, keys, values = project(picked, vec, qkv)
        third = swap_halves(join_shards(third_pair, third_second, [tall // 2]))
        attended, probs, queries, keys, values, normed, *qkv = attend(bias, queries, keys, values, (normed, *qkv))
        attn_out, normed_mlp, grad_mlp, gating = project_out(attended, full_out, picked, branch_grad, vec)
        second_other = join_rows(second[1], second[3])
        second_other_far = swap(second_other, "c")
        *third, third_both = join_chips(*third)
        third = swap_halves(third, "yx")
        third_both_far = swap(third_both, "c")
        cover()
        up_near, up_far = assemble(
            (w_up,), (up_at,), halved(second_rows), (second_both, second_other, second_both_far, second_other_far)
        )
        act_far, slope_far, grad_far = project_up(normed_mlp, grad_mlp, up_far)
        act_near, slope_near, grad_near = project_up(normed_mlp, grad_mlp, up_near)

        down_keep, down_send = down_blocks(grad_near, grad_far)
        down_got = swap(down_send, "c")
        third_other = join_rows(third[1], third[3])
        third_other_far = swap(third_other, "c")
        down_near, down_far = assemble(
            (w_down,), (down_at,), halved(tall), (third_both, third_other, third_both_far, third_other_far)
        )
        far, near = (act_far, slope_far, up_far, down_far), (act_near, slope_near, up_near, down_near)

        def down_step(half, step, carried=()):
            act, slope, w_in, w_back = half
            *carried, blocks = down(step, up_at, act, slope, normed_mlp, grad_mlp, w_in, w_back, carried)
            return carried, blocks

        carried, up_send = down_step(far, 0)
        up_got = swap(up_send, "c")
        d_sums = swap_sums(add_first([(down_keep, down_got)], tall // 2), "xy")
        carried, up_keep = down_step(near, 0, carried)
        u_first = swap_sums(add_first([(up_keep, up_got)], small), "xy")
        carried, up_send = down_step(far, 1, carried)
        up_got = swap(up_send, "c")
        carried, up_keep = down_step(near, 1, carried)
        new_rows, grad_attn, grad_middle, grad_logit, gain_sums = branch(
            *carried, attn_out, picked, branch_grad, gating, vec
        )
        d_sums = swap_sums(add_second(d_sums), "yx")
        u_first = tuple(hold(*u_first))
        grad_attended, out_keep, out_send = out_back(first_weights[3], grad_attn, attended, full_out)
        out_got = swap(out_send, "c")
        cover()
        u_last = swap_sums(add_first([(up_keep, up_got), (out_keep, out_got)], 64), "xy")
        grads = []
        for seq in range(seqs):
            grads += attend_back(seq, grad_attended, queries, keys, values, probs)
            if seq == seqs - 2:
                d_away, d_keep = add_third(*d_sums)
                d_got = swap_shard(d_away, 1)
        first_keep, first_send = project_grads(first_weights[:3], normed, grads)
        first_got = swap(first_send, "c")
        d_away, d_keep = add_fourth(d_keep, d_got)
        u_sums = swap_sums(add_second(u_first, u_last), "yx")
        cover()
        grad_rows, sums = project_back(
            grads, qkv, picked, grad_middle, branch_grad, grad_logit, vec, gain_sums
        )
        f_sums = swap_sums(add_first([(first_keep, first_got)], 80, (sums, swap(sums, "c"))), "xy")
        (d_away,) = hold(d_away)
        d_got = swap_shard(d_away, 2)
        u_away, u_keep = add_third(*u_sums)
        u_got = swap_shard(u_away, 1)
        out_hidden = place_rows(range(seqs), selected, new_rows, hidden)
        f_sums = swap_sums(add_second(f_sums), "yx")
        u_away, u_keep = add_fourth(u_keep, u_got)
        u_got = swap_shard(u_away, 2)
        d_own = over_planes(add_last(d_keep, d_got))
        d_got = swap(d_own, "x")
        grad_hidden = place_rows(range(1), selected, grad_rows, cotangent)
        f_away, f_keep = add_third(*f_sums)
        f_got = swap_shard(f_away, 1)
        d_pair = join(d_own, d_got)
        d_got = swap(d_pair, "y")
        u_own = over_planes(add_last(u_keep, u_got))
        u_spread = [u_own] + [swap(u_own, way) for way in "xyd"]
        grad_hidden = place_rows(range(1, 2), selected, grad_rows, cotangent, grad_hidden)
        f_away, f_keep = add_fourth(f_keep, f_got)
        f_got = swap_shard(f_away, 2)
        grad_hidden = place_rows(range(2, seqs), selected, grad_rows, cotangent, grad_hidden)
        d_near = join(d_pair, d_got).reshape(4, *d_own.shape)
        d_far = swap(d_near, "c")
        u_near = join(*u_spread)
        u_far = swap(u_near, "c")
        f_own = over_planes(add_last(f_keep, f_got))
        f_spread = [f_own] + [swap(f_own, way) for way in "xyd"]
        cover()
        (grad_down,) = unpack((Weight(0, tall, 1, lanes),), d_near, d_far)
        up_pieces = [
            (0, 0, small, 0),
            (2 * small + 16, 0, small, lanes),
            (small, 0, small, 2 * lanes),
            (2 * small, 0, 16, 3 * lanes),
            (3 * small + 16, 16, small - 16, 3 * lanes),
        ]
        grad_up, grad_out = unpack(
            (Weight(0, small, wide, lanes, pieces=up_pieces), Weight(4 * small, small, 1, lanes)), u_near, u_far
        )
        f_near = join(*f_spread)
        grad_qkv = unpack(first_weights[:3], f_near, swap(f_near, "c"))
        sums = f_own[3 * small :].reshape(2, 8, lanes)[:, :3].swapaxes(0, 1).reshape(3, width).astype(F32)
        sums = lax.dynamic_slice(sums, (0, shard * w_router.shape[0]), (3, w_router.shape[0]))
        return (out_hidden, grad_hidden, *grad_qkv, grad_out, grad_up, grad_down, sums[0], sums[1], sums[2])

    placed = (
        P(("rep", "fsdp"), None, None),
        P(("rep", "fsdp"), None),
        P(("rep", "fsdp"), None),
        P("fsdp", None),
        P("fsdp", None),
        P("fsdp", None),
        P("fsdp", None),
        P("fsdp", None),
        P("fsdp", None),
        P("fsdp"),
        P("fsdp"),
        P("fsdp"),
        P(("rep", "fsdp"), None, None),
    )
    return jax.shard_map(
        on_device,
        mesh=mesh,
        in_specs=placed,
        out_specs=(
            P(("rep", "fsdp"), None, None),
            P(("rep", "fsdp"), None, None),
            P("fsdp", None),
            P("fsdp", None),
            P("fsdp", None),
            P("fsdp", None),
            P("fsdp", None),
            P("fsdp", None),
            P("fsdp"),
            P("fsdp"),
            P("fsdp"),
        ),
        check_vma=False,
    )
```
